32 devices in a mesh: wide: 16 (over z, x, core), narrow: 2 (over y).
Axes of the slice: x: 2, y: 2, z: 4, core: 2. Of those that a mesh axis runs over, the one named last changes fastest.
Arguments:
- states: bfloat16 [768, 128, 1024], P('wide', None, 'narrow'), may hold values from -6 to 6
- proj_weight: bfloat16 [1024, 128], P('narrow'), may hold values from -0.1875 to 0.1875
- lengths: int32 [768], replicated, may hold values from 64 to 128
- query_block: int32 [192], P('wide'), may hold values from 0 to 3
- cand_block: int32 [192], P('wide'), may hold values from 0 to 63, as said below
- pair_valid: int32 [192], P('wide'), may hold values 0 or 1
Outputs:
- pair_scores: float32 [192, 12, 12], P('wide')
The draws below stay inside these ranges and needn't reach their ends.
Inputs may be any that keep to these rules, and one draw needn't show every extreme that they name: `cand_block`: pair k of index r of wide is pair r * 12 + k. Among the 12 pairs of one index of wide, every owner (owner = block // 4) is named by either no pair or exactly 2 pairs, and pairs naming the same owner name the same block.
All inputs are finite; a program needn't handle non-finite values. No bound on the sum of `pair_valid` on one device may be relied on, other than what follows from the above.
Results may differ from the reference program's by a relative error of at most 0.0003.
Values may be sent and summed in bfloat16 or wider, within the bound.
No kernel may reach another device: no remote copies, remote signals or barrier semaphores. Data moves between devices by JAX's collectives and lax.ppermute only.
A program may use at most 128 MiB of HBM per device.

```python
import jax
import jax.numpy as jnp
from jax import lax

H = 1024
E = 128
L = 128
BLK = 12
BPD = 4
OWNERS = 16
PAIRS_DEV = 12
PARAS = 768
PAIRS_ALL = 192


def draw_cand_block(key, part):
    first, second, third = jax.random.split(key, 3)
    perms = jax.vmap(lambda k: jax.random.permutation(k, OWNERS))(jax.random.split(first, OWNERS))
    halves = jnp.arange(PAIRS_DEV) // 2
    owner_ids = perms[:, halves]
    local = jax.random.randint(second, (OWNERS, OWNERS), 0, BPD)
    blocks = owner_ids * BPD + jnp.take_along_axis(local, owner_ids, axis=1)
    order = jax.vmap(lambda k: jax.random.permutation(k, PAIRS_DEV))(jax.random.split(third, OWNERS))
    blocks = jnp.take_along_axis(blocks, order, axis=1)
    return blocks.reshape(OWNERS * PAIRS_DEV).astype(jnp.int32)


def place_ends(entries, key, low, high):
    dims = entries.shape
    index_at = [jax.random.randint(jax.random.fold_in(key, axis), (), 0, dims[axis]) for axis in range(len(dims))]
    entries = entries.at[tuple(index_at)].set(low)
    longest = dims.index(max(dims))
    index_at[longest] = (index_at[longest] + 1) % dims[longest]
    return entries.at[tuple(index_at)].set(high)


def block_scale(rng, dims, pieces, least, top_value):
    def one(dim, shards_of):
        steps = jax.random.uniform(jax.random.fold_in(jax.random.fold_in(rng, 6), dim), (shards_of,), jnp.float32, least / len(pieces), top_value / len(pieces))
        return jnp.repeat(jnp.exp(steps), dims[dim] // shards_of).reshape((-1,) + (1,) * (len(dims) - dim - 1))

    level = one(*pieces[0])
    for cut in pieces[1:]:
        level = level * one(*cut)
    return level


def noise(key, shape, scale, bound, shards=(), kind=jnp.bfloat16):
    factor_of = block_scale(key, shape, shards, -0.22, 0.18) if shards else 1.0
    array = jax.random.normal(key, shape, jnp.float32) * scale * factor_of
    return jnp.minimum(jnp.maximum(array, -bound), bound).astype(kind)


def setup_inputs(seed: int = 0) -> dict:
    arg_keys = jax.random.split(jax.random.key(seed), 7)
    states = noise(arg_keys[0], (PARAS, L, H), 1.0, 6.0, ((0, 16), (2, 2)))
    proj_weight = noise(arg_keys[1], (H, E), H ** -0.5, 0.1875, ((0, 2),))
    lengths = place_ends(jax.random.randint(arg_keys[2], (PARAS,), L // 2, L + 1), jax.random.fold_in(arg_keys[2], 1), L // 2, L).astype(jnp.int32)
    query_block = place_ends(jax.random.randint(arg_keys[3], (PAIRS_ALL,), 0, BPD), jax.random.fold_in(arg_keys[3], 1), 0, BPD - 1).astype(jnp.int32)
    cand_block = draw_cand_block(jax.random.fold_in(arg_keys[6], 71), 0)
    pair_valid = place_ends((jax.random.randint(arg_keys[5], (PAIRS_ALL,), 0, 4) < 3).astype(jnp.int32), jax.random.fold_in(arg_keys[5], 1), 0, 1)
    return dict(states=states, proj_weight=proj_weight, lengths=lengths, query_block=query_block, cand_block=cand_block, pair_valid=pair_valid)


sharpness = 20.0

def unit_rows(values):
    return values * lax.rsqrt(lax.optimization_barrier(jnp.sum(values * values, axis=-1, keepdims=True)) + 1e-06)

def reference(states, proj_weight, lengths, query_block, cand_block, pair_valid):
    flat = jnp.dot(states.reshape(PARAS * L, H), proj_weight, preferred_element_type=jnp.float32)
    rows = unit_rows(flat).astype(jnp.bfloat16).reshape(PARAS // BLK, BLK, L, E)
    block_len = lengths.reshape(PARAS // BLK, BLK)
    tokens = jnp.arange(L).astype(jnp.int32)
    requester = (jnp.arange(PAIRS_ALL) // PAIRS_DEV).astype(jnp.int32)
    query_global = (requester * BPD + query_block).astype(jnp.int32)

    def score_pair(items):
        qb, cb, keep = items
        query = rows[qb].astype(jnp.float32)
        cand = rows[cb].astype(jnp.float32)
        sim = jnp.einsum('bje,aie->bjai', cand, query, precision=lax.Precision.HIGHEST)
        cand_mask = (tokens[None, :] < block_len[cb][:, None]).astype(jnp.float32)
        totals = lax.optimization_barrier(jnp.sum(jnp.exp(sharpness * sim) * cand_mask[:, :, None, None], axis=1))
        query_mask = (tokens[None, :] < block_len[qb][:, None]).astype(jnp.float32)
        smooth = jnp.log(totals) / sharpness * query_mask[None, :, :]
        return lax.optimization_barrier(jnp.sum(smooth, axis=2)) / L * keep
    return lax.map(score_pair, (query_global, cand_block, pair_valid.astype(jnp.float32)))
```

```python
import functools
import math

import jax
import jax.numpy as jnp
from jax import lax
from jax.experimental import pallas as pl
from jax.experimental.pallas import tpu as pltpu
from jax.sharding import PartitionSpec as P

BLK = 12
SHARPNESS = 20.0
EXP2_SCALE = SHARPNESS * math.log2(math.e)
COLS = 256
SMEM = pltpu.SMEM
VMEM = pltpu.VMEM


def vmem_params(mib):
    return pltpu.CompilerParams(vmem_limit_bytes=mib * 2**20)


def plan_kernel(pairs, cand_ref, sel_ref, first_ref, second_ref, slot_ref):
    def step(k, count):
        block = cand_ref[k]
        found = lax.fori_loop(
            0, k, lambda e, f: jnp.where(cand_ref[e] == block, slot_ref[e], f), jnp.int32(-1)
        )
        new = found < 0
        slot = jnp.where(new, count, found)
        slot = jnp.minimum(slot, pairs // 2 - 1)
        slot_ref[k] = slot

        @pl.when(new)
        def _():
            sel_ref[slot] = block
            first_ref[slot] = k
            second_ref[slot] = k

        @pl.when(jnp.logical_not(new))
        def _():
            second_ref[slot] = k

        return count + new.astype(jnp.int32)

    lax.fori_loop(0, pairs, step, jnp.int32(0))


def plan(cand_block):
    pairs = cand_block.shape[0]
    out = jax.ShapeDtypeStruct((pairs // 2,), jnp.int32)
    return pl.pallas_call(
        functools.partial(plan_kernel, pairs),
        out_shape=(out, out, out),
        in_specs=[pl.BlockSpec(memory_space=SMEM)],
        out_specs=[pl.BlockSpec(memory_space=SMEM)] * 3,
        scratch_shapes=[SMEM((pairs,), jnp.int32)],
    )(cand_block)


def project_kernel(me_ref, states_ref, weight_ref, out_ref):
    out_ref[0, 0] = jnp.dot(
        states_ref[0], weight_ref[...], preferred_element_type=jnp.float32
    ).astype(out_ref.dtype)


def project(me, states, weight, shares, offset, count, dtype):
    blocks, rows, width = states.shape
    out_width = weight.shape[1]
    part = rows // shares
    return pl.pallas_call(
        project_kernel,
        out_shape=jax.ShapeDtypeStruct((count, blocks, part, out_width), dtype),
        grid_spec=pltpu.PrefetchScalarGridSpec(
            num_scalar_prefetch=1,
            grid=(count, blocks),
            in_specs=[
                pl.BlockSpec(
                    (1, part, width), lambda d, b, m: (b, lax.rem(m[0] + offset + d, shares), 0)
                ),
                pl.BlockSpec((width, out_width), lambda d, b, m: (0, 0)),
            ],
            out_specs=pl.BlockSpec((1, 1, part, out_width), lambda d, b, m: (d, b, 0, 0)),
        ),
        cost_estimate=pl.CostEstimate(
            flops=2 * count * blocks * part * width * out_width,
            bytes_accessed=2 * count * blocks * part * width,
            transcendentals=0,
        ),
    )(me, states, weight)


def unit_kernel(others, pieces, keep_ref, *refs):
    out_ref = refs[-1]
    total = keep_ref[0, 0]
    for ref in refs[:others]:
        total = total + ref[0].astype(jnp.float32)
    norm = jnp.sum(total * total, axis=-1, keepdims=True)
    unit = (total * lax.rsqrt(norm + 1e-06)).astype(jnp.bfloat16)
    if pieces is None:
        out_ref[0] = unit
    else:
        size = unit.shape[0] // pieces
        for m in range(pieces):
            out_ref[m, 0] = unit[m * size : (m + 1) * size]


def unit_rows(keep, received, owners):
    _, blocks, part, width = keep.shape
    size = part // owners
    direct = size % 16 == 0
    if direct:
        shape = (owners, blocks, size, width)
        out_spec = pl.BlockSpec((owners, 1, size, width), lambda b: (0, b, 0, 0))
    else:
        shape = (blocks, part, width)
        out_spec = pl.BlockSpec((1, part, width), lambda b: (b, 0, 0))
    out = pl.pallas_call(
        functools.partial(unit_kernel, len(received), owners if direct else None),
        out_shape=jax.ShapeDtypeStruct(shape, jnp.bfloat16),
        grid=(blocks,),
        in_specs=[pl.BlockSpec((1, 1, part, width), lambda b: (0, b, 0, 0))]
        + [pl.BlockSpec((1, part, width), lambda b: (b, 0, 0))] * len(received),
        out_specs=out_spec,
    )(keep, *received)
    if direct:
        return out
    return out.reshape(blocks, owners, size, width).transpose(1, 0, 2, 3)


def route_kernel(dests, slots, owners, asked_ref, pieces_ref, out_ref):
    def step(d, carry):
        side = d // owners
        requester = d - side * owners
        for k in range(slots):
            out_ref[d, k] = pieces_ref[asked_ref[requester, side * slots + k]]
        return carry

    lax.fori_loop(0, dests, step, 0)


def route(asked, pieces, owners, shares):
    slots = asked.shape[1] // shares
    dests = owners * shares
    return pl.pallas_call(
        functools.partial(route_kernel, dests, slots, owners),
        out_shape=jax.ShapeDtypeStruct((dests, slots) + pieces.shape[1:], jnp.bfloat16),
        in_specs=[pl.BlockSpec(memory_space=SMEM), pl.BlockSpec(memory_space=VMEM)],
        out_specs=pl.BlockSpec(memory_space=VMEM),
        compiler_params=vmem_params(48),
    )(asked, pieces)


def score_kernel(
    length, where_ref, sel_ref, first_ref, second_ref, query_block_ref, lengths_ref, valid_ref,
    query_ref, cand_ref, out_ref, totals_ref,
):
    owner, side = where_ref[0], where_ref[1]
    slots, rows, _ = cand_ref.shape
    blocks = query_ref.shape[0]
    out_ref[...] = jnp.zeros_like(out_ref)
    totals_ref[...] = jnp.ones_like(totals_ref)
    upper = lax.broadcasted_iota(jnp.int32, (length // 2, COLS), 0) + length // 2
    lane = lax.broadcasted_iota(jnp.int32, (16, length), 1)

    def slot_step(k, carry):
        slot = side * slots + k
        block = sel_ref[slot]
        for which_ref in (first_ref, second_ref):
            pair = which_ref[slot]
            query = query_block_ref[pair]

            def column_step(c, carry):
                start = pl.multiple_of(c * COLS, COLS)
                sim = lax.dot_general(
                    cand_ref[k],
                    query_ref[query, pl.ds(start, COLS)],
                    (((1,), (1,)), ((), ())),
                    preferred_element_type=jnp.float32,
                )
                for b in range(BLK):
                    live = lengths_ref[block * BLK + b]
                    low = jnp.exp2(sim[b * length : b * length + length // 2] * EXP2_SCALE)
                    high = jnp.exp2(sim[b * length + length // 2 : (b + 1) * length] * EXP2_SCALE)
                    both = low + jnp.where(upper < live, high, 0.0)
                    totals_ref[pl.ds(b, 1), pl.ds(start, COLS)] = jnp.sum(both, axis=0, keepdims=True)
                return carry

            lax.fori_loop(0, rows // COLS, column_step, 0)
            score = jnp.zeros((16, length), jnp.float32)
            for a in range(BLK):
                live = lengths_ref[(owner * blocks + query) * BLK + a]
                logs = jnp.log(totals_ref[:, a * length : (a + 1) * length])
                summed = jnp.sum(jnp.where(lane < live, logs, 0.0), axis=1, keepdims=True)
                score = jnp.where(lane == a, summed, score)
            keep = valid_ref[pair].astype(jnp.float32) / (SHARPNESS * length)
            out_ref[pair] = score[:BLK, :BLK] * keep
        return carry

    lax.fori_loop(0, slots, slot_step, 0)


def score(where, sel, first, second, query_block, lengths, valid, query, cand, length):
    pairs = query_block.shape[0]
    slots, rows, width = cand.shape
    count = 2 * slots * rows * rows
    return pl.pallas_call(
        functools.partial(score_kernel, length),
        out_shape=jax.ShapeDtypeStruct((pairs, BLK, BLK), jnp.float32),
        in_specs=[pl.BlockSpec(memory_space=SMEM)] * 7 + [pl.BlockSpec(memory_space=VMEM)] * 2,
        out_specs=pl.BlockSpec(memory_space=VMEM),
        scratch_shapes=[VMEM((16, rows), jnp.float32)],
        compiler_params=vmem_params(48),
        cost_estimate=pl.CostEstimate(
            flops=2 * count * width, bytes_accessed=4 * rows * width, transcendentals=count
        ),
    )(where, sel, first, second, query_block, lengths, valid, query, cand)


def local(states, proj_weight, lengths, query_block, cand_block, pair_valid):
    shares = lax.axis_size("narrow")
    owners = lax.axis_size("wide")
    side = lax.axis_index("narrow").astype(jnp.int32)
    owner = lax.axis_index("wide").astype(jnp.int32)
    paras, length, width_part = states.shape
    width = proj_weight.shape[1]
    blocks = paras // BLK
    rows = BLK * length
    flat = states.reshape(blocks, rows, width_part)
    me = side.reshape(1)

    def shift(d):
        return [(i, (i + d) % shares) for i in range(shares)]

    sel, first, second = plan(cand_block)
    sent = project(me, flat, proj_weight, shares, 1, shares - 1, jnp.bfloat16)
    received = [lax.ppermute(sent[d - 1], "narrow", shift(d)) for d in range(1, shares)]
    asked = lax.all_to_all(
        jnp.broadcast_to(sel[None], (owners,) + sel.shape), "wide", 0, 0, tiled=True
    )
    kept = project(me, flat, proj_weight, shares, 0, 1, jnp.float32)
    mine = unit_rows(kept, received, owners)
    spread = lax.all_to_all(mine, "wide", 0, 0, tiled=True)
    size = mine.shape[2]
    by_side = [mine] + [lax.ppermute(mine, "narrow", shift(d)) for d in range(1, shares)]
    order = jnp.stack(by_side)
    query = jnp.stack(
        [lax.dynamic_index_in_dim(order, lax.rem(side - s + shares, shares), 0, False) for s in range(shares)]
    )
    query = query.transpose(2, 0, 1, 3, 4).reshape(blocks, rows, width)
    outgoing = route(asked, spread.reshape(owners * blocks, size, width), owners, shares)
    incoming = lax.all_to_all(outgoing, ("narrow", "wide"), 0, 0, tiled=True)
    cand = incoming.transpose(1, 0, 2, 3).reshape(-1, rows, width)
    part = score(
        jnp.stack([owner, side]), sel, first, second, query_block, lengths, pair_valid, query, cand, length
    )
    out = part
    for d in range(1, shares):
        out = out + lax.ppermute(part, "narrow", shift(d))
    return out


def solution(mesh):
    in_specs = (P("wide", None, "narrow"), P("narrow", None), P(), P("wide"), P("wide"), P("wide"))
    out_specs = P("wide", None, None)
    return jax.shard_map(local, mesh=mesh, in_specs=in_specs, out_specs=out_specs, check_vma=False)
```

```python
import functools
import math

import jax
import jax.numpy as jnp
from jax import lax
from jax.experimental import pallas as pl
from jax.experimental.pallas import tpu as pltpu
from jax.sharding import PartitionSpec as P

BLK = 12
SHARPNESS = 20.0
EXP2_SCALE = SHARPNESS * math.log2(math.e)
COLS = 256
CHUNK = 2
SMEM = pltpu.SMEM
VMEM = pltpu.VMEM


def vmem_params(mib):
    return pltpu.CompilerParams(vmem_limit_bytes=mib * 2**20)


def plan_kernel(pairs, cand_ref, sel_ref, first_ref, second_ref, slot_ref):
    def step(k, count):
        block = cand_ref[k]
        found = lax.fori_loop(
            0, k, lambda e, f: jnp.where(cand_ref[e] == block, slot_ref[e], f), jnp.int32(-1)
        )
        new = found < 0
        slot = jnp.where(new, count, found)
        slot = jnp.minimum(slot, pairs // 2 - 1)
        slot_ref[k] = slot

        @pl.when(new)
        def _():
            sel_ref[slot] = block
            first_ref[slot] = k
            second_ref[slot] = k

        @pl.when(jnp.logical_not(new))
        def _():
            second_ref[slot] = k

        return count + new.astype(jnp.int32)

    lax.fori_loop(0, pairs, step, jnp.int32(0))


def plan(cand_block):
    pairs = cand_block.shape[0]
    out = jax.ShapeDtypeStruct((pairs // 2,), jnp.int32)
    return pl.pallas_call(
        functools.partial(plan_kernel, pairs),
        out_shape=(out, out, out),
        in_specs=[pl.BlockSpec(memory_space=SMEM)],
        out_specs=[pl.BlockSpec(memory_space=SMEM)] * 3,
        scratch_shapes=[SMEM((pairs,), jnp.int32)],
    )(cand_block)


def project_kernel(me_ref, states_ref, weight_ref, out_ref):
    out_ref[0, 0] = jnp.dot(
        states_ref[0], weight_ref[...], preferred_element_type=jnp.float32
    ).astype(out_ref.dtype)


def project(me, states, weight, shares, offset, count, dtype):
    blocks, rows, width = states.shape
    out_width = weight.shape[1]
    part = rows // shares
    return pl.pallas_call(
        project_kernel,
        out_shape=jax.ShapeDtypeStruct((count, blocks, part, out_width), dtype),
        grid_spec=pltpu.PrefetchScalarGridSpec(
            num_scalar_prefetch=1,
            grid=(count, blocks),
            in_specs=[
                pl.BlockSpec(
                    (1, part, width), lambda d, b, m: (b, lax.rem(m[0] + offset + d, shares), 0)
                ),
                pl.BlockSpec((width, out_width), lambda d, b, m: (0, 0)),
            ],
            out_specs=pl.BlockSpec((1, 1, part, out_width), lambda d, b, m: (d, b, 0, 0)),
        ),
        cost_estimate=pl.CostEstimate(
            flops=2 * count * blocks * part * width * out_width,
            bytes_accessed=2 * count * blocks * part * width,
            transcendentals=0,
        ),
    )(me, states, weight)


def unit_kernel(others, pieces, keep_ref, *refs):
    out_ref = refs[-1]
    total = keep_ref[0, 0]
    for ref in refs[:others]:
        total = total + ref[0].astype(jnp.float32)
    norm = jnp.sum(total * total, axis=-1, keepdims=True)
    unit = (total * lax.rsqrt(norm + 1e-06)).astype(jnp.bfloat16)
    if pieces is None:
        out_ref[0] = unit
    else:
        size = unit.shape[0] // pieces
        for m in range(pieces):
            out_ref[m, 0] = unit[m * size : (m + 1) * size]


def unit_rows(keep, received, owners):
    _, blocks, part, width = keep.shape
    size = part // owners
    direct = size % 16 == 0
    if direct:
        shape = (owners, blocks, size, width)
        out_spec = pl.BlockSpec((owners, 1, size, width), lambda b: (0, b, 0, 0))
    else:
        shape = (blocks, part, width)
        out_spec = pl.BlockSpec((1, part, width), lambda b: (b, 0, 0))
    out = pl.pallas_call(
        functools.partial(unit_kernel, len(received), owners if direct else None),
        out_shape=jax.ShapeDtypeStruct(shape, jnp.bfloat16),
        grid=(blocks,),
        in_specs=[pl.BlockSpec((1, 1, part, width), lambda b: (0, b, 0, 0))]
        + [pl.BlockSpec((1, part, width), lambda b: (b, 0, 0))] * len(received),
        out_specs=out_spec,
    )(keep, *received)
    if direct:
        return out
    return out.reshape(blocks, owners, size, width).transpose(1, 0, 2, 3)


def route_kernel(dests, slots, owners, asked_ref, pieces_ref, out_ref):
    def step(d, carry):
        side = d // owners
        requester = d - side * owners
        for k in range(slots):
            out_ref[d, k] = pieces_ref[asked_ref[requester, side * slots + k]]
        return carry

    lax.fori_loop(0, dests, step, 0)


def route(asked, pieces, owners, shares):
    slots = asked.shape[1] // shares
    dests = owners * shares
    return pl.pallas_call(
        functools.partial(route_kernel, dests, slots, owners),
        out_shape=jax.ShapeDtypeStruct((dests, slots) + pieces.shape[1:], jnp.bfloat16),
        in_specs=[pl.BlockSpec(memory_space=SMEM), pl.BlockSpec(memory_space=VMEM)],
        out_specs=pl.BlockSpec(memory_space=VMEM),
        compiler_params=vmem_params(48),
    )(asked, pieces)


def score_kernel(
    length, where_ref, sel_ref, first_ref, second_ref, query_block_ref, lengths_ref, valid_ref,
    query_ref, cand_ref, out_ref, totals_ref,
):
    owner, side = where_ref[0], where_ref[1]
    slots, rows, _ = cand_ref.shape
    blocks = query_ref.shape[0]
    out_ref[...] = jnp.zeros_like(out_ref)
    totals_ref[...] = jnp.ones_like(totals_ref)
    upper = lax.broadcasted_iota(jnp.int32, (length // 2, COLS), 0) + length // 2
    lane = lax.broadcasted_iota(jnp.int32, (16, length), 1)

    def pair_step(i, carry):
        k = i // 2
        slot = side * slots + k
        block = sel_ref[slot]
        pair = jnp.where(i - 2 * k == 0, first_ref[slot], second_ref[slot])
        query = query_block_ref[pair]
        for start in range(0, rows, COLS):
            sim = lax.dot_general(
                cand_ref[k],
                query_ref[query, start : start + COLS],
                (((1,), (1,)), ((), ())),
                preferred_element_type=jnp.float32,
            )
            for b in range(BLK):
                live = lengths_ref[block * BLK + b]
                low = jnp.exp2(sim[b * length : b * length + length // 2] * EXP2_SCALE)
                high = jnp.exp2(sim[b * length + length // 2 : (b + 1) * length] * EXP2_SCALE)
                both = low + jnp.where(upper < live, high, 0.0)
                totals_ref[b : b + 1, start : start + COLS] = jnp.sum(both, axis=0, keepdims=True)
        score = jnp.zeros((16, length), jnp.float32)
        for a in range(BLK):
            live = lengths_ref[(owner * blocks + query) * BLK + a]
            logs = jnp.log(totals_ref[:, a * length : (a + 1) * length])
            summed = jnp.sum(jnp.where(lane < live, logs, 0.0), axis=1, keepdims=True)
            score = jnp.where(lane == a, summed, score)
        keep = valid_ref[pair].astype(jnp.float32) / (SHARPNESS * length)
        out_ref[pair] = score[:BLK, :BLK] * keep
        return carry

    lax.fori_loop(0, 2 * slots, pair_step, 0)


def score(where, sel, first, second, query_block, lengths, valid, query, cand, length):
    pairs = query_block.shape[0]
    slots, rows, width = cand.shape
    count = 2 * slots * rows * rows
    return pl.pallas_call(
        functools.partial(score_kernel, length),
        out_shape=jax.ShapeDtypeStruct((pairs, BLK, BLK), jnp.float32),
        in_specs=[pl.BlockSpec(memory_space=SMEM)] * 7 + [pl.BlockSpec(memory_space=VMEM)] * 2,
        out_specs=pl.BlockSpec(memory_space=VMEM),
        scratch_shapes=[VMEM((16, rows), jnp.float32)],
        compiler_params=vmem_params(24),
        cost_estimate=pl.CostEstimate(
            flops=2 * count * width, bytes_accessed=4 * rows * width, transcendentals=count
        ),
    )(where, sel, first, second, query_block, lengths, valid, query, cand)


def local_general(states, proj_weight, lengths, query_block, cand_block, pair_valid):
    shares = lax.axis_size("narrow")
    owners = lax.axis_size("wide")
    side = lax.axis_index("narrow").astype(jnp.int32)
    owner = lax.axis_index("wide").astype(jnp.int32)
    paras, length, width_part = states.shape
    width = proj_weight.shape[1]
    blocks = paras // BLK
    rows = BLK * length
    flat = states.reshape(blocks, rows, width_part)
    me = side.reshape(1)

    def shift(d):
        return [(i, (i + d) % shares) for i in range(shares)]

    sel, first, second = plan(cand_block)
    sent = project(me, flat, proj_weight, shares, 1, shares - 1, jnp.bfloat16)
    received = [lax.ppermute(sent[d - 1], "narrow", shift(d)) for d in range(1, shares)]
    asked = lax.all_to_all(
        jnp.broadcast_to(sel[None], (owners,) + sel.shape), "wide", 0, 0, tiled=True
    )
    kept = project(me, flat, proj_weight, shares, 0, 1, jnp.float32)
    mine = unit_rows(kept, received, owners)
    spread = lax.all_to_all(mine, "wide", 0, 0, tiled=True)
    size = mine.shape[2]
    by_side = [mine] + [lax.ppermute(mine, "narrow", shift(d)) for d in range(1, shares)]
    order = jnp.stack(by_side)
    query = jnp.stack(
        [lax.dynamic_index_in_dim(order, lax.rem(side - s + shares, shares), 0, False) for s in range(shares)]
    )
    query = query.transpose(2, 0, 1, 3, 4).reshape(blocks, rows, width)
    outgoing = route(asked, spread.reshape(owners * blocks, size, width), owners, shares)
    incoming = lax.all_to_all(outgoing, ("narrow", "wide"), 0, 0, tiled=True)
    cand = incoming.transpose(1, 0, 2, 3).reshape(-1, rows, width)
    part = score(
        jnp.stack([owner, side]), sel, first, second, query_block, lengths, pair_valid, query, cand, length
    )
    out = part
    for d in range(1, shares):
        out = out + lax.ppermute(part, "narrow", shift(d))
    return out


def split_kernel(first, sel_count, place_ref, *refs):
    if sel_count:
        sel_ref, refs = refs[0], refs[1:]
    states_ref, weight_ref = refs[:2]
    outs, all_ref = refs[2:6], refs[6]
    b, half = pl.program_id(0), pl.program_id(1)
    part = states_ref.shape[1]
    blocks = pl.num_programs(0)
    all_ref[pl.ds(pl.multiple_of(half * part, part), part)] = jnp.dot(
        states_ref[0], weight_ref[...], preferred_element_type=jnp.float32
    ).astype(all_ref.dtype)

    @pl.when(half == 1)
    def _():
        x, side = place_ref[1], place_ref[3]
        size = part // 16
        for rel, out_ref in enumerate(outs):
            base = (side ^ (rel // 2)) * part + (x ^ (rel % 2)) * (2 * size)
            for z in range(4):
                for c in range(2):
                    source = pl.multiple_of(base + z * 4 * size + c * size, 16)
                    target = pl.multiple_of(((z * 2 + c) * CHUNK + b) * size, 16)
                    out_ref[pl.ds(target, size)] = all_ref[pl.ds(source, size)]

    if sel_count:

        @pl.when((half == 1) & (b == 0))
        def _():
            lane = lax.broadcasted_iota(jnp.int32, (16, all_ref.shape[1]), 1)
            row = jnp.zeros_like(lane)
            for k in range(sel_count):
                row = jnp.where(lane == k, sel_ref[k], row)
            row = row.astype(jnp.float32).astype(all_ref.dtype)
            for out_ref in outs:
                out_ref[8 * CHUNK * (part // 16) :] = row


def split(place, sel, states, weight, first):
    _, rows, width = states.shape
    out_width = weight.shape[1]
    part = rows // 2
    sel_count = 0 if sel is None else sel.shape[0]
    out_rows = 8 * CHUNK * (part // 16) + (16 if sel_count else 0)
    out = jax.ShapeDtypeStruct((out_rows, out_width), jnp.bfloat16)
    whole = pl.BlockSpec((out_rows, out_width), lambda b, h, *m: (0, 0))
    scalars = (place,) if sel is None else (place, sel)
    return pl.pallas_call(
        functools.partial(split_kernel, first, sel_count),
        out_shape=(out,) * 4,
        grid_spec=pltpu.PrefetchScalarGridSpec(
            num_scalar_prefetch=len(scalars),
            grid=(CHUNK, 2),
            in_specs=[
                pl.BlockSpec((1, part, width), lambda b, h, *m: (first + b, h, 0)),
                pl.BlockSpec((width, out_width), lambda b, h, *m: (0, 0)),
            ],
            out_specs=[whole] * 4,
            scratch_shapes=[VMEM((rows, out_width), jnp.bfloat16)],
        ),
        compiler_params=vmem_params(58),
        cost_estimate=pl.CostEstimate(
            flops=2 * CHUNK * rows * width * out_width,
            bytes_accessed=2 * CHUNK * rows * width,
            transcendentals=0,
        ),
    )(*scalars, states, weight)


def gather_unit_kernel(size, place_ref, own_ref, x_ref, y_ref, xy_ref, *outs):
    z, c = place_ref[0], place_ref[2]
    sends, queries = outs[:8], outs[8:]
    span = CHUNK * size
    for rel, send_ref in enumerate(sends):
        source = pl.multiple_of(((z ^ (rel // 2)) * 2 + (c ^ (rel % 2))) * span, 16)
        for dx, (one_ref, two_ref) in enumerate(((own_ref, y_ref), (x_ref, xy_ref))):
            total = one_ref[pl.ds(source, span)].astype(jnp.float32)
            total = total + two_ref[pl.ds(source, span)].astype(jnp.float32)
            norm = jnp.sum(total * total, axis=-1, keepdims=True)
            unit = (total * lax.rsqrt(norm + 1e-06)).astype(jnp.bfloat16)
            send_ref[dx * span : (dx + 1) * span] = unit
            queries[dx][pl.ds(source, span)] = unit
        if send_ref.shape[0] > 2 * span:
            row = lax.broadcasted_iota(jnp.int32, (16, own_ref.shape[1]), 0)
            send_ref[2 * span :] = jnp.where(
                row == 0,
                own_ref[8 * span :].astype(jnp.float32),
                x_ref[8 * span :].astype(jnp.float32),
            ).astype(jnp.bfloat16)


def gather_unit(place, own, x, y, xy, size):
    width = own.shape[1]
    span = CHUNK * size
    extra = own.shape[0] - 8 * span
    send = jax.ShapeDtypeStruct((2 * span + extra, width), jnp.bfloat16)
    query = jax.ShapeDtypeStruct((8 * span, width), jnp.bfloat16)
    return pl.pallas_call(
        functools.partial(gather_unit_kernel, size),
        out_shape=(send,) * 8 + (query,) * 2,
        in_specs=[pl.BlockSpec(memory_space=SMEM)] + [pl.BlockSpec(memory_space=VMEM)] * 4,
        out_specs=[pl.BlockSpec(memory_space=VMEM)] * 10,
        compiler_params=vmem_params(16),
    )(place, own, x, y, xy)


def cube_route_kernel(size, slots, parts, place_ref, *refs):
    spread, out_ref, pieces_ref, rows_ref, asked_ref, sem = refs[:parts], *refs[parts:]
    z, x, c = place_ref[0], place_ref[1], place_ref[2]
    blocks = pieces_ref.shape[0] // 16
    span = CHUNK * size
    for i, ref in enumerate(spread):
        first, rel = i // 8 * CHUNK, i % 8
        for dx in range(2):
            owner = (z ^ (rel // 2)) * 4 + (x ^ dx) * 2 + (c ^ (rel % 2))
            for b in range(CHUNK):
                begin = dx * span + b * size
                pieces_ref[owner * blocks + first + b] = ref[begin : begin + size]
            if ref.shape[0] > 2 * span:
                row = ref[2 * span :].astype(jnp.float32)[dx : dx + 1]
                rows_ref[pl.ds(owner, 1)] = row.astype(jnp.int32)
    copy = pltpu.make_async_copy(rows_ref, asked_ref, sem)
    copy.start()
    copy.wait()

    def step(d, carry):
        side = d // 16
        for k in range(slots):
            out_ref[d, k] = pieces_ref[asked_ref[d - side * 16, side * slots + k]]
        return carry

    lax.fori_loop(0, 32, step, 0, unroll=4)


def cube_route(place, spread, size, slots, blocks):
    width = spread[0].shape[1]
    return pl.pallas_call(
        functools.partial(cube_route_kernel, size, slots, len(spread)),
        out_shape=jax.ShapeDtypeStruct((32, slots, size, width), jnp.bfloat16),
        in_specs=[pl.BlockSpec(memory_space=SMEM)]
        + [pl.BlockSpec(memory_space=VMEM)] * len(spread),
        out_specs=pl.BlockSpec(memory_space=VMEM),
        scratch_shapes=[
            VMEM((16 * blocks, size, width), jnp.bfloat16),
            VMEM((16, width), jnp.int32),
            SMEM((16, width), jnp.int32),
            pltpu.SemaphoreType.DMA,
        ],
        compiler_params=vmem_params(16),
    )(place, *spread)


def queries_kernel(size, place_ref, *refs):
    parts, out_ref = refs[:-1], refs[-1]
    x, side = place_ref[1], place_ref[3]
    for i, ref in enumerate(parts):
        first, rel = i // 4 * CHUNK, i % 4
        base = (side ^ (rel // 2)) * (16 * size) + (x ^ (rel % 2)) * (2 * size)
        for z in range(4):
            for c in range(2):
                target = pl.multiple_of(base + z * 4 * size + c * size, 16)
                for b in range(CHUNK):
                    begin = ((z * 2 + c) * CHUNK + b) * size
                    out_ref[first + b, pl.ds(target, size)] = ref[begin : begin + size]


def queries(place, parts, size, blocks):
    width = parts[0].shape[1]
    return pl.pallas_call(
        functools.partial(queries_kernel, size),
        out_shape=jax.ShapeDtypeStruct((blocks, 32 * size, width), jnp.bfloat16),
        in_specs=[pl.BlockSpec(memory_space=SMEM)] + [pl.BlockSpec(memory_space=VMEM)] * len(parts),
        out_specs=pl.BlockSpec(memory_space=VMEM),
        compiler_params=vmem_params(16),
    )(place, *parts)


def local_cube(states, proj_weight, lengths, query_block, cand_block, pair_valid):
    side = lax.axis_index("narrow").astype(jnp.int32)
    owner = lax.axis_index("wide").astype(jnp.int32)
    place = jnp.stack([owner // 4, owner // 2 % 2, owner % 2, side])
    paras, length, width_part = states.shape
    width = proj_weight.shape[1]
    blocks = paras // BLK
    rows = BLK * length
    size = rows // 32
    slots = cand_block.shape[0] // 4
    flat = states.reshape(blocks, rows, width_part)

    def near(array, rel):
        flip = rel % 2 * 4 + rel // 2
        return lax.ppermute(array, ("wide", "narrow"), [(i, i ^ flip) for i in range(32)])

    def along(array, rel):
        flip = rel // 2 * 4 + rel % 2
        return lax.ppermute(array, "wide", [(i, i ^ flip) for i in range(16)])

    sel, first, second = plan(cand_block)
    spread, query_parts = [], []
    for c in range(0, blocks, CHUNK):
        last = c + CHUNK == blocks
        parts = split(place, sel if last else None, flat, proj_weight, c)
        parts = [parts[0]] + [near(parts[rel], rel) for rel in (1, 2, 3)]
        *sends, own, other = gather_unit(place, *parts, size)
        spread += [sends[0]] + [along(sends[rel], rel) for rel in range(1, 8)]
        query_parts.append((own, other))
    outgoing = cube_route(place, spread, size, slots, blocks)
    outgoing, query_parts = lax.optimization_barrier((outgoing, query_parts))
    incoming = lax.all_to_all(outgoing, ("narrow", "wide"), 0, 0, tiled=True)
    gathered = []
    for own, other in query_parts:
        gathered += [own, near(other, 1), near(own, 2), near(other, 3)]
    query = queries(place, gathered, size, blocks)
    cand = incoming.transpose(1, 0, 2, 3).reshape(-1, rows, width)
    part = score(
        jnp.stack([owner, side]), sel, first, second, query_block, lengths, pair_valid, query, cand, length
    )
    return part + lax.ppermute(part, "narrow", [(0, 1), (1, 0)])


def solution(mesh):
    in_specs = (P("wide", None, "narrow"), P("narrow", None), P(), P("wide"), P("wide"), P("wide"))
    out_specs = P("wide", None, None)
    cube = mesh.shape["wide"] == 16 and mesh.shape["narrow"] == 2
    local = local_cube if cube else local_general
    return jax.shard_map(local, mesh=mesh, in_specs=in_specs, out_specs=out_specs, check_vma=False)
```

```python
import functools
import math

import jax
import jax.numpy as jnp
from jax import lax
from jax.experimental import pallas as pl
from jax.experimental.pallas import tpu as pltpu
from jax.sharding import PartitionSpec as P

BLK = 12
SHARPNESS = 20.0
EXP2_SCALE = SHARPNESS * math.log2(math.e)
COLS = 256
CHUNK = 2
SMEM = pltpu.SMEM
VMEM = pltpu.VMEM


def vmem_params(mib):
    return pltpu.CompilerParams(vmem_limit_bytes=mib * 2**20)


def plan_kernel(pairs, cand_ref, sel_ref, first_ref, second_ref, slot_ref):
    def step(k, count):
        block = cand_ref[k]
        found = lax.fori_loop(
            0, k, lambda e, f: jnp.where(cand_ref[e] == block, slot_ref[e], f), jnp.int32(-1)
        )
        new = found < 0
        slot = jnp.where(new, count, found)
        slot = jnp.minimum(slot, pairs // 2 - 1)
        slot_ref[k] = slot

        @pl.when(new)
        def _():
            sel_ref[slot] = block
            first_ref[slot] = k
            second_ref[slot] = k

        @pl.when(jnp.logical_not(new))
        def _():
            second_ref[slot] = k

        return count + new.astype(jnp.int32)

    lax.fori_loop(0, pairs, step, jnp.int32(0))


def plan(cand_block):
    pairs = cand_block.shape[0]
    out = jax.ShapeDtypeStruct((pairs // 2,), jnp.int32)
    return pl.pallas_call(
        functools.partial(plan_kernel, pairs),
        out_shape=(out, out, out),
        in_specs=[pl.BlockSpec(memory_space=SMEM)],
        out_specs=[pl.BlockSpec(memory_space=SMEM)] * 3,
        scratch_shapes=[SMEM((pairs,), jnp.int32)],
    )(cand_block)


def project_kernel(me_ref, states_ref, weight_ref, out_ref):
    out_ref[0, 0] = jnp.dot(
        states_ref[0], weight_ref[...], preferred_element_type=jnp.float32
    ).astype(out_ref.dtype)


def project(me, states, weight, shares, offset, count, dtype):
    blocks, rows, width = states.shape
    out_width = weight.shape[1]
    part = rows // shares
    return pl.pallas_call(
        project_kernel,
        out_shape=jax.ShapeDtypeStruct((count, blocks, part, out_width), dtype),
        grid_spec=pltpu.PrefetchScalarGridSpec(
            num_scalar_prefetch=1,
            grid=(count, blocks),
            in_specs=[
                pl.BlockSpec(
                    (1, part, width), lambda d, b, m: (b, lax.rem(m[0] + offset + d, shares), 0)
                ),
                pl.BlockSpec((width, out_width), lambda d, b, m: (0, 0)),
            ],
            out_specs=pl.BlockSpec((1, 1, part, out_width), lambda d, b, m: (d, b, 0, 0)),
        ),
        cost_estimate=pl.CostEstimate(
            flops=2 * count * blocks * part * width * out_width,
            bytes_accessed=2 * count * blocks * part * width,
            transcendentals=0,
        ),
    )(me, states, weight)


def unit_kernel(others, pieces, keep_ref, *refs):
    out_ref = refs[-1]
    total = keep_ref[0, 0]
    for ref in refs[:others]:
        total = total + ref[0].astype(jnp.float32)
    norm = jnp.sum(total * total, axis=-1, keepdims=True)
    unit = (total * lax.rsqrt(norm + 1e-06)).astype(jnp.bfloat16)
    if pieces is None:
        out_ref[0] = unit
    else:
        size = unit.shape[0] // pieces
        for m in range(pieces):
            out_ref[m, 0] = unit[m * size : (m + 1) * size]


def unit_rows(keep, received, owners):
    _, blocks, part, width = keep.shape
    size = part // owners
    direct = size % 16 == 0
    if direct:
        shape = (owners, blocks, size, width)
        out_spec = pl.BlockSpec((owners, 1, size, width), lambda b: (0, b, 0, 0))
    else:
        shape = (blocks, part, width)
        out_spec = pl.BlockSpec((1, part, width), lambda b: (b, 0, 0))
    out = pl.pallas_call(
        functools.partial(unit_kernel, len(received), owners if direct else None),
        out_shape=jax.ShapeDtypeStruct(shape, jnp.bfloat16),
        grid=(blocks,),
        in_specs=[pl.BlockSpec((1, 1, part, width), lambda b: (0, b, 0, 0))]
        + [pl.BlockSpec((1, part, width), lambda b: (b, 0, 0))] * len(received),
        out_specs=out_spec,
    )(keep, *received)
    if direct:
        return out
    return out.reshape(blocks, owners, size, width).transpose(1, 0, 2, 3)


def route_kernel(dests, slots, owners, asked_ref, pieces_ref, out_ref):
    def step(d, carry):
        side = d // owners
        requester = d - side * owners
        for k in range(slots):
            out_ref[d, k] = pieces_ref[asked_ref[requester, side * slots + k]]
        return carry

    lax.fori_loop(0, dests, step, 0)


def route(asked, pieces, owners, shares):
    slots = asked.shape[1] // shares
    dests = owners * shares
    return pl.pallas_call(
        functools.partial(route_kernel, dests, slots, owners),
        out_shape=jax.ShapeDtypeStruct((dests, slots) + pieces.shape[1:], jnp.bfloat16),
        in_specs=[pl.BlockSpec(memory_space=SMEM), pl.BlockSpec(memory_space=VMEM)],
        out_specs=pl.BlockSpec(memory_space=VMEM),
        compiler_params=vmem_params(48),
    )(asked, pieces)


def score_kernel(
    length, where_ref, sel_ref, first_ref, second_ref, query_block_ref, lengths_ref, valid_ref,
    query_ref, cand_ref, out_ref, totals_ref,
):
    owner, side = where_ref[0], where_ref[1]
    slots, rows, _ = cand_ref.shape
    blocks = query_ref.shape[0]
    out_ref[...] = jnp.zeros_like(out_ref)
    totals_ref[...] = jnp.ones_like(totals_ref)
    upper = lax.broadcasted_iota(jnp.int32, (length // 2, COLS), 0) + length // 2
    lane = lax.broadcasted_iota(jnp.int32, (16, length), 1)

    def pair_step(i, carry):
        k = i // 2
        slot = side * slots + k
        block = sel_ref[slot]
        pair = jnp.where(i - 2 * k == 0, first_ref[slot], second_ref[slot])
        query = query_block_ref[pair]
        for start in range(0, rows, COLS):
            sim = lax.dot_general(
                cand_ref[k],
                query_ref[query, start : start + COLS],
                (((1,), (1,)), ((), ())),
                preferred_element_type=jnp.float32,
            )
            for b in range(BLK):
                live = lengths_ref[block * BLK + b]
                low = jnp.exp2(sim[b * length : b * length + length // 2] * EXP2_SCALE)
                high = jnp.exp2(sim[b * length + length // 2 : (b + 1) * length] * EXP2_SCALE)
                both = low + jnp.where(upper < live, high, 0.0)
                totals_ref[b : b + 1, start : start + COLS] = jnp.sum(both, axis=0, keepdims=True)
        score = jnp.zeros((16, length), jnp.float32)
        for a in range(BLK):
            live = lengths_ref[(owner * blocks + query) * BLK + a]
            logs = jnp.log(totals_ref[:, a * length : (a + 1) * length])
            summed = jnp.sum(jnp.where(lane < live, logs, 0.0), axis=1, keepdims=True)
            score = jnp.where(lane == a, summed, score)
        keep = valid_ref[pair].astype(jnp.float32) / (SHARPNESS * length)
        out_ref[pair] = score[:BLK, :BLK] * keep
        return carry

    lax.fori_loop(0, 2 * slots, pair_step, 0)


def score(where, sel, first, second, query_block, lengths, valid, query, cand, length):
    pairs = query_block.shape[0]
    slots, rows, width = cand.shape
    count = 2 * slots * rows * rows
    return pl.pallas_call(
        functools.partial(score_kernel, length),
        out_shape=jax.ShapeDtypeStruct((pairs, BLK, BLK), jnp.float32),
        in_specs=[pl.BlockSpec(memory_space=SMEM)] * 7 + [pl.BlockSpec(memory_space=VMEM)] * 2,
        out_specs=pl.BlockSpec(memory_space=VMEM),
        scratch_shapes=[VMEM((16, rows), jnp.float32)],
        compiler_params=vmem_params(24),
        cost_estimate=pl.CostEstimate(
            flops=2 * count * width, bytes_accessed=4 * rows * width, transcendentals=count
        ),
    )(where, sel, first, second, query_block, lengths, valid, query, cand)


def local_general(states, proj_weight, lengths, query_block, cand_block, pair_valid):
    shares = lax.axis_size("narrow")
    owners = lax.axis_size("wide")
    side = lax.axis_index("narrow").astype(jnp.int32)
    owner = lax.axis_index("wide").astype(jnp.int32)
    paras, length, width_part = states.shape
    width = proj_weight.shape[1]
    blocks = paras // BLK
    rows = BLK * length
    flat = states.reshape(blocks, rows, width_part)
    me = side.reshape(1)

    def shift(d):
        return [(i, (i + d) % shares) for i in range(shares)]

    sel, first, second = plan(cand_block)
    sent = project(me, flat, proj_weight, shares, 1, shares - 1, jnp.bfloat16)
    received = [lax.ppermute(sent[d - 1], "narrow", shift(d)) for d in range(1, shares)]
    asked = lax.all_to_all(
        jnp.broadcast_to(sel[None], (owners,) + sel.shape), "wide", 0, 0, tiled=True
    )
    kept = project(me, flat, proj_weight, shares, 0, 1, jnp.float32)
    mine = unit_rows(kept, received, owners)
    spread = lax.all_to_all(mine, "wide", 0, 0, tiled=True)
    size = mine.shape[2]
    by_side = [mine] + [lax.ppermute(mine, "narrow", shift(d)) for d in range(1, shares)]
    order = jnp.stack(by_side)
    query = jnp.stack(
        [lax.dynamic_index_in_dim(order, lax.rem(side - s + shares, shares), 0, False) for s in range(shares)]
    )
    query = query.transpose(2, 0, 1, 3, 4).reshape(blocks, rows, width)
    outgoing = route(asked, spread.reshape(owners * blocks, size, width), owners, shares)
    incoming = lax.all_to_all(outgoing, ("narrow", "wide"), 0, 0, tiled=True)
    cand = incoming.transpose(1, 0, 2, 3).reshape(-1, rows, width)
    part = score(
        jnp.stack([owner, side]), sel, first, second, query_block, lengths, pair_valid, query, cand, length
    )
    out = part
    for d in range(1, shares):
        out = out + lax.ppermute(part, "narrow", shift(d))
    return out


def place():
    owner = lax.axis_index("wide")
    return owner // 4, owner // 2 % 2, owner % 2, lax.axis_index("narrow")


def split_kernel(first, over, sel_count, *refs):
    if sel_count:
        sel_ref, refs = refs[0], refs[1:]
    states_ref, weight_ref, *outs, rows_ref, sems = refs
    _, x, _, side = place()
    blocks, part, _ = rows_ref.shape
    size = part // 16
    start = pl.multiple_of((side ^ over) * part, part)

    def load(b):
        return pltpu.make_async_copy(
            states_ref.at[first + b, pl.ds(start, part)], rows_ref.at[b], sems.at[b]
        )

    for b in range(blocks):
        load(b).start()
    for b in range(blocks):
        load(b).wait()
        for z in range(4):
            for dx in range(2):
                source = pl.multiple_of((x ^ dx) * (2 * size) + z * 4 * size, 16)
                both = jnp.dot(
                    rows_ref[b, pl.ds(source, 2 * size)],
                    weight_ref[...],
                    preferred_element_type=jnp.float32,
                ).astype(jnp.bfloat16)
                for c in range(2):
                    target = ((z * 2 + c) * blocks + b) * size
                    outs[dx][target : target + size] = both[c * size : (c + 1) * size]
    if sel_count:
        lane = lax.broadcasted_iota(jnp.int32, (16, outs[0].shape[1]), 1)
        row = jnp.zeros_like(lane)
        for k in range(sel_count):
            row = jnp.where(lane == k, sel_ref[k], row)
        row = row.astype(jnp.float32).astype(jnp.bfloat16)
        for out_ref in outs:
            out_ref[8 * blocks * size :] = row


def split(over, sel, states, weight, first):
    _, rows, width = states.shape
    out_width = weight.shape[1]
    part = rows // 2
    sel_count = 0 if sel is None else sel.shape[0]
    out_rows = 8 * CHUNK * (part // 16) + (16 if sel_count else 0)
    scalars = () if sel is None else (sel,)
    return pl.pallas_call(
        functools.partial(split_kernel, first, over, sel_count),
        out_shape=(jax.ShapeDtypeStruct((out_rows, out_width), jnp.bfloat16),) * 2,
        in_specs=[pl.BlockSpec(memory_space=SMEM)] * len(scalars)
        + [pl.BlockSpec(memory_space=pltpu.HBM), pl.BlockSpec(memory_space=VMEM)],
        out_specs=[pl.BlockSpec(memory_space=VMEM)] * 2,
        scratch_shapes=[
            VMEM((CHUNK, part, width), jnp.bfloat16),
            pltpu.SemaphoreType.DMA((CHUNK,)),
        ],
        compiler_params=vmem_params(50),
        cost_estimate=pl.CostEstimate(
            flops=2 * CHUNK * part * width * out_width,
            bytes_accessed=2 * CHUNK * part * width,
            transcendentals=0,
        ),
    )(*scalars, states, weight)


def gather_unit_kernel(size, before, own_ref, x_ref, y_ref, xy_ref, *refs):
    z, _, c, _ = place()
    earlier, sends, query = refs[:before], refs[before : before + 8], refs[before + 8 :]
    span = CHUNK * size
    base = 0
    for ref, out_ref in zip(earlier, query):
        base = ref.shape[0]
        out_ref[:base] = ref[...]
    for rel, send_ref in enumerate(sends):
        source = pl.multiple_of(((z ^ (rel // 2)) * 2 + (c ^ (rel % 2))) * span, 16)
        for dx, (one_ref, two_ref) in enumerate(((own_ref, y_ref), (x_ref, xy_ref))):
            total = one_ref[pl.ds(source, span)].astype(jnp.float32)
            total = total + two_ref[pl.ds(source, span)].astype(jnp.float32)
            norm = jnp.sum(total * total, axis=-1, keepdims=True)
            unit = (total * lax.rsqrt(norm + 1e-06)).astype(jnp.bfloat16)
            send_ref[dx * span : (dx + 1) * span] = unit
            query[dx][pl.ds(pl.multiple_of(base + source, 16), span)] = unit
        if send_ref.shape[0] > 2 * span:
            row = lax.broadcasted_iota(jnp.int32, (16, own_ref.shape[1]), 0)
            send_ref[2 * span :] = jnp.where(
                row == 0,
                own_ref[8 * span :].astype(jnp.float32),
                x_ref[8 * span :].astype(jnp.float32),
            ).astype(jnp.bfloat16)


def gather_unit(own, x, y, xy, earlier, size):
    width = own.shape[1]
    span = CHUNK * size
    extra = own.shape[0] - 8 * span
    base = earlier[0].shape[0] if earlier else 0
    send = jax.ShapeDtypeStruct((2 * span + extra, width), jnp.bfloat16)
    query = jax.ShapeDtypeStruct((base + 8 * span, width), jnp.bfloat16)
    return pl.pallas_call(
        functools.partial(gather_unit_kernel, size, len(earlier)),
        out_shape=(send,) * 8 + (query,) * 2,
        in_specs=[pl.BlockSpec(memory_space=VMEM)] * (4 + len(earlier)),
        out_specs=[pl.BlockSpec(memory_space=VMEM)] * 10,
        compiler_params=vmem_params(12),
    )(own, x, y, xy, *earlier)


def cube_route_kernel(size, slots, parts, *refs):
    spread, out_ref, pieces_ref, rows_ref, asked_ref, sem = refs[:parts], *refs[parts:]
    z, x, c, _ = place()
    blocks = pieces_ref.shape[0] // 16
    span = CHUNK * size
    for i, ref in enumerate(spread):
        first, rel = i // 8 * CHUNK, i % 8
        for dx in range(2):
            owner = (z ^ (rel // 2)) * 4 + (x ^ dx) * 2 + (c ^ (rel % 2))
            for b in range(CHUNK):
                begin = dx * span + b * size
                pieces_ref[owner * blocks + first + b] = ref[begin : begin + size]
            if ref.shape[0] > 2 * span:
                row = ref[2 * span :].astype(jnp.float32)[dx : dx + 1]
                rows_ref[pl.ds(owner, 1)] = row.astype(jnp.int32)
    copy = pltpu.make_async_copy(rows_ref, asked_ref, sem)
    copy.start()
    copy.wait()

    def step(d, carry):
        side = d // 16
        for k in range(slots):
            out_ref[d, k] = pieces_ref[asked_ref[d - side * 16, side * slots + k]]
        return carry

    lax.fori_loop(0, 32, step, 0, unroll=4)


def cube_route(spread, size, slots, blocks):
    width = spread[0].shape[1]
    return pl.pallas_call(
        functools.partial(cube_route_kernel, size, slots, len(spread)),
        out_shape=jax.ShapeDtypeStruct((32, slots, size, width), jnp.bfloat16),
        in_specs=[pl.BlockSpec(memory_space=VMEM)] * len(spread),
        out_specs=pl.BlockSpec(memory_space=VMEM),
        scratch_shapes=[
            VMEM((16 * blocks, size, width), jnp.bfloat16),
            VMEM((16, width), jnp.int32),
            SMEM((16, width), jnp.int32),
            pltpu.SemaphoreType.DMA,
        ],
        compiler_params=vmem_params(16),
    )(*spread)


def queries_kernel(size, *refs):
    parts, out_ref = refs[:-1], refs[-1]
    _, x, _, side = place()
    for rel, ref in enumerate(parts):
        base = (side ^ (rel // 2)) * (16 * size) + (x ^ (rel % 2)) * (2 * size)
        for first in range(0, out_ref.shape[0], CHUNK):
            for z in range(4):
                for c in range(2):
                    target = pl.multiple_of(base + z * 4 * size + c * size, 16)
                    for b in range(CHUNK):
                        begin = (8 * first + (z * 2 + c) * CHUNK + b) * size
                        out_ref[first + b, pl.ds(target, size)] = ref[begin : begin + size]


def queries(parts, size, blocks):
    width = parts[0].shape[1]
    return pl.pallas_call(
        functools.partial(queries_kernel, size),
        out_shape=jax.ShapeDtypeStruct((blocks, 32 * size, width), jnp.bfloat16),
        in_specs=[pl.BlockSpec(memory_space=VMEM)] * len(parts),
        out_specs=pl.BlockSpec(memory_space=VMEM),
        compiler_params=vmem_params(12),
    )(*parts)


def local_cube(states, proj_weight, lengths, query_block, cand_block, pair_valid):
    side = lax.axis_index("narrow").astype(jnp.int32)
    owner = lax.axis_index("wide").astype(jnp.int32)
    paras, length, width_part = states.shape
    width = proj_weight.shape[1]
    blocks = paras // BLK
    rows = BLK * length
    size = rows // 32
    slots = cand_block.shape[0] // 4
    flat = states.reshape(blocks, rows, width_part)

    def near(array, rel):
        flip = rel % 2 * 4 + rel // 2
        return lax.ppermute(array, ("wide", "narrow"), [(i, i ^ flip) for i in range(32)])

    def along(array, rel):
        flip = rel // 2 * 4 + rel % 2
        return lax.ppermute(array, "wide", [(i, i ^ flip) for i in range(16)])

    sel, first, second = plan(cand_block)
    spread, query_parts = [], ()
    for c in range(0, blocks, CHUNK):
        ids = sel if c + CHUNK == blocks else None
        far = split(1, ids, flat, proj_weight, c)
        own, aside = split(0, ids, flat, proj_weight, c)
        if c:
            far, aside, y, xy, x = lax.optimization_barrier((far, aside, y, xy, x))
        y, xy, x = near(far[0], 2), near(far[1], 3), near(aside, 1)
        *sends, own, other = gather_unit(own, x, y, xy, query_parts, size)
        moved = {rel: along(sends[rel], rel) for rel in (4, 5, 6, 7, 2, 3, 1)}
        spread += [sends[0]] + [moved[rel] for rel in range(1, 8)]
        query_parts = (own, other)
    outgoing = cube_route(spread, size, slots, blocks)
    outgoing, (own, other) = lax.optimization_barrier((outgoing, query_parts))
    incoming = lax.all_to_all(outgoing, ("narrow", "wide"), 0, 0, tiled=True)
    gathered = {2: near(own, 2), 3: near(other, 3), 1: near(other, 1)}
    query = queries([own] + [gathered[rel] for rel in (1, 2, 3)], size, blocks)
    cand = incoming.transpose(1, 0, 2, 3).reshape(-1, rows, width)
    part = score(
        jnp.stack([owner, side]), sel, first, second, query_block, lengths, pair_valid, query, cand, length
    )
    return part + lax.ppermute(part, "narrow", [(0, 1), (1, 0)])


def solution(mesh):
    in_specs = (P("wide", None, "narrow"), P("narrow", None), P(), P("wide"), P("wide"), P("wide"))
    out_specs = P("wide", None, None)
    cube = mesh.shape["wide"] == 16 and mesh.shape["narrow"] == 2
    local = local_cube if cube else local_general
    return jax.shard_map(local, mesh=mesh, in_specs=in_specs, out_specs=out_specs, check_vma=False)
```

```python
import functools
import math

import jax
import jax.numpy as jnp
from jax import lax
from jax.experimental import pallas as pl
from jax.experimental.pallas import tpu as pltpu
from jax.sharding import PartitionSpec as P

BLK = 12
SHARPNESS = 20.0
EXP2_SCALE = SHARPNESS * math.log2(math.e)
COLS = 256
CHUNK = 4
SMEM = pltpu.SMEM
VMEM = pltpu.VMEM


def vmem_params(mib):
    return pltpu.CompilerParams(vmem_limit_bytes=mib * 2**20)


def plan_kernel(pairs, cand_ref, sel_ref, first_ref, second_ref, slot_ref):
    def step(k, count):
        block = cand_ref[k]
        found = lax.fori_loop(
            0, k, lambda e, f: jnp.where(cand_ref[e] == block, slot_ref[e], f), jnp.int32(-1)
        )
        new = found < 0
        slot = jnp.where(new, count, found)
        slot = jnp.minimum(slot, pairs // 2 - 1)
        slot_ref[k] = slot

        @pl.when(new)
        def _():
            sel_ref[slot] = block
            first_ref[slot] = k
            second_ref[slot] = k

        @pl.when(jnp.logical_not(new))
        def _():
            second_ref[slot] = k

        return count + new.astype(jnp.int32)

    lax.fori_loop(0, pairs, step, jnp.int32(0))


def plan(cand_block):
    pairs = cand_block.shape[0]
    out = jax.ShapeDtypeStruct((pairs // 2,), jnp.int32)
    return pl.pallas_call(
        functools.partial(plan_kernel, pairs),
        out_shape=(out, out, out),
        in_specs=[pl.BlockSpec(memory_space=SMEM)],
        out_specs=[pl.BlockSpec(memory_space=SMEM)] * 3,
        scratch_shapes=[SMEM((pairs,), jnp.int32)],
    )(cand_block)


def project_kernel(me_ref, states_ref, weight_ref, out_ref):
    out_ref[0, 0] = jnp.dot(
        states_ref[0], weight_ref[...], preferred_element_type=jnp.float32
    ).astype(out_ref.dtype)


def project(me, states, weight, shares, offset, count, dtype):
    blocks, rows, width = states.shape
    out_width = weight.shape[1]
    part = rows // shares
    return pl.pallas_call(
        project_kernel,
        out_shape=jax.ShapeDtypeStruct((count, blocks, part, out_width), dtype),
        grid_spec=pltpu.PrefetchScalarGridSpec(
            num_scalar_prefetch=1,
            grid=(count, blocks),
            in_specs=[
                pl.BlockSpec(
                    (1, part, width), lambda d, b, m: (b, lax.rem(m[0] + offset + d, shares), 0)
                ),
                pl.BlockSpec((width, out_width), lambda d, b, m: (0, 0)),
            ],
            out_specs=pl.BlockSpec((1, 1, part, out_width), lambda d, b, m: (d, b, 0, 0)),
        ),
        cost_estimate=pl.CostEstimate(
            flops=2 * count * blocks * part * width * out_width,
            bytes_accessed=2 * count * blocks * part * width,
            transcendentals=0,
        ),
    )(me, states, weight)


def unit_kernel(others, pieces, keep_ref, *refs):
    out_ref = refs[-1]
    total = keep_ref[0, 0]
    for ref in refs[:others]:
        total = total + ref[0].astype(jnp.float32)
    norm = jnp.sum(total * total, axis=-1, keepdims=True)
    unit = (total * lax.rsqrt(norm + 1e-06)).astype(jnp.bfloat16)
    if pieces is None:
        out_ref[0] = unit
    else:
        size = unit.shape[0] // pieces
        for m in range(pieces):
            out_ref[m, 0] = unit[m * size : (m + 1) * size]


def unit_rows(keep, received, owners):
    _, blocks, part, width = keep.shape
    size = part // owners
    direct = size % 16 == 0
    if direct:
        shape = (owners, blocks, size, width)
        out_spec = pl.BlockSpec((owners, 1, size, width), lambda b: (0, b, 0, 0))
    else:
        shape = (blocks, part, width)
        out_spec = pl.BlockSpec((1, part, width), lambda b: (b, 0, 0))
    out = pl.pallas_call(
        functools.partial(unit_kernel, len(received), owners if direct else None),
        out_shape=jax.ShapeDtypeStruct(shape, jnp.bfloat16),
        grid=(blocks,),
        in_specs=[pl.BlockSpec((1, 1, part, width), lambda b: (0, b, 0, 0))]
        + [pl.BlockSpec((1, part, width), lambda b: (b, 0, 0))] * len(received),
        out_specs=out_spec,
    )(keep, *received)
    if direct:
        return out
    return out.reshape(blocks, owners, size, width).transpose(1, 0, 2, 3)


def route_kernel(dests, slots, owners, asked_ref, pieces_ref, out_ref):
    def step(d, carry):
        side = d // owners
        requester = d - side * owners
        for k in range(slots):
            out_ref[d, k] = pieces_ref[asked_ref[requester, side * slots + k]]
        return carry

    lax.fori_loop(0, dests, step, 0)


def route(asked, pieces, owners, shares):
    slots = asked.shape[1] // shares
    dests = owners * shares
    return pl.pallas_call(
        functools.partial(route_kernel, dests, slots, owners),
        out_shape=jax.ShapeDtypeStruct((dests, slots) + pieces.shape[1:], jnp.bfloat16),
        in_specs=[pl.BlockSpec(memory_space=SMEM), pl.BlockSpec(memory_space=VMEM)],
        out_specs=pl.BlockSpec(memory_space=VMEM),
        compiler_params=vmem_params(48),
    )(asked, pieces)


def score_kernel(
    length, where_ref, sel_ref, first_ref, second_ref, query_block_ref, lengths_ref, valid_ref,
    query_ref, cand_ref, out_ref, totals_ref, *block_refs,
):
    owner, side = where_ref[0], where_ref[1]
    rows = query_ref.shape[1]
    slots = cand_ref.shape[-3]
    blocks = query_ref.shape[0]
    out_ref[...] = jnp.zeros_like(out_ref)
    totals_ref[...] = jnp.ones_like(totals_ref)
    upper = lax.broadcasted_iota(jnp.int32, (length // 2, COLS), 0) + length // 2
    lane = lax.broadcasted_iota(jnp.int32, (16, length), 1)

    def pair_step(i, carry):
        k = i // 2
        slot = side * slots + k
        block = sel_ref[slot]
        pair = jnp.where(i - 2 * k == 0, first_ref[slot], second_ref[slot])
        query = query_block_ref[pair]
        if block_refs:
            pieces, _, size, _ = cand_ref.shape
            for piece in range(pieces):
                block_refs[0][piece * size : (piece + 1) * size] = cand_ref[piece, k]
        for start in range(0, rows, COLS):
            sim = lax.dot_general(
                block_refs[0][...] if block_refs else cand_ref[k],
                query_ref[query, start : start + COLS],
                (((1,), (1,)), ((), ())),
                preferred_element_type=jnp.float32,
            )
            for b in range(BLK):
                live = lengths_ref[block * BLK + b]
                low = jnp.exp2(sim[b * length : b * length + length // 2] * EXP2_SCALE)
                high = jnp.exp2(sim[b * length + length // 2 : (b + 1) * length] * EXP2_SCALE)
                both = low + jnp.where(upper < live, high, 0.0)
                totals_ref[b : b + 1, start : start + COLS] = jnp.sum(both, axis=0, keepdims=True)
        score = jnp.zeros((16, length), jnp.float32)
        for a in range(BLK):
            live = lengths_ref[(owner * blocks + query) * BLK + a]
            logs = jnp.log(totals_ref[:, a * length : (a + 1) * length])
            summed = jnp.sum(jnp.where(lane < live, logs, 0.0), axis=1, keepdims=True)
            score = jnp.where(lane == a, summed, score)
        keep = valid_ref[pair].astype(jnp.float32) / (SHARPNESS * length)
        out_ref[pair] = score[:BLK, :BLK] * keep
        return carry

    lax.fori_loop(0, 2 * slots, pair_step, 0)


def score(where, sel, first, second, query_block, lengths, valid, query, cand, length):
    pairs = query_block.shape[0]
    slots, width = cand.shape[-3], cand.shape[-1]
    rows = query.shape[1]
    count = 2 * slots * rows * rows
    block = [VMEM((rows, width), jnp.bfloat16)] if cand.ndim == 4 else []
    return pl.pallas_call(
        functools.partial(score_kernel, length),
        out_shape=jax.ShapeDtypeStruct((pairs, BLK, BLK), jnp.float32),
        in_specs=[pl.BlockSpec(memory_space=SMEM)] * 7 + [pl.BlockSpec(memory_space=VMEM)] * 2,
        out_specs=pl.BlockSpec(memory_space=VMEM),
        scratch_shapes=[VMEM((16, rows), jnp.float32)] + block,
        compiler_params=vmem_params(24),
        cost_estimate=pl.CostEstimate(
            flops=2 * count * width, bytes_accessed=4 * rows * width, transcendentals=count
        ),
    )(where, sel, first, second, query_block, lengths, valid, query, cand)


def local_general(states, proj_weight, lengths, query_block, cand_block, pair_valid):
    shares = lax.axis_size("narrow")
    owners = lax.axis_size("wide")
    side = lax.axis_index("narrow").astype(jnp.int32)
    owner = lax.axis_index("wide").astype(jnp.int32)
    paras, length, width_part = states.shape
    width = proj_weight.shape[1]
    blocks = paras // BLK
    rows = BLK * length
    flat = states.reshape(blocks, rows, width_part)
    me = side.reshape(1)

    def shift(d):
        return [(i, (i + d) % shares) for i in range(shares)]

    sel, first, second = plan(cand_block)
    sent = project(me, flat, proj_weight, shares, 1, shares - 1, jnp.bfloat16)
    received = [lax.ppermute(sent[d - 1], "narrow", shift(d)) for d in range(1, shares)]
    asked = lax.all_to_all(
        jnp.broadcast_to(sel[None], (owners,) + sel.shape), "wide", 0, 0, tiled=True
    )
    kept = project(me, flat, proj_weight, shares, 0, 1, jnp.float32)
    mine = unit_rows(kept, received, owners)
    spread = lax.all_to_all(mine, "wide", 0, 0, tiled=True)
    size = mine.shape[2]
    by_side = [mine] + [lax.ppermute(mine, "narrow", shift(d)) for d in range(1, shares)]
    order = jnp.stack(by_side)
    query = jnp.stack(
        [lax.dynamic_index_in_dim(order, lax.rem(side - s + shares, shares), 0, False) for s in range(shares)]
    )
    query = query.transpose(2, 0, 1, 3, 4).reshape(blocks, rows, width)
    outgoing = route(asked, spread.reshape(owners * blocks, size, width), owners, shares)
    incoming = lax.all_to_all(outgoing, ("narrow", "wide"), 0, 0, tiled=True)
    cand = incoming.transpose(1, 0, 2, 3).reshape(-1, rows, width)
    part = score(
        jnp.stack([owner, side]), sel, first, second, query_block, lengths, pair_valid, query, cand, length
    )
    out = part
    for d in range(1, shares):
        out = out + lax.ppermute(part, "narrow", shift(d))
    return out


def place():
    owner = lax.axis_index("wide")
    return owner // 4, owner // 2 % 2, owner % 2, lax.axis_index("narrow")


def split_kernel(first, over, states_ref, weight_ref, *refs):
    *outs, rows_ref, sems = refs
    _, x, _, side = place()
    blocks, part, _ = rows_ref.shape
    size = part // 16
    start = pl.multiple_of((side ^ over) * part, part)

    def load(b):
        return pltpu.make_async_copy(
            states_ref.at[first + b, pl.ds(start, part)], rows_ref.at[b], sems.at[b]
        )

    for b in range(blocks):
        load(b).start()
    for b in range(blocks):
        load(b).wait()
        for z in range(4):
            for dx in range(2):
                source = pl.multiple_of((x ^ dx) * (2 * size) + z * 4 * size, 16)
                both = jnp.dot(
                    rows_ref[b, pl.ds(source, 2 * size)],
                    weight_ref[...],
                    preferred_element_type=jnp.float32,
                ).astype(jnp.bfloat16)
                for c in range(2):
                    target = ((z * 2 + c) * blocks + b) * size
                    outs[dx][target : target + size] = both[c * size : (c + 1) * size]


def split(over, states, weight, first):
    _, rows, width = states.shape
    out_width = weight.shape[1]
    part = rows // 2
    out_rows = 8 * CHUNK * (part // 16)
    return pl.pallas_call(
        functools.partial(split_kernel, first, over),
        out_shape=(jax.ShapeDtypeStruct((out_rows, out_width), jnp.bfloat16),) * 2,
        in_specs=[pl.BlockSpec(memory_space=pltpu.HBM), pl.BlockSpec(memory_space=VMEM)],
        out_specs=[pl.BlockSpec(memory_space=VMEM)] * 2,
        scratch_shapes=[
            VMEM((CHUNK, part, width), jnp.bfloat16),
            pltpu.SemaphoreType.DMA((CHUNK,)),
        ],
        compiler_params=vmem_params(50),
        cost_estimate=pl.CostEstimate(
            flops=2 * CHUNK * part * width * out_width,
            bytes_accessed=2 * CHUNK * part * width,
            transcendentals=0,
        ),
    )(states, weight)


def gather_unit_kernel(size, sel_ref, sel_x_ref, own_ref, x_ref, y_ref, xy_ref, *outs):
    z, _, c, _ = place()
    sends, query = outs[:8], outs[8:]
    span = CHUNK * size
    shape = (16, own_ref.shape[1])
    row, lane = (lax.broadcasted_iota(jnp.int32, shape, axis) for axis in range(2))
    asked = jnp.zeros(shape, jnp.int32)
    for dx, ids_ref in enumerate((sel_ref, sel_x_ref)):
        for k in range(ids_ref.shape[0]):
            asked = jnp.where((row == dx) & (lane == k), ids_ref[k], asked)
    asked = asked.astype(jnp.float32).astype(jnp.bfloat16)
    for rel, send_ref in enumerate(sends):
        source = pl.multiple_of(((z ^ (rel // 2)) * 2 + (c ^ (rel % 2))) * span, 16)
        for dx, (one_ref, two_ref) in enumerate(((own_ref, y_ref), (x_ref, xy_ref))):
            total = one_ref[pl.ds(source, span)].astype(jnp.float32)
            total = total + two_ref[pl.ds(source, span)].astype(jnp.float32)
            norm = jnp.sum(total * total, axis=-1, keepdims=True)
            unit = (total * lax.rsqrt(norm + 1e-06)).astype(jnp.bfloat16)
            send_ref[dx * span : (dx + 1) * span] = unit
            query[dx][pl.ds(source, span)] = unit
        send_ref[2 * span :] = asked


def gather_unit(sel, sel_x, own, x, y, xy, size):
    rows, width = own.shape
    send = jax.ShapeDtypeStruct((2 * CHUNK * size + 16, width), jnp.bfloat16)
    query = jax.ShapeDtypeStruct((rows, width), jnp.bfloat16)
    return pl.pallas_call(
        functools.partial(gather_unit_kernel, size),
        out_shape=(send,) * 8 + (query,) * 2,
        in_specs=[pl.BlockSpec(memory_space=SMEM)] * 2 + [pl.BlockSpec(memory_space=VMEM)] * 4,
        out_specs=[pl.BlockSpec(memory_space=VMEM)] * 10,
        compiler_params=vmem_params(12),
    )(sel, sel_x, own, x, y, xy)


def cube_route_kernel(size, slots, parts, *refs):
    spread, out_ref, pieces_ref, rows_ref, asked_ref, sem = refs[:parts], *refs[parts:]
    z, x, c, _ = place()
    blocks = pieces_ref.shape[0] // 16
    span = CHUNK * size
    for i, ref in enumerate(spread):
        first, rel = i // 8 * CHUNK, i % 8
        for dx in range(2):
            owner = (z ^ (rel // 2)) * 4 + (x ^ dx) * 2 + (c ^ (rel % 2))
            for b in range(CHUNK):
                begin = dx * span + b * size
                pieces_ref[owner * blocks + first + b] = ref[begin : begin + size]
            if ref.shape[0] > 2 * span:
                row = ref[2 * span :].astype(jnp.float32)[dx : dx + 1]
                rows_ref[pl.ds(owner, 1)] = row.astype(jnp.int32)
    copy = pltpu.make_async_copy(rows_ref, asked_ref, sem)
    copy.start()
    copy.wait()

    def step(d, carry):
        side = d // 16
        for k in range(slots):
            out_ref[d, k] = pieces_ref[asked_ref[d - side * 16, side * slots + k]]
        return carry

    lax.fori_loop(0, 32, step, 0, unroll=4)


def cube_route(spread, size, slots, blocks):
    width = spread[0].shape[1]
    return pl.pallas_call(
        functools.partial(cube_route_kernel, size, slots, len(spread)),
        out_shape=jax.ShapeDtypeStruct((32, slots, size, width), jnp.bfloat16),
        in_specs=[pl.BlockSpec(memory_space=VMEM)] * len(spread),
        out_specs=pl.BlockSpec(memory_space=VMEM),
        scratch_shapes=[
            VMEM((16 * blocks, size, width), jnp.bfloat16),
            VMEM((16, width), jnp.int32),
            SMEM((16, width), jnp.int32),
            pltpu.SemaphoreType.DMA,
        ],
        compiler_params=vmem_params(16),
    )(*spread)


def queries_kernel(size, *refs):
    parts, out_ref = refs[:-1], refs[-1]
    _, x, _, side = place()
    for rel, ref in enumerate(parts):
        base = (side ^ (rel // 2)) * (16 * size) + (x ^ (rel % 2)) * (2 * size)
        for first in range(0, out_ref.shape[0], CHUNK):
            for z in range(4):
                for c in range(2):
                    target = pl.multiple_of(base + z * 4 * size + c * size, 16)
                    for b in range(CHUNK):
                        begin = (8 * first + (z * 2 + c) * CHUNK + b) * size
                        out_ref[first + b, pl.ds(target, size)] = ref[begin : begin + size]


def queries(parts, size, blocks):
    width = parts[0].shape[1]
    return pl.pallas_call(
        functools.partial(queries_kernel, size),
        out_shape=jax.ShapeDtypeStruct((blocks, 32 * size, width), jnp.bfloat16),
        in_specs=[pl.BlockSpec(memory_space=VMEM)] * len(parts),
        out_specs=pl.BlockSpec(memory_space=VMEM),
        compiler_params=vmem_params(12),
    )(*parts)


def local_cube(states, proj_weight, lengths, query_block, cand_block, pair_valid):
    side = lax.axis_index("narrow").astype(jnp.int32)
    owner = lax.axis_index("wide").astype(jnp.int32)
    paras, length, width_part = states.shape
    width = proj_weight.shape[1]
    blocks = paras // BLK
    rows = BLK * length
    size = rows // 32
    slots = cand_block.shape[0] // 4
    flat = states.reshape(blocks, rows, width_part)

    def near(array, rel):
        flip = rel % 2 * 4 + rel // 2
        return lax.ppermute(array, ("wide", "narrow"), [(i, i ^ flip) for i in range(32)])

    def along(array, rel):
        flip = rel // 2 * 4 + rel % 2
        return lax.ppermute(array, "wide", [(i, i ^ flip) for i in range(16)])

    sel, first, second = plan(cand_block)
    sel_x = near(sel, 1)
    far = split(1, flat, proj_weight, 0)
    weight, *far = lax.optimization_barrier((proj_weight, *far))
    y, xy = near(far[0], 2), near(far[1], 3)
    own, aside = split(0, flat, weight, 0)
    x = near(aside, 1)
    *sends, own, other = gather_unit(sel, sel_x, own, x, y, xy, size)
    moved = {rel: along(sends[rel], rel) for rel in (4, 5, 6, 7, 2, 3, 1)}
    other = near(other, 1)
    spread = [sends[0]] + [moved[rel] for rel in range(1, 8)]
    outgoing = cube_route(spread, size, slots, blocks)
    outgoing, own, other = lax.optimization_barrier((outgoing, own, other))
    incoming = lax.all_to_all(outgoing, ("narrow", "wide"), 0, 0, tiled=True)
    query = queries([own, other, near(own, 2), near(other, 2)], size, blocks)
    part = score(
        jnp.stack([owner, side]), sel, first, second, query_block, lengths, pair_valid, query, incoming, length
    )
    return part + lax.ppermute(part, "narrow", [(0, 1), (1, 0)])


def solution(mesh):
    in_specs = (P("wide", None, "narrow"), P("narrow", None), P(), P("wide"), P("wide"), P("wide"))
    out_specs = P("wide", None, None)
    cube = mesh.shape["wide"] == 16 and mesh.shape["narrow"] == 2
    local = local_cube if cube else local_general
    return jax.shard_map(local, mesh=mesh, in_specs=in_specs, out_specs=out_specs, check_vma=False)
```

```python
import functools
import math

import jax
import jax.numpy as jnp
from jax import lax
from jax.experimental import pallas as pl
from jax.experimental.pallas import tpu as pltpu
from jax.sharding import PartitionSpec as P

BLK = 12
SHARPNESS = 20.0
EXP2_SCALE = SHARPNESS * math.log2(math.e)
COLS = 256
CHUNK = 4
LINE = 32
SPREAD = (0, 4, 6, 5, 7, 2, 3, 1)
SMEM = pltpu.SMEM
VMEM = pltpu.VMEM


def vmem_params(mib):
    return pltpu.CompilerParams(vmem_limit_bytes=mib * 2**20)


def plan_kernel(pairs, slots, places_ref, cand_ref, query_block_ref, valid_ref, lengths_ref, sel_ref, table_ref, *scratch):
    first_ref, second_ref, slot_ref = scratch
    owner, side, blocks = places_ref[0], places_ref[1], places_ref[2]

    def step(k, count):
        block = cand_ref[k]
        found = lax.fori_loop(
            0, k, lambda e, f: jnp.where(cand_ref[e] == block, slot_ref[e], f), jnp.int32(-1)
        )
        new = found < 0
        slot = jnp.minimum(jnp.where(new, count, found), pairs // 2 - 1)
        slot_ref[k] = slot

        @pl.when(new)
        def _():
            sel_ref[slot] = block
            first_ref[slot] = k

        second_ref[slot] = k
        return count + new.astype(jnp.int32)

    lax.fori_loop(0, pairs, step, jnp.int32(0))

    def line(i, carry):
        k = i // 2
        slot = side * slots + k
        pair = jnp.where(i - 2 * k == 0, first_ref[slot], second_ref[slot])
        query = query_block_ref[pair]
        table_ref[i * LINE] = pair
        table_ref[i * LINE + 1] = query
        table_ref[i * LINE + 2] = valid_ref[pair]
        for a in range(BLK):
            table_ref[i * LINE + 3 + a] = lengths_ref[sel_ref[slot] * BLK + a]
            table_ref[i * LINE + 3 + BLK + a] = lengths_ref[(owner * blocks + query) * BLK + a]
        return carry

    lax.fori_loop(0, 2 * slots, line, 0)


def plan(places, cand_block, query_block, valid, lengths, slots):
    pairs = cand_block.shape[0]
    shapes = (pairs // 2, 2 * slots * LINE)
    return pl.pallas_call(
        functools.partial(plan_kernel, pairs, slots),
        out_shape=[jax.ShapeDtypeStruct((n,), jnp.int32) for n in shapes],
        in_specs=[pl.BlockSpec(memory_space=SMEM)] * 5,
        out_specs=[pl.BlockSpec(memory_space=SMEM)] * 2,
        scratch_shapes=[SMEM((pairs,), jnp.int32)] * 3,
    )(places, cand_block, query_block, valid, lengths)


def project_kernel(me_ref, states_ref, weight_ref, out_ref):
    out_ref[0, 0] = jnp.dot(
        states_ref[0], weight_ref[...], preferred_element_type=jnp.float32
    ).astype(out_ref.dtype)


def project(me, states, weight, shares, offset, count, dtype):
    blocks, rows, width = states.shape
    out_width = weight.shape[1]
    part = rows // shares
    return pl.pallas_call(
        project_kernel,
        out_shape=jax.ShapeDtypeStruct((count, blocks, part, out_width), dtype),
        grid_spec=pltpu.PrefetchScalarGridSpec(
            num_scalar_prefetch=1,
            grid=(count, blocks),
            in_specs=[
                pl.BlockSpec(
                    (1, part, width), lambda d, b, m: (b, lax.rem(m[0] + offset + d, shares), 0)
                ),
                pl.BlockSpec((width, out_width), lambda d, b, m: (0, 0)),
            ],
            out_specs=pl.BlockSpec((1, 1, part, out_width), lambda d, b, m: (d, b, 0, 0)),
        ),
        cost_estimate=pl.CostEstimate(
            flops=2 * count * blocks * part * width * out_width,
            bytes_accessed=2 * count * blocks * part * width,
            transcendentals=0,
        ),
    )(me, states, weight)


def unit_kernel(others, pieces, keep_ref, *refs):
    out_ref = refs[-1]
    total = keep_ref[0, 0]
    for ref in refs[:others]:
        total = total + ref[0].astype(jnp.float32)
    norm = jnp.sum(total * total, axis=-1, keepdims=True)
    unit = (total * lax.rsqrt(norm + 1e-06)).astype(jnp.bfloat16)
    if pieces is None:
        out_ref[0] = unit
    else:
        size = unit.shape[0] // pieces
        for m in range(pieces):
            out_ref[m, 0] = unit[m * size : (m + 1) * size]


def unit_rows(keep, received, owners):
    _, blocks, part, width = keep.shape
    size = part // owners
    direct = size % 16 == 0
    if direct:
        shape = (owners, blocks, size, width)
        out_spec = pl.BlockSpec((owners, 1, size, width), lambda b: (0, b, 0, 0))
    else:
        shape = (blocks, part, width)
        out_spec = pl.BlockSpec((1, part, width), lambda b: (b, 0, 0))
    out = pl.pallas_call(
        functools.partial(unit_kernel, len(received), owners if direct else None),
        out_shape=jax.ShapeDtypeStruct(shape, jnp.bfloat16),
        grid=(blocks,),
        in_specs=[pl.BlockSpec((1, 1, part, width), lambda b: (0, b, 0, 0))]
        + [pl.BlockSpec((1, part, width), lambda b: (b, 0, 0))] * len(received),
        out_specs=out_spec,
    )(keep, *received)
    if direct:
        return out
    return out.reshape(blocks, owners, size, width).transpose(1, 0, 2, 3)


def route_kernel(dests, slots, owners, asked_ref, pieces_ref, out_ref):
    def step(d, carry):
        side = d // owners
        requester = d - side * owners
        for k in range(slots):
            out_ref[d, k] = pieces_ref[asked_ref[requester, side * slots + k]]
        return carry

    lax.fori_loop(0, dests, step, 0)


def route(asked, pieces, owners, shares):
    slots = asked.shape[1] // shares
    dests = owners * shares
    return pl.pallas_call(
        functools.partial(route_kernel, dests, slots, owners),
        out_shape=jax.ShapeDtypeStruct((dests, slots) + pieces.shape[1:], jnp.bfloat16),
        in_specs=[pl.BlockSpec(memory_space=SMEM), pl.BlockSpec(memory_space=VMEM)],
        out_specs=pl.BlockSpec(memory_space=VMEM),
        compiler_params=vmem_params(48),
    )(asked, pieces)


def query_rows(parts, out_ref):
    _, x, _, side = place()
    size = out_ref.shape[1] // 32
    blocks = out_ref.shape[0]
    for rel, ref in enumerate(parts):
        base = (side ^ (rel // 2)) * (16 * size) + (x ^ (rel % 2)) * (2 * size)
        for z in range(4):
            for c in range(2):
                target = pl.multiple_of(base + z * 4 * size + c * size, 16)
                for b in range(blocks):
                    begin = ((z * 2 + c) * blocks + b) * size
                    out_ref[b, pl.ds(target, size)] = ref[begin : begin + size]


def score_kernel(length, parts, table_ref, *refs):
    if parts:
        cand_ref, out_ref, totals_ref, block_ref, query_ref = refs[parts:]
        query_rows(refs[:parts], query_ref)
    else:
        query_ref, cand_ref, out_ref, totals_ref = refs
    rows = query_ref.shape[1]
    slots = cand_ref.shape[-3]
    out_ref[...] = jnp.zeros_like(out_ref)
    totals_ref[...] = jnp.ones_like(totals_ref)
    upper = lax.broadcasted_iota(jnp.int32, (length // 2, COLS), 0) + length // 2
    lane = lax.broadcasted_iota(jnp.int32, (16, length), 1)

    def pair_step(i, carry):
        k = i // 2
        line = i * LINE
        pair, query = table_ref[line], table_ref[line + 1]
        if parts:
            pieces, _, size, _ = cand_ref.shape
            for piece in range(pieces):
                block_ref[piece * size : (piece + 1) * size] = cand_ref[piece, k]
        for start in range(0, rows, COLS):
            sim = lax.dot_general(
                block_ref[...] if parts else cand_ref[k],
                query_ref[query, start : start + COLS],
                (((1,), (1,)), ((), ())),
                preferred_element_type=jnp.float32,
            )
            for b in range(BLK):
                live = table_ref[line + 3 + b]
                low = jnp.exp2(sim[b * length : b * length + length // 2] * EXP2_SCALE)
                high = jnp.exp2(sim[b * length + length // 2 : (b + 1) * length] * EXP2_SCALE)
                both = low + jnp.where(upper < live, high, 0.0)
                totals_ref[b : b + 1, start : start + COLS] = jnp.sum(both, axis=0, keepdims=True)
        score = jnp.zeros((16, length), jnp.float32)
        for a in range(BLK):
            live = table_ref[line + 3 + BLK + a]
            logs = jnp.log(totals_ref[:, a * length : (a + 1) * length])
            summed = jnp.sum(jnp.where(lane < live, logs, 0.0), axis=1, keepdims=True)
            score = jnp.where(lane == a, summed, score)
        keep = table_ref[line + 2].astype(jnp.float32) / (SHARPNESS * length)
        out_ref[pair] = score[:BLK, :BLK] * keep
        return carry

    lax.fori_loop(0, 2 * slots, pair_step, 0)


def score(table, query, cand, pairs, blocks, length):
    slots, width = cand.shape[-3], cand.shape[-1]
    rows = BLK * length
    parts = len(query) if isinstance(query, list) else 0
    count = 2 * slots * rows * rows
    scratch = [VMEM((16, rows), jnp.float32)]
    if parts:
        scratch += [VMEM((rows, width), jnp.bfloat16), VMEM((blocks, rows, width), jnp.bfloat16)]
    return pl.pallas_call(
        functools.partial(score_kernel, length, parts),
        out_shape=jax.ShapeDtypeStruct((pairs, BLK, BLK), jnp.float32),
        in_specs=[pl.BlockSpec(memory_space=SMEM)]
        + [pl.BlockSpec(memory_space=VMEM)] * (max(parts, 1) + 1),
        out_specs=pl.BlockSpec(memory_space=VMEM),
        scratch_shapes=scratch,
        compiler_params=vmem_params(28),
        cost_estimate=pl.CostEstimate(
            flops=2 * count * width, bytes_accessed=4 * rows * width, transcendentals=count
        ),
    )(table, *(query if parts else [query]), cand)


def local_general(states, proj_weight, lengths, query_block, cand_block, pair_valid):
    shares = lax.axis_size("narrow")
    owners = lax.axis_size("wide")
    side = lax.axis_index("narrow").astype(jnp.int32)
    owner = lax.axis_index("wide").astype(jnp.int32)
    paras, length, width_part = states.shape
    width = proj_weight.shape[1]
    blocks = paras // BLK
    rows = BLK * length
    flat = states.reshape(blocks, rows, width_part)
    me = side.reshape(1)

    def shift(d):
        return [(i, (i + d) % shares) for i in range(shares)]

    slots = cand_block.shape[0] // 2 // shares
    places = jnp.stack([owner, side, jnp.int32(blocks)])
    sel, table = plan(places, cand_block, query_block, pair_valid, lengths, slots)
    sent = project(me, flat, proj_weight, shares, 1, shares - 1, jnp.bfloat16)
    received = [lax.ppermute(sent[d - 1], "narrow", shift(d)) for d in range(1, shares)]
    asked = lax.all_to_all(
        jnp.broadcast_to(sel[None], (owners,) + sel.shape), "wide", 0, 0, tiled=True
    )
    kept = project(me, flat, proj_weight, shares, 0, 1, jnp.float32)
    mine = unit_rows(kept, received, owners)
    spread = lax.all_to_all(mine, "wide", 0, 0, tiled=True)
    size = mine.shape[2]
    by_side = [mine] + [lax.ppermute(mine, "narrow", shift(d)) for d in range(1, shares)]
    order = jnp.stack(by_side)
    query = jnp.stack(
        [lax.dynamic_index_in_dim(order, lax.rem(side - s + shares, shares), 0, False) for s in range(shares)]
    )
    query = query.transpose(2, 0, 1, 3, 4).reshape(blocks, rows, width)
    outgoing = route(asked, spread.reshape(owners * blocks, size, width), owners, shares)
    incoming = lax.all_to_all(outgoing, ("narrow", "wide"), 0, 0, tiled=True)
    cand = incoming.transpose(1, 0, 2, 3).reshape(-1, rows, width)
    part = score(table, query, cand, cand_block.shape[0], blocks, length)
    out = part
    for d in range(1, shares):
        out = out + lax.ppermute(part, "narrow", shift(d))
    return out


def place():
    owner = lax.axis_index("wide")
    return owner // 4, owner // 2 % 2, owner % 2, lax.axis_index("narrow")


def split_kernel(first, over, states_ref, weight_ref, *refs):
    *outs, rows_ref, sems = refs
    _, x, _, side = place()
    blocks, part, _ = rows_ref.shape
    size = part // 16
    start = pl.multiple_of((side ^ over) * part, part)

    def load(b):
        return pltpu.make_async_copy(
            states_ref.at[first + b, pl.ds(start, part)], rows_ref.at[b], sems.at[b]
        )

    for b in range(blocks):
        load(b).start()
    for b in range(blocks):
        load(b).wait()
        for z in range(4):
            for dx in range(2):
                source = pl.multiple_of((x ^ dx) * (2 * size) + z * 4 * size, 16)
                both = jnp.dot(
                    rows_ref[b, pl.ds(source, 2 * size)],
                    weight_ref[...],
                    preferred_element_type=jnp.float32,
                ).astype(jnp.bfloat16)
                for c in range(2):
                    target = ((z * 2 + c) * blocks + b) * size
                    outs[dx][target : target + size] = both[c * size : (c + 1) * size]


def split(over, states, weight, first):
    _, rows, width = states.shape
    out_width = weight.shape[1]
    part = rows // 2
    out_rows = 8 * CHUNK * (part // 16)
    return pl.pallas_call(
        functools.partial(split_kernel, first, over),
        out_shape=(jax.ShapeDtypeStruct((out_rows, out_width), jnp.bfloat16),) * 2,
        in_specs=[pl.BlockSpec(memory_space=pltpu.HBM), pl.BlockSpec(memory_space=VMEM)],
        out_specs=[pl.BlockSpec(memory_space=VMEM)] * 2,
        scratch_shapes=[
            VMEM((CHUNK, part, width), jnp.bfloat16),
            pltpu.SemaphoreType.DMA((CHUNK,)),
        ],
        compiler_params=vmem_params(50),
        cost_estimate=pl.CostEstimate(
            flops=2 * CHUNK * part * width * out_width,
            bytes_accessed=2 * CHUNK * part * width,
            transcendentals=0,
        ),
    )(states, weight)


def gather_unit_kernel(size, sel_ref, sel_x_ref, y_ref, xy_ref, own_ref, x_ref, *outs):
    z, _, c, _ = place()
    sends, query = outs[:8], outs[8:]
    span = CHUNK * size
    shape = (16, own_ref.shape[1])
    row, lane = (lax.broadcasted_iota(jnp.int32, shape, axis) for axis in range(2))
    asked = jnp.zeros(shape, jnp.int32)
    for dx, ids_ref in enumerate((sel_ref, sel_x_ref)):
        for k in range(ids_ref.shape[0]):
            asked = jnp.where((row == dx) & (lane == k), ids_ref[k], asked)
    asked = asked.astype(jnp.float32).astype(jnp.bfloat16)
    for rel, send_ref in enumerate(sends):
        source = pl.multiple_of(((z ^ (rel // 2)) * 2 + (c ^ (rel % 2))) * span, 16)
        for dx, (one_ref, two_ref) in enumerate(((own_ref, y_ref), (x_ref, xy_ref))):
            total = one_ref[pl.ds(source, span)].astype(jnp.float32)
            total = total + two_ref[pl.ds(source, span)].astype(jnp.float32)
            norm = jnp.sum(total * total, axis=-1, keepdims=True)
            unit = (total * lax.rsqrt(norm + 1e-06)).astype(jnp.bfloat16)
            send_ref[dx * span : (dx + 1) * span] = unit
            query[dx][pl.ds(source, span)] = unit
        send_ref[2 * span :] = asked


def gather_unit(sel, sel_x, y, xy, own, x, size):
    rows, width = own.shape
    send = jax.ShapeDtypeStruct((2 * CHUNK * size + 16, width), jnp.bfloat16)
    query = jax.ShapeDtypeStruct((rows, width), jnp.bfloat16)
    return pl.pallas_call(
        functools.partial(gather_unit_kernel, size),
        out_shape=(send,) * 8 + (query,) * 2,
        in_specs=[pl.BlockSpec(memory_space=SMEM)] * 2 + [pl.BlockSpec(memory_space=VMEM)] * 4,
        out_specs=[pl.BlockSpec(memory_space=VMEM)] * 10,
        compiler_params=vmem_params(12),
    )(sel, sel_x, y, xy, own, x)


def cube_route_kernel(size, slots, parts, *refs):
    spread, out_ref, pieces_ref, rows_ref, asked_ref, sem = refs[:parts], *refs[parts:]
    z, x, c, _ = place()
    blocks = pieces_ref.shape[0] // 16
    span = CHUNK * size
    for rel, ref in zip(SPREAD, spread):
        for dx in range(2):
            owner = (z ^ (rel // 2)) * 4 + (x ^ dx) * 2 + (c ^ (rel % 2))
            for b in range(CHUNK):
                begin = dx * span + b * size
                pieces_ref[owner * blocks + b] = ref[begin : begin + size]
            row = ref[2 * span :].astype(jnp.float32)[dx : dx + 1]
            rows_ref[pl.ds(owner, 1)] = row.astype(jnp.int32)
    copy = pltpu.make_async_copy(rows_ref, asked_ref, sem)
    copy.start()
    copy.wait()

    def step(d, carry):
        side = d // 16
        for k in range(slots):
            out_ref[d, k] = pieces_ref[asked_ref[d - side * 16, side * slots + k]]
        return carry

    lax.fori_loop(0, 32, step, 0, unroll=4)


def cube_route(spread, size, slots, blocks):
    width = spread[0].shape[1]
    return pl.pallas_call(
        functools.partial(cube_route_kernel, size, slots, len(spread)),
        out_shape=jax.ShapeDtypeStruct((32, slots, size, width), jnp.bfloat16),
        in_specs=[pl.BlockSpec(memory_space=VMEM)] * len(spread),
        out_specs=pl.BlockSpec(memory_space=VMEM),
        scratch_shapes=[
            VMEM((16 * blocks, size, width), jnp.bfloat16),
            VMEM((16, width), jnp.int32),
            SMEM((16, width), jnp.int32),
            pltpu.SemaphoreType.DMA,
        ],
        compiler_params=vmem_params(16),
    )(*spread)


def local_cube(states, proj_weight, lengths, query_block, cand_block, pair_valid):
    side = lax.axis_index("narrow").astype(jnp.int32)
    owner = lax.axis_index("wide").astype(jnp.int32)
    paras, length, width_part = states.shape
    width = proj_weight.shape[1]
    blocks = paras // BLK
    rows = BLK * length
    size = rows // 32
    slots = cand_block.shape[0] // 4
    flat = states.reshape(blocks, rows, width_part)

    def near(array, rel):
        flip = rel % 2 * 4 + rel // 2
        return lax.ppermute(array, ("wide", "narrow"), [(i, i ^ flip) for i in range(32)])

    def along(array, rel):
        flip = rel // 2 * 4 + rel % 2
        return lax.ppermute(array, "wide", [(i, i ^ flip) for i in range(16)])

    places = jnp.stack([owner, side, jnp.int32(blocks)])
    sel, table = plan(places, cand_block, query_block, pair_valid, lengths, slots)
    sel_x = near(sel, 1)
    far = split(1, flat, proj_weight, 0)
    weight, *far = lax.optimization_barrier((proj_weight, *far))
    y, xy = near(far[0], 2), near(far[1], 3)
    own, aside = split(0, flat, weight, 0)
    x = near(aside, 1)
    *sends, own, other = gather_unit(sel, sel_x, y, xy, own, x, size)
    spread = [along(sends[rel], rel) if rel else sends[rel] for rel in SPREAD]
    own_y, other = near(own, 2), near(other, 1)
    outgoing = cube_route(spread, size, slots, blocks)
    outgoing, own_y, other = lax.optimization_barrier((outgoing, own_y, other))
    incoming = lax.all_to_all(outgoing, ("narrow", "wide"), 0, 0, tiled=True)
    query = [own, other, own_y, near(other, 2)]
    part = score(table, query, incoming, cand_block.shape[0], blocks, length)
    return part + lax.ppermute(part, "narrow", [(0, 1), (1, 0)])


def solution(mesh):
    in_specs = (P("wide", None, "narrow"), P("narrow", None), P(), P("wide"), P("wide"), P("wide"))
    out_specs = P("wide", None, None)
    cube = mesh.shape["wide"] == 16 and mesh.shape["narrow"] == 2
    local = local_cube if cube else local_general
    return jax.shard_map(local, mesh=mesh, in_specs=in_specs, out_specs=out_specs, check_vma=False)
```

```python
import functools
import math

import jax
import jax.numpy as jnp
from jax import lax
from jax.experimental import pallas as pl
from jax.experimental.pallas import tpu as pltpu
from jax.sharding import PartitionSpec as P

BLK = 12
SHARPNESS = 20.0
EXP2_SCALE = SHARPNESS * math.log2(math.e)
COLS = 256
CHUNK = 4
LINE = 32
SPREAD = (0, 1, 2, 4, 3, 6, 5, 7)
SMEM = pltpu.SMEM
VMEM = pltpu.VMEM


def vmem_params(mib):
    return pltpu.CompilerParams(vmem_limit_bytes=mib * 2**20)


def plan_kernel(pairs, slots, places_ref, cand_ref, query_block_ref, valid_ref, lengths_ref, sel_ref, table_ref, *scratch):
    first_ref, second_ref, slot_ref = scratch
    owner, side, blocks = places_ref[0], places_ref[1], places_ref[2]

    def step(k, count):
        block = cand_ref[k]
        found = lax.fori_loop(
            0, k, lambda e, f: jnp.where(cand_ref[e] == block, slot_ref[e], f), jnp.int32(-1)
        )
        new = found < 0
        slot = jnp.minimum(jnp.where(new, count, found), pairs // 2 - 1)
        slot_ref[k] = slot

        @pl.when(new)
        def _():
            sel_ref[slot] = block
            first_ref[slot] = k

        second_ref[slot] = k
        return count + new.astype(jnp.int32)

    lax.fori_loop(0, pairs, step, jnp.int32(0))

    def line(i, carry):
        k = i // 2
        slot = side * slots + k
        pair = jnp.where(i - 2 * k == 0, first_ref[slot], second_ref[slot])
        query = query_block_ref[pair]
        table_ref[i * LINE] = pair
        table_ref[i * LINE + 1] = query
        table_ref[i * LINE + 2] = valid_ref[pair]
        for a in range(BLK):
            table_ref[i * LINE + 3 + a] = lengths_ref[sel_ref[slot] * BLK + a]
            table_ref[i * LINE + 3 + BLK + a] = lengths_ref[(owner * blocks + query) * BLK + a]
        return carry

    lax.fori_loop(0, 2 * slots, line, 0)


def plan(places, cand_block, query_block, valid, lengths, slots):
    pairs = cand_block.shape[0]
    shapes = (pairs // 2, 2 * slots * LINE)
    return pl.pallas_call(
        functools.partial(plan_kernel, pairs, slots),
        out_shape=[jax.ShapeDtypeStruct((n,), jnp.int32) for n in shapes],
        in_specs=[pl.BlockSpec(memory_space=SMEM)] * 5,
        out_specs=[pl.BlockSpec(memory_space=SMEM)] * 2,
        scratch_shapes=[SMEM((pairs,), jnp.int32)] * 3,
    )(places, cand_block, query_block, valid, lengths)


def project_kernel(me_ref, states_ref, weight_ref, out_ref):
    out_ref[0, 0] = jnp.dot(
        states_ref[0], weight_ref[...], preferred_element_type=jnp.float32
    ).astype(out_ref.dtype)


def project(me, states, weight, shares, offset, count, dtype):
    blocks, rows, width = states.shape
    out_width = weight.shape[1]
    part = rows // shares
    return pl.pallas_call(
        project_kernel,
        out_shape=jax.ShapeDtypeStruct((count, blocks, part, out_width), dtype),
        grid_spec=pltpu.PrefetchScalarGridSpec(
            num_scalar_prefetch=1,
            grid=(count, blocks),
            in_specs=[
                pl.BlockSpec(
                    (1, part, width), lambda d, b, m: (b, lax.rem(m[0] + offset + d, shares), 0)
                ),
                pl.BlockSpec((width, out_width), lambda d, b, m: (0, 0)),
            ],
            out_specs=pl.BlockSpec((1, 1, part, out_width), lambda d, b, m: (d, b, 0, 0)),
        ),
        cost_estimate=pl.CostEstimate(
            flops=2 * count * blocks * part * width * out_width,
            bytes_accessed=2 * count * blocks * part * width,
            transcendentals=0,
        ),
    )(me, states, weight)


def unit_kernel(others, pieces, keep_ref, *refs):
    out_ref = refs[-1]
    total = keep_ref[0, 0]
    for ref in refs[:others]:
        total = total + ref[0].astype(jnp.float32)
    norm = jnp.sum(total * total, axis=-1, keepdims=True)
    unit = (total * lax.rsqrt(norm + 1e-06)).astype(jnp.bfloat16)
    if pieces is None:
        out_ref[0] = unit
    else:
        size = unit.shape[0] // pieces
        for m in range(pieces):
            out_ref[m, 0] = unit[m * size : (m + 1) * size]


def unit_rows(keep, received, owners):
    _, blocks, part, width = keep.shape
    size = part // owners
    direct = size % 16 == 0
    if direct:
        shape = (owners, blocks, size, width)
        out_spec = pl.BlockSpec((owners, 1, size, width), lambda b: (0, b, 0, 0))
    else:
        shape = (blocks, part, width)
        out_spec = pl.BlockSpec((1, part, width), lambda b: (b, 0, 0))
    out = pl.pallas_call(
        functools.partial(unit_kernel, len(received), owners if direct else None),
        out_shape=jax.ShapeDtypeStruct(shape, jnp.bfloat16),
        grid=(blocks,),
        in_specs=[pl.BlockSpec((1, 1, part, width), lambda b: (0, b, 0, 0))]
        + [pl.BlockSpec((1, part, width), lambda b: (b, 0, 0))] * len(received),
        out_specs=out_spec,
    )(keep, *received)
    if direct:
        return out
    return out.reshape(blocks, owners, size, width).transpose(1, 0, 2, 3)


def route_kernel(dests, slots, owners, asked_ref, pieces_ref, out_ref):
    def step(d, carry):
        side = d // owners
        requester = d - side * owners
        for k in range(slots):
            out_ref[d, k] = pieces_ref[asked_ref[requester, side * slots + k]]
        return carry

    lax.fori_loop(0, dests, step, 0)


def route(asked, pieces, owners, shares):
    slots = asked.shape[1] // shares
    dests = owners * shares
    return pl.pallas_call(
        functools.partial(route_kernel, dests, slots, owners),
        out_shape=jax.ShapeDtypeStruct((dests, slots) + pieces.shape[1:], jnp.bfloat16),
        in_specs=[pl.BlockSpec(memory_space=SMEM), pl.BlockSpec(memory_space=VMEM)],
        out_specs=pl.BlockSpec(memory_space=VMEM),
        compiler_params=vmem_params(48),
    )(asked, pieces)


def query_rows(parts, out_ref):
    _, _, core, side = place()
    size = out_ref.shape[1] // 32
    blocks = out_ref.shape[0]
    for rel, ref in enumerate(parts):
        base = (side ^ (rel // 2)) * (16 * size) + (core ^ (rel % 2)) * (2 * size)
        for z in range(4):
            for x in range(2):
                target = pl.multiple_of(base + z * 4 * size + x * size, 16)
                for b in range(blocks):
                    begin = ((z * 2 + x) * blocks + b) * size
                    out_ref[b, pl.ds(target, size)] = ref[begin : begin + size]


def score_kernel(length, parts, table_ref, *refs):
    if parts:
        cand_ref, out_ref, totals_ref, block_ref, query_ref = refs[parts:]
        query_rows(refs[:parts], query_ref)
    else:
        query_ref, cand_ref, out_ref, totals_ref = refs
    rows = query_ref.shape[1]
    slots = cand_ref.shape[-3]
    out_ref[...] = jnp.zeros_like(out_ref)
    totals_ref[...] = jnp.ones_like(totals_ref)
    upper = lax.broadcasted_iota(jnp.int32, (length // 2, COLS), 0) + length // 2
    lane = lax.broadcasted_iota(jnp.int32, (16, length), 1)

    def pair_step(i, carry):
        k = i // 2
        line = i * LINE
        pair, query = table_ref[line], table_ref[line + 1]
        if parts:
            pieces, _, size, _ = cand_ref.shape
            for piece in range(pieces):
                begin = (piece // 4 * 4 + piece % 2 * 2 + piece // 2 % 2) * size
                block_ref[begin : begin + size] = cand_ref[piece, k]
        for start in range(0, rows, COLS):
            sim = lax.dot_general(
                block_ref[...] if parts else cand_ref[k],
                query_ref[query, start : start + COLS],
                (((1,), (1,)), ((), ())),
                preferred_element_type=jnp.float32,
            )
            for b in range(BLK):
                live = table_ref[line + 3 + b]
                low = jnp.exp2(sim[b * length : b * length + length // 2] * EXP2_SCALE)
                high = jnp.exp2(sim[b * length + length // 2 : (b + 1) * length] * EXP2_SCALE)
                both = low + jnp.where(upper < live, high, 0.0)
                totals_ref[b : b + 1, start : start + COLS] = jnp.sum(both, axis=0, keepdims=True)
        score = jnp.zeros((16, length), jnp.float32)
        for a in range(BLK):
            live = table_ref[line + 3 + BLK + a]
            logs = jnp.log(totals_ref[:, a * length : (a + 1) * length])
            summed = jnp.sum(jnp.where(lane < live, logs, 0.0), axis=1, keepdims=True)
            score = jnp.where(lane == a, summed, score)
        keep = table_ref[line + 2].astype(jnp.float32) / (SHARPNESS * length)
        out_ref[pair] = score[:BLK, :BLK] * keep
        return carry

    lax.fori_loop(0, 2 * slots, pair_step, 0)


def score(table, query, cand, pairs, blocks, length):
    slots, width = cand.shape[-3], cand.shape[-1]
    rows = BLK * length
    parts = len(query) if isinstance(query, list) else 0
    count = 2 * slots * rows * rows
    scratch = [VMEM((16, rows), jnp.float32)]
    if parts:
        scratch += [VMEM((rows, width), jnp.bfloat16), VMEM((blocks, rows, width), jnp.bfloat16)]
    return pl.pallas_call(
        functools.partial(score_kernel, length, parts),
        out_shape=jax.ShapeDtypeStruct((pairs, BLK, BLK), jnp.float32),
        in_specs=[pl.BlockSpec(memory_space=SMEM)]
        + [pl.BlockSpec(memory_space=VMEM)] * (max(parts, 1) + 1),
        out_specs=pl.BlockSpec(memory_space=VMEM),
        scratch_shapes=scratch,
        compiler_params=vmem_params(28),
        cost_estimate=pl.CostEstimate(
            flops=2 * count * width, bytes_accessed=4 * rows * width, transcendentals=count
        ),
    )(table, *(query if parts else [query]), cand)


def local_general(states, proj_weight, lengths, query_block, cand_block, pair_valid):
    shares = lax.axis_size("narrow")
    owners = lax.axis_size("wide")
    side = lax.axis_index("narrow").astype(jnp.int32)
    owner = lax.axis_index("wide").astype(jnp.int32)
    paras, length, width_part = states.shape
    width = proj_weight.shape[1]
    blocks = paras // BLK
    rows = BLK * length
    flat = states.reshape(blocks, rows, width_part)
    me = side.reshape(1)

    def shift(d):
        return [(i, (i + d) % shares) for i in range(shares)]

    slots = cand_block.shape[0] // 2 // shares
    places = jnp.stack([owner, side, jnp.int32(blocks)])
    sel, table = plan(places, cand_block, query_block, pair_valid, lengths, slots)
    sent = project(me, flat, proj_weight, shares, 1, shares - 1, jnp.bfloat16)
    received = [lax.ppermute(sent[d - 1], "narrow", shift(d)) for d in range(1, shares)]
    asked = lax.all_to_all(
        jnp.broadcast_to(sel[None], (owners,) + sel.shape), "wide", 0, 0, tiled=True
    )
    kept = project(me, flat, proj_weight, shares, 0, 1, jnp.float32)
    mine = unit_rows(kept, received, owners)
    spread = lax.all_to_all(mine, "wide", 0, 0, tiled=True)
    size = mine.shape[2]
    by_side = [mine] + [lax.ppermute(mine, "narrow", shift(d)) for d in range(1, shares)]
    order = jnp.stack(by_side)
    query = jnp.stack(
        [lax.dynamic_index_in_dim(order, lax.rem(side - s + shares, shares), 0, False) for s in range(shares)]
    )
    query = query.transpose(2, 0, 1, 3, 4).reshape(blocks, rows, width)
    outgoing = route(asked, spread.reshape(owners * blocks, size, width), owners, shares)
    incoming = lax.all_to_all(outgoing, ("narrow", "wide"), 0, 0, tiled=True)
    cand = incoming.transpose(1, 0, 2, 3).reshape(-1, rows, width)
    part = score(table, query, cand, cand_block.shape[0], blocks, length)
    out = part
    for d in range(1, shares):
        out = out + lax.ppermute(part, "narrow", shift(d))
    return out


def place():
    owner = lax.axis_index("wide")
    return owner // 4, owner // 2 % 2, owner % 2, lax.axis_index("narrow")


def split_kernel(first, over, states_ref, weight_ref, *refs):
    *outs, rows_ref, sems = refs
    _, _, core, side = place()
    blocks, part, _ = rows_ref.shape
    size = part // 16
    start = pl.multiple_of((side ^ over) * part, part)

    def load(b):
        return pltpu.make_async_copy(
            states_ref.at[first + b, pl.ds(start, part)], rows_ref.at[b], sems.at[b]
        )

    for b in range(blocks):
        load(b).start()
    for b in range(blocks):
        load(b).wait()
        for z in range(4):
            for flip in range(2):
                source = pl.multiple_of((core ^ flip) * (2 * size) + z * 4 * size, 16)
                both = jnp.dot(
                    rows_ref[b, pl.ds(source, 2 * size)],
                    weight_ref[...],
                    preferred_element_type=jnp.float32,
                ).astype(jnp.bfloat16)
                for x in range(2):
                    target = ((z * 2 + x) * blocks + b) * size
                    outs[flip][target : target + size] = both[x * size : (x + 1) * size]


def split(over, states, weight, first):
    _, rows, width = states.shape
    out_width = weight.shape[1]
    part = rows // 2
    out_rows = 8 * CHUNK * (part // 16)
    return pl.pallas_call(
        functools.partial(split_kernel, first, over),
        out_shape=(jax.ShapeDtypeStruct((out_rows, out_width), jnp.bfloat16),) * 2,
        in_specs=[pl.BlockSpec(memory_space=pltpu.HBM), pl.BlockSpec(memory_space=VMEM)],
        out_specs=[pl.BlockSpec(memory_space=VMEM)] * 2,
        scratch_shapes=[
            VMEM((CHUNK, part, width), jnp.bfloat16),
            pltpu.SemaphoreType.DMA((CHUNK,)),
        ],
        compiler_params=vmem_params(50),
        cost_estimate=pl.CostEstimate(
            flops=2 * CHUNK * part * width * out_width,
            bytes_accessed=2 * CHUNK * part * width,
            transcendentals=0,
        ),
    )(states, weight)


def gather_unit_kernel(size, sel_ref, sel_near_ref, y_ref, cy_ref, own_ref, c_ref, *outs):
    z, x, _, _ = place()
    sends, query = outs[:8], outs[8:]
    span = CHUNK * size
    shape = (16, own_ref.shape[1])
    row, lane = (lax.broadcasted_iota(jnp.int32, shape, axis) for axis in range(2))
    asked = jnp.zeros(shape, jnp.int32)
    for flip, ids_ref in enumerate((sel_ref, sel_near_ref)):
        for k in range(ids_ref.shape[0]):
            asked = jnp.where((row == flip) & (lane == k), ids_ref[k], asked)
    asked = asked.astype(jnp.float32).astype(jnp.bfloat16)
    for rel, send_ref in zip(SPREAD, sends):
        source = pl.multiple_of(((z ^ (rel // 2)) * 2 + (x ^ (rel % 2))) * span, 16)
        for flip, (one_ref, two_ref) in enumerate(((own_ref, y_ref), (c_ref, cy_ref))):
            total = one_ref[pl.ds(source, span)].astype(jnp.float32)
            total = total + two_ref[pl.ds(source, span)].astype(jnp.float32)
            norm = jnp.sum(total * total, axis=-1, keepdims=True)
            unit = (total * lax.rsqrt(norm + 1e-06)).astype(jnp.bfloat16)
            send_ref[flip * span : (flip + 1) * span] = unit
            query[flip][pl.ds(source, span)] = unit
        send_ref[2 * span :] = asked


def gather_unit(sel, sel_near, y, cy, own, c, size):
    rows, width = own.shape
    send = jax.ShapeDtypeStruct((2 * CHUNK * size + 16, width), jnp.bfloat16)
    query = jax.ShapeDtypeStruct((rows, width), jnp.bfloat16)
    return pl.pallas_call(
        functools.partial(gather_unit_kernel, size),
        out_shape=(send,) * 8 + (query,) * 2,
        in_specs=[pl.BlockSpec(memory_space=SMEM)] * 2 + [pl.BlockSpec(memory_space=VMEM)] * 4,
        out_specs=[pl.BlockSpec(memory_space=VMEM)] * 10,
        compiler_params=vmem_params(12),
    )(sel, sel_near, y, cy, own, c)


def cube_route_kernel(size, slots, parts, *refs):
    spread, out_ref, pieces_ref, rows_ref, asked_ref, sem = refs[:parts], *refs[parts:]
    z, x, core, _ = place()
    blocks = pieces_ref.shape[0] // 16
    span = CHUNK * size
    for rel, ref in zip(SPREAD, spread):
        for flip in range(2):
            owner = (z ^ (rel // 2)) * 4 + (x ^ (rel % 2)) * 2 + (core ^ flip)
            for b in range(CHUNK):
                begin = flip * span + b * size
                pieces_ref[owner * blocks + b] = ref[begin : begin + size]
            row = ref[2 * span :].astype(jnp.float32)[flip : flip + 1]
            rows_ref[pl.ds(owner, 1)] = row.astype(jnp.int32)
    copy = pltpu.make_async_copy(rows_ref, asked_ref, sem)
    copy.start()
    copy.wait()

    def step(d, carry):
        side = d // 16
        for k in range(slots):
            out_ref[d, k] = pieces_ref[asked_ref[d - side * 16, side * slots + k]]
        return carry

    lax.fori_loop(0, 32, step, 0, unroll=4)


def cube_route(spread, size, slots, blocks):
    width = spread[0].shape[1]
    return pl.pallas_call(
        functools.partial(cube_route_kernel, size, slots, len(spread)),
        out_shape=jax.ShapeDtypeStruct((32, slots, size, width), jnp.bfloat16),
        in_specs=[pl.BlockSpec(memory_space=VMEM)] * len(spread),
        out_specs=pl.BlockSpec(memory_space=VMEM),
        scratch_shapes=[
            VMEM((16 * blocks, size, width), jnp.bfloat16),
            VMEM((16, width), jnp.int32),
            SMEM((16, width), jnp.int32),
            pltpu.SemaphoreType.DMA,
        ],
        compiler_params=vmem_params(16),
    )(*spread)


def local_cube(states, proj_weight, lengths, query_block, cand_block, pair_valid):
    side = lax.axis_index("narrow").astype(jnp.int32)
    owner = lax.axis_index("wide").astype(jnp.int32)
    paras, length, width_part = states.shape
    width = proj_weight.shape[1]
    blocks = paras // BLK
    rows = BLK * length
    size = rows // 32
    slots = cand_block.shape[0] // 4
    flat = states.reshape(blocks, rows, width_part)

    def near(array, rel):
        flip = rel % 2 * 2 + rel // 2
        return lax.ppermute(array, ("wide", "narrow"), [(i, i ^ flip) for i in range(32)])

    def along(array, rel):
        flip = rel * 2
        return lax.ppermute(array, "wide", [(i, i ^ flip) for i in range(16)])

    places = jnp.stack([owner, side, jnp.int32(blocks)])
    sel, table = plan(places, cand_block, query_block, pair_valid, lengths, slots)
    sel_near = near(sel, 1)
    far = split(1, flat, proj_weight, 0)
    weight, *far = lax.optimization_barrier((proj_weight, *far))
    y, cy = near(far[0], 2), near(far[1], 3)
    own, aside = split(0, flat, weight, 0)
    c = near(aside, 1)
    *sends, own, other = gather_unit(sel, sel_near, y, cy, own, c, size)
    other = near(other, 1)
    sends[4], other = lax.optimization_barrier((sends[4], other))
    spread = [along(send, rel) if rel else send for rel, send in zip(SPREAD, sends)]
    own_y = near(own, 2)
    outgoing = cube_route(spread, size, slots, blocks)
    outgoing, own_y, other = lax.optimization_barrier((outgoing, own_y, other))
    incoming = lax.all_to_all(outgoing, ("narrow", "wide"), 0, 0, tiled=True)
    query = [own, other, own_y, near(other, 2)]
    part = score(table, query, incoming, cand_block.shape[0], blocks, length)
    return part + lax.ppermute(part, "narrow", [(0, 1), (1, 0)])


def solution(mesh):
    in_specs = (P("wide", None, "narrow"), P("narrow", None), P(), P("wide"), P("wide"), P("wide"))
    out_specs = P("wide", None, None)
    cube = mesh.shape["wide"] == 16 and mesh.shape["narrow"] == 2
    local = local_cube if cube else local_general
    return jax.shard_map(local, mesh=mesh, in_specs=in_specs, out_specs=out_specs, check_vma=False)
```

```python
import functools
import math

import jax
import jax.numpy as jnp
from jax import lax
from jax.experimental import pallas as pl
from jax.experimental.pallas import tpu as pltpu
from jax.sharding import PartitionSpec as P

BLK = 12
SHARPNESS = 20.0
EXP2_SCALE = SHARPNESS * math.log2(math.e)
COLS = 256
CHUNK = 4
LINE = 32
PACK = 6
SPREAD = (0, 2, 4, 6, 5, 7, 1, 3)
SMEM = pltpu.SMEM
VMEM = pltpu.VMEM


def vmem_params(mib):
    return pltpu.CompilerParams(vmem_limit_bytes=mib * 2**20)


def plan_kernel(pairs, slots, places_ref, cand_ref, query_block_ref, valid_ref, lengths_ref, sel_ref, table_ref, pairs_ref, *scratch):
    first_ref, second_ref, slot_ref = scratch
    owner, side, blocks = places_ref[0], places_ref[1], places_ref[2]

    def step(k, count):
        block = cand_ref[k]
        found = lax.fori_loop(
            0, k, lambda e, f: jnp.where(cand_ref[e] == block, slot_ref[e], f), jnp.int32(-1)
        )
        new = found < 0
        slot = jnp.minimum(jnp.where(new, count, found), pairs // 2 - 1)
        slot_ref[k] = slot

        @pl.when(new)
        def _():
            sel_ref[slot] = block
            first_ref[slot] = k

        second_ref[slot] = k
        return count + new.astype(jnp.int32)

    lax.fori_loop(0, pairs, step, jnp.int32(0))

    def line(i, carry):
        k = i // 2
        slot = side * slots + k
        pair = jnp.where(i - 2 * k == 0, first_ref[slot], second_ref[slot])
        query = query_block_ref[pair]
        table_ref[i * LINE + 1] = query
        table_ref[i * LINE + 2] = valid_ref[pair]
        for a in range(BLK):
            table_ref[i * LINE + 3 + a] = lengths_ref[sel_ref[slot] * BLK + a]
            table_ref[i * LINE + 3 + BLK + a] = lengths_ref[(owner * blocks + query) * BLK + a]
        return carry

    lax.fori_loop(0, 2 * slots, line, 0)

    def both(slot, carry):
        pairs_ref[2 * slot] = first_ref[slot]
        pairs_ref[2 * slot + 1] = second_ref[slot]
        return carry

    lax.fori_loop(0, pairs // 2, both, 0)


def plan(places, cand_block, query_block, valid, lengths, slots):
    pairs = cand_block.shape[0]
    shapes = (pairs // 2, 2 * slots * LINE, pairs)
    return pl.pallas_call(
        functools.partial(plan_kernel, pairs, slots),
        out_shape=[jax.ShapeDtypeStruct((n,), jnp.int32) for n in shapes],
        in_specs=[pl.BlockSpec(memory_space=SMEM)] * 5,
        out_specs=[pl.BlockSpec(memory_space=SMEM)] * 3,
        scratch_shapes=[SMEM((pairs,), jnp.int32)] * 3,
    )(places, cand_block, query_block, valid, lengths)


def project_kernel(me_ref, states_ref, weight_ref, out_ref):
    out_ref[0, 0] = jnp.dot(
        states_ref[0], weight_ref[...], preferred_element_type=jnp.float32
    ).astype(out_ref.dtype)


def project(me, states, weight, shares, offset, count, dtype):
    blocks, rows, width = states.shape
    out_width = weight.shape[1]
    part = rows // shares
    return pl.pallas_call(
        project_kernel,
        out_shape=jax.ShapeDtypeStruct((count, blocks, part, out_width), dtype),
        grid_spec=pltpu.PrefetchScalarGridSpec(
            num_scalar_prefetch=1,
            grid=(count, blocks),
            in_specs=[
                pl.BlockSpec(
                    (1, part, width), lambda d, b, m: (b, lax.rem(m[0] + offset + d, shares), 0)
                ),
                pl.BlockSpec((width, out_width), lambda d, b, m: (0, 0)),
            ],
            out_specs=pl.BlockSpec((1, 1, part, out_width), lambda d, b, m: (d, b, 0, 0)),
        ),
        cost_estimate=pl.CostEstimate(
            flops=2 * count * blocks * part * width * out_width,
            bytes_accessed=2 * count * blocks * part * width,
            transcendentals=0,
        ),
    )(me, states, weight)


def unit_kernel(others, pieces, keep_ref, *refs):
    out_ref = refs[-1]
    total = keep_ref[0, 0]
    for ref in refs[:others]:
        total = total + ref[0].astype(jnp.float32)
    norm = jnp.sum(total * total, axis=-1, keepdims=True)
    unit = (total * lax.rsqrt(norm + 1e-06)).astype(jnp.bfloat16)
    if pieces is None:
        out_ref[0] = unit
    else:
        size = unit.shape[0] // pieces
        for m in range(pieces):
            out_ref[m, 0] = unit[m * size : (m + 1) * size]


def unit_rows(keep, received, owners):
    _, blocks, part, width = keep.shape
    size = part // owners
    direct = size % 16 == 0
    if direct:
        shape = (owners, blocks, size, width)
        out_spec = pl.BlockSpec((owners, 1, size, width), lambda b: (0, b, 0, 0))
    else:
        shape = (blocks, part, width)
        out_spec = pl.BlockSpec((1, part, width), lambda b: (b, 0, 0))
    out = pl.pallas_call(
        functools.partial(unit_kernel, len(received), owners if direct else None),
        out_shape=jax.ShapeDtypeStruct(shape, jnp.bfloat16),
        grid=(blocks,),
        in_specs=[pl.BlockSpec((1, 1, part, width), lambda b: (0, b, 0, 0))]
        + [pl.BlockSpec((1, part, width), lambda b: (b, 0, 0))] * len(received),
        out_specs=out_spec,
    )(keep, *received)
    if direct:
        return out
    return out.reshape(blocks, owners, size, width).transpose(1, 0, 2, 3)


def route_kernel(dests, slots, owners, asked_ref, pieces_ref, out_ref):
    def step(d, carry):
        side = d // owners
        requester = d - side * owners
        for k in range(slots):
            out_ref[d, k] = pieces_ref[asked_ref[requester, side * slots + k]]
        return carry

    lax.fori_loop(0, dests, step, 0)


def route(asked, pieces, owners, shares):
    slots = asked.shape[1] // shares
    dests = owners * shares
    return pl.pallas_call(
        functools.partial(route_kernel, dests, slots, owners),
        out_shape=jax.ShapeDtypeStruct((dests, slots) + pieces.shape[1:], jnp.bfloat16),
        in_specs=[pl.BlockSpec(memory_space=SMEM), pl.BlockSpec(memory_space=VMEM)],
        out_specs=pl.BlockSpec(memory_space=VMEM),
        compiler_params=vmem_params(48),
    )(asked, pieces)


def query_rows(parts, out_ref):
    _, _, core, side = place()
    size = out_ref.shape[1] // 32
    blocks = out_ref.shape[0]
    for rel, ref in enumerate(parts):
        base = (side ^ (rel // 2)) * (16 * size) + (core ^ (rel % 2)) * (2 * size)
        for z in range(4):
            for x in range(2):
                target = pl.multiple_of(base + z * 4 * size + x * size, 16)
                for b in range(blocks):
                    begin = ((z * 2 + x) * blocks + b) * size
                    out_ref[b, pl.ds(target, size)] = ref[begin : begin + size]


def score_kernel(length, parts, table_ref, *refs):
    if parts:
        cand_ref, out_ref, totals_ref, block_ref, query_ref = refs[parts:]
        query_rows(refs[:parts], query_ref)
    else:
        query_ref, cand_ref, out_ref, totals_ref = refs
    rows = query_ref.shape[1]
    slots = cand_ref.shape[-3]
    out_ref[...] = jnp.zeros_like(out_ref)
    totals_ref[...] = jnp.ones_like(totals_ref)
    upper = lax.broadcasted_iota(jnp.int32, (length // 2, COLS), 0) + length // 2
    lane = lax.broadcasted_iota(jnp.int32, (16, length), 1)

    def pair_step(i, carry):
        k = i // 2
        line = i * LINE
        query = table_ref[line + 1]
        if parts:
            pieces, _, size, _ = cand_ref.shape
            for piece in range(pieces):
                begin = (piece // 4 * 4 + piece % 2 * 2 + piece // 2 % 2) * size
                block_ref[begin : begin + size] = cand_ref[piece, k]
        for start in range(0, rows, COLS):
            sim = lax.dot_general(
                block_ref[...] if parts else cand_ref[k],
                query_ref[query, start : start + COLS],
                (((1,), (1,)), ((), ())),
                preferred_element_type=jnp.float32,
            )
            for b in range(BLK):
                live = table_ref[line + 3 + b]
                low = jnp.exp2(sim[b * length : b * length + length // 2] * EXP2_SCALE)
                high = jnp.exp2(sim[b * length + length // 2 : (b + 1) * length] * EXP2_SCALE)
                both = low + jnp.where(upper < live, high, 0.0)
                totals_ref[b : b + 1, start : start + COLS] = jnp.sum(both, axis=0, keepdims=True)
        keep = table_ref[line + 2].astype(jnp.float32) / (SHARPNESS * length)
        score = out_ref[i // PACK]
        for a in range(BLK):
            live = table_ref[line + 3 + BLK + a]
            logs = jnp.log(totals_ref[:, a * length : (a + 1) * length])
            summed = jnp.sum(jnp.where(lane < live, logs, 0.0), axis=1, keepdims=True)
            score = jnp.where(lane == lax.rem(i, PACK) * BLK + a, summed * keep, score)
        out_ref[i // PACK] = score
        return carry

    lax.fori_loop(0, 2 * slots, pair_step, 0)


def score(table, query, cand, blocks, length):
    slots, width = cand.shape[-3], cand.shape[-1]
    rows = BLK * length
    parts = len(query) if isinstance(query, list) else 0
    count = 2 * slots * rows * rows
    scratch = [VMEM((16, rows), jnp.float32)]
    if parts:
        scratch += [VMEM((rows, width), jnp.bfloat16), VMEM((blocks, rows, width), jnp.bfloat16)]
    return pl.pallas_call(
        functools.partial(score_kernel, length, parts),
        out_shape=jax.ShapeDtypeStruct((-(-2 * slots // PACK), 16, length), jnp.float32),
        in_specs=[pl.BlockSpec(memory_space=SMEM)]
        + [pl.BlockSpec(memory_space=VMEM)] * (max(parts, 1) + 1),
        out_specs=pl.BlockSpec(memory_space=VMEM),
        scratch_shapes=scratch,
        compiler_params=vmem_params(28),
        cost_estimate=pl.CostEstimate(
            flops=2 * count * width, bytes_accessed=4 * rows * width, transcendentals=count
        ),
    )(table, *(query if parts else [query]), cand)


def place_kernel(shares, count, where_ref, pairs_ref, *refs):
    parts, out_ref = refs[:-1], refs[-1]
    for d, ref in enumerate(parts):
        side = lax.rem(where_ref[1] - d + shares, shares)
        for i in range(count):
            tile = ref[i // PACK]
            if i % PACK:
                tile = pltpu.roll(tile, tile.shape[1] - i % PACK * BLK, 1)
            out_ref[pairs_ref[side * count + i]] = tile[:BLK, :BLK]


def place_scores(where, pair_of, parts, pairs):
    shares = len(parts)
    return pl.pallas_call(
        functools.partial(place_kernel, shares, pairs // shares),
        out_shape=jax.ShapeDtypeStruct((pairs, BLK, BLK), jnp.float32),
        in_specs=[pl.BlockSpec(memory_space=SMEM)] * 2 + [pl.BlockSpec(memory_space=VMEM)] * shares,
        out_specs=pl.BlockSpec(memory_space=VMEM),
        compiler_params=vmem_params(4),
    )(where, pair_of, *parts)


def local_general(states, proj_weight, lengths, query_block, cand_block, pair_valid):
    shares = lax.axis_size("narrow")
    owners = lax.axis_size("wide")
    side = lax.axis_index("narrow").astype(jnp.int32)
    owner = lax.axis_index("wide").astype(jnp.int32)
    paras, length, width_part = states.shape
    width = proj_weight.shape[1]
    blocks = paras // BLK
    rows = BLK * length
    flat = states.reshape(blocks, rows, width_part)
    me = side.reshape(1)

    def shift(d):
        return [(i, (i + d) % shares) for i in range(shares)]

    slots = cand_block.shape[0] // 2 // shares
    places = jnp.stack([owner, side, jnp.int32(blocks)])
    sel, table, pair_of = plan(places, cand_block, query_block, pair_valid, lengths, slots)
    sent = project(me, flat, proj_weight, shares, 1, shares - 1, jnp.bfloat16)
    received = [lax.ppermute(sent[d - 1], "narrow", shift(d)) for d in range(1, shares)]
    asked = lax.all_to_all(
        jnp.broadcast_to(sel[None], (owners,) + sel.shape), "wide", 0, 0, tiled=True
    )
    kept = project(me, flat, proj_weight, shares, 0, 1, jnp.float32)
    mine = unit_rows(kept, received, owners)
    spread = lax.all_to_all(mine, "wide", 0, 0, tiled=True)
    size = mine.shape[2]
    by_side = [mine] + [lax.ppermute(mine, "narrow", shift(d)) for d in range(1, shares)]
    order = jnp.stack(by_side)
    query = jnp.stack(
        [lax.dynamic_index_in_dim(order, lax.rem(side - s + shares, shares), 0, False) for s in range(shares)]
    )
    query = query.transpose(2, 0, 1, 3, 4).reshape(blocks, rows, width)
    outgoing = route(asked, spread.reshape(owners * blocks, size, width), owners, shares)
    incoming = lax.all_to_all(outgoing, ("narrow", "wide"), 0, 0, tiled=True)
    cand = incoming.transpose(1, 0, 2, 3).reshape(-1, rows, width)
    part = score(table, query, cand, blocks, length)
    parts = [part] + [lax.ppermute(part, "narrow", shift(d)) for d in range(1, shares)]
    return place_scores(places, pair_of, parts, cand_block.shape[0])


def place():
    owner = lax.axis_index("wide")
    return owner // 4, owner // 2 % 2, owner % 2, lax.axis_index("narrow")


def split_kernel(over, states_ref, weight_ref, *refs):
    flips, blocks = len(over), states_ref.shape[0]
    outs, rows_ref, sems = refs[:flips], refs[flips], refs[flips + 1]
    _, _, core, side = place()
    _, _, _, zs, double, _ = rows_ref.shape
    size = double // 2

    def load(i, b):
        dn, dc = over[i]
        return pltpu.make_async_copy(
            states_ref.at[b, side ^ dn, :, core ^ dc], rows_ref.at[i, b, 0], sems.at[i, b]
        )

    for i in range(flips):
        for b in range(blocks):
            load(i, b).start()
    for i in range(flips):
        for b in range(blocks):
            load(i, b).wait()
            for z in range(zs):
                both = jnp.dot(
                    rows_ref[i, b, 0, z], weight_ref[...], preferred_element_type=jnp.float32
                ).astype(jnp.bfloat16)
                for x in range(2):
                    target = ((z * 2 + x) * blocks + b) * size
                    outs[i][target : target + size] = both[x * size : (x + 1) * size]


def split(over, states, weight):
    blocks, _, zs, _, double, width = states.shape
    out_width = weight.shape[1]
    out_rows = blocks * zs * double
    return pl.pallas_call(
        functools.partial(split_kernel, over),
        out_shape=(jax.ShapeDtypeStruct((out_rows, out_width), jnp.bfloat16),) * len(over),
        in_specs=[pl.BlockSpec(memory_space=pltpu.HBM), pl.BlockSpec(memory_space=VMEM)],
        out_specs=[pl.BlockSpec(memory_space=VMEM)] * len(over),
        scratch_shapes=[
            VMEM((len(over), blocks, 1, zs, double, width), jnp.bfloat16),
            pltpu.SemaphoreType.DMA((len(over), blocks)),
        ],
        compiler_params=vmem_params(50),
        cost_estimate=pl.CostEstimate(
            flops=2 * len(over) * out_rows * width * out_width,
            bytes_accessed=2 * len(over) * out_rows * width,
            transcendentals=0,
        ),
    )(states, weight)


def gather_unit_kernel(size, sel_ref, sel_near_ref, cy_ref, y_ref, own_ref, c_ref, *outs):
    z, x, _, _ = place()
    sends, query = outs[:8], outs[8:]
    span = CHUNK * size
    shape = (16, own_ref.shape[1])
    row, lane = (lax.broadcasted_iota(jnp.int32, shape, axis) for axis in range(2))
    asked = jnp.zeros(shape, jnp.int32)
    for flip, ids_ref in enumerate((sel_ref, sel_near_ref)):
        for k in range(ids_ref.shape[0]):
            asked = jnp.where((row == flip) & (lane == k), ids_ref[k], asked)
    asked = asked.astype(jnp.float32).astype(jnp.bfloat16)
    for rel, send_ref in zip(SPREAD, sends):
        source = pl.multiple_of(((z ^ (rel // 2)) * 2 + (x ^ (rel % 2))) * span, 16)
        for flip, (one_ref, two_ref) in enumerate(((own_ref, y_ref), (c_ref, cy_ref))):
            total = one_ref[pl.ds(source, span)].astype(jnp.float32)
            total = total + two_ref[pl.ds(source, span)].astype(jnp.float32)
            norm = jnp.sum(total * total, axis=-1, keepdims=True)
            unit = (total * lax.rsqrt(norm + 1e-06)).astype(jnp.bfloat16)
            send_ref[flip * span : (flip + 1) * span] = unit
            query[flip][pl.ds(source, span)] = unit
        send_ref[2 * span :] = asked


def gather_unit(sel, sel_near, cy, y, own, c, size):
    rows, width = own.shape
    send = jax.ShapeDtypeStruct((2 * CHUNK * size + 16, width), jnp.bfloat16)
    query = jax.ShapeDtypeStruct((rows, width), jnp.bfloat16)
    return pl.pallas_call(
        functools.partial(gather_unit_kernel, size),
        out_shape=(send,) * 8 + (query,) * 2,
        in_specs=[pl.BlockSpec(memory_space=SMEM)] * 2 + [pl.BlockSpec(memory_space=VMEM)] * 4,
        out_specs=[pl.BlockSpec(memory_space=VMEM)] * 10,
        compiler_params=vmem_params(12),
    )(sel, sel_near, cy, y, own, c)


def cube_route_kernel(size, slots, parts, *refs):
    spread, out_ref, pieces_ref, rows_ref, asked_ref, sem = refs[:parts], *refs[parts:]
    z, x, core, _ = place()
    blocks = pieces_ref.shape[0] // 16
    span = CHUNK * size
    for rel, ref in zip(SPREAD, spread):
        for flip in range(2):
            owner = (z ^ (rel // 2)) * 4 + (x ^ (rel % 2)) * 2 + (core ^ flip)
            for b in range(CHUNK):
                begin = flip * span + b * size
                pieces_ref[owner * blocks + b] = ref[begin : begin + size]
            row = ref[2 * span :].astype(jnp.float32)[flip : flip + 1]
            rows_ref[pl.ds(owner, 1)] = row.astype(jnp.int32)
    copy = pltpu.make_async_copy(rows_ref, asked_ref, sem)
    copy.start()
    copy.wait()

    def step(d, carry):
        side = d // 16
        for k in range(slots):
            out_ref[d, k] = pieces_ref[asked_ref[d - side * 16, side * slots + k]]
        return carry

    lax.fori_loop(0, 32, step, 0, unroll=4)


def cube_route(spread, size, slots, blocks):
    width = spread[0].shape[1]
    return pl.pallas_call(
        functools.partial(cube_route_kernel, size, slots, len(spread)),
        out_shape=jax.ShapeDtypeStruct((32, slots, size, width), jnp.bfloat16),
        in_specs=[pl.BlockSpec(memory_space=VMEM)] * len(spread),
        out_specs=pl.BlockSpec(memory_space=VMEM),
        scratch_shapes=[
            VMEM((16 * blocks, size, width), jnp.bfloat16),
            VMEM((16, width), jnp.int32),
            SMEM((16, width), jnp.int32),
            pltpu.SemaphoreType.DMA,
        ],
        compiler_params=vmem_params(16),
    )(*spread)


def local_cube(states, proj_weight, lengths, query_block, cand_block, pair_valid):
    side = lax.axis_index("narrow").astype(jnp.int32)
    owner = lax.axis_index("wide").astype(jnp.int32)
    paras, length, width_part = states.shape
    width = proj_weight.shape[1]
    blocks = paras // BLK
    rows = BLK * length
    size = rows // 32
    slots = cand_block.shape[0] // 4
    flat = states.reshape(blocks, rows, width_part)

    def near(array, rel):
        flip = rel % 2 * 2 + rel // 2
        return lax.ppermute(array, ("wide", "narrow"), [(i, i ^ flip) for i in range(32)])

    def along(array, rel):
        flip = rel * 2
        return lax.ppermute(array, "wide", [(i, i ^ flip) for i in range(16)])

    places = jnp.stack([owner, side, jnp.int32(blocks)])
    sel, table, pair_of = plan(places, cand_block, query_block, pair_valid, lengths, slots)
    sel_near = near(sel, 1)
    view = flat.reshape(blocks, 2, 4, 2, 2 * size, width_part)
    (far,) = split([(1, 0)], view, proj_weight)
    weight, far = lax.optimization_barrier((proj_weight, far))
    (far_aside,) = split([(1, 1)], view, weight)
    weight, far_aside = lax.optimization_barrier((weight, far_aside))
    y, cy = near(far, 2), near(far_aside, 3)
    own, aside = split([(0, 0), (0, 1)], view, weight)
    c = near(aside, 1)
    *sends, own, other = gather_unit(sel, sel_near, cy, y, own, c, size)
    sends = dict(zip(SPREAD, sends))
    other = near(other, 1)
    sends[3], other = lax.optimization_barrier((sends[3], other))
    moved = {rel: along(sends[rel], rel) if rel else sends[rel] for rel in SPREAD}
    own_y = near(own, 2)
    outgoing = cube_route([moved[rel] for rel in SPREAD], size, slots, blocks)
    outgoing, own_y, other = lax.optimization_barrier((outgoing, own_y, other))
    incoming = lax.all_to_all(outgoing, ("narrow", "wide"), 0, 0, tiled=True)
    query = [own, other, own_y, near(other, 2)]
    part = score(table, query, incoming, blocks, length)
    parts = [part, lax.ppermute(part, "narrow", [(0, 1), (1, 0)])]
    return place_scores(places, pair_of, parts, cand_block.shape[0])


def solution(mesh):
    in_specs = (P("wide", None, "narrow"), P("narrow", None), P(), P("wide"), P("wide"), P("wide"))
    out_specs = P("wide", None, None)
    cube = mesh.shape["wide"] == 16 and mesh.shape["narrow"] == 2
    local = local_cube if cube else local_general
    return jax.shard_map(local, mesh=mesh, in_specs=in_specs, out_specs=out_specs, check_vma=False)
```

```python
import functools
import math

import jax
import jax.numpy as jnp
from jax import lax
from jax.experimental import pallas as pl
from jax.experimental.pallas import tpu as pltpu
from jax.sharding import PartitionSpec as P

BLK = 12
SHARPNESS = 20.0
EXP2_SCALE = SHARPNESS * math.log2(math.e)
COLS = 512
CHUNK = 4
LINE = 32
PACK = 6
FAR = (4, 6, 5, 7)
SMEM = pltpu.SMEM
VMEM = pltpu.VMEM


def vmem_params(mib):
    return pltpu.CompilerParams(vmem_limit_bytes=mib * 2**20)


def plan_kernel(pairs, slots, places_ref, cand_ref, query_block_ref, valid_ref, lengths_ref, sel_ref, table_ref, pairs_ref, *scratch):
    first_ref, second_ref, slot_ref = scratch
    owner, side, blocks = places_ref[0], places_ref[1], places_ref[2]

    def step(k, count):
        block = cand_ref[k]
        found = lax.fori_loop(
            0, k, lambda e, f: jnp.where(cand_ref[e] == block, slot_ref[e], f), jnp.int32(-1)
        )
        new = found < 0
        slot = jnp.minimum(jnp.where(new, count, found), pairs // 2 - 1)
        slot_ref[k] = slot

        @pl.when(new)
        def _():
            sel_ref[slot] = block
            first_ref[slot] = k

        second_ref[slot] = k
        return count + new.astype(jnp.int32)

    lax.fori_loop(0, pairs, step, jnp.int32(0))

    def line(i, carry):
        k = i // 2
        slot = side * slots + k
        pair = jnp.where(i - 2 * k == 0, first_ref[slot], second_ref[slot])
        query = query_block_ref[pair]
        table_ref[i * LINE + 1] = query
        table_ref[i * LINE + 2] = valid_ref[pair]
        for a in range(BLK):
            table_ref[i * LINE + 3 + a] = lengths_ref[sel_ref[slot] * BLK + a]
            table_ref[i * LINE + 3 + BLK + a] = lengths_ref[(owner * blocks + query) * BLK + a]
        return carry

    lax.fori_loop(0, 2 * slots, line, 0)

    def both(slot, carry):
        pairs_ref[2 * slot] = first_ref[slot]
        pairs_ref[2 * slot + 1] = second_ref[slot]
        return carry

    lax.fori_loop(0, pairs // 2, both, 0)


def plan(places, cand_block, query_block, valid, lengths, slots):
    pairs = cand_block.shape[0]
    shapes = (pairs // 2, 2 * slots * LINE, pairs)
    return pl.pallas_call(
        functools.partial(plan_kernel, pairs, slots),
        out_shape=[jax.ShapeDtypeStruct((n,), jnp.int32) for n in shapes],
        in_specs=[pl.BlockSpec(memory_space=SMEM)] * 5,
        out_specs=[pl.BlockSpec(memory_space=SMEM)] * 3,
        scratch_shapes=[SMEM((pairs,), jnp.int32)] * 3,
    )(places, cand_block, query_block, valid, lengths)


def project_kernel(me_ref, states_ref, weight_ref, out_ref):
    out_ref[0, 0] = jnp.dot(
        states_ref[0], weight_ref[...], preferred_element_type=jnp.float32
    ).astype(out_ref.dtype)


def project(me, states, weight, shares, offset, count, dtype):
    blocks, rows, width = states.shape
    out_width = weight.shape[1]
    part = rows // shares
    return pl.pallas_call(
        project_kernel,
        out_shape=jax.ShapeDtypeStruct((count, blocks, part, out_width), dtype),
        grid_spec=pltpu.PrefetchScalarGridSpec(
            num_scalar_prefetch=1,
            grid=(count, blocks),
            in_specs=[
                pl.BlockSpec(
                    (1, part, width), lambda d, b, m: (b, lax.rem(m[0] + offset + d, shares), 0)
                ),
                pl.BlockSpec((width, out_width), lambda d, b, m: (0, 0)),
            ],
            out_specs=pl.BlockSpec((1, 1, part, out_width), lambda d, b, m: (d, b, 0, 0)),
        ),
        cost_estimate=pl.CostEstimate(
            flops=2 * count * blocks * part * width * out_width,
            bytes_accessed=2 * count * blocks * part * width,
            transcendentals=0,
        ),
    )(me, states, weight)


def unit_kernel(others, pieces, keep_ref, *refs):
    out_ref = refs[-1]
    total = keep_ref[0, 0]
    for ref in refs[:others]:
        total = total + ref[0].astype(jnp.float32)
    norm = jnp.sum(total * total, axis=-1, keepdims=True)
    unit = (total * lax.rsqrt(norm + 1e-06)).astype(jnp.bfloat16)
    if pieces is None:
        out_ref[0] = unit
    else:
        size = unit.shape[0] // pieces
        for m in range(pieces):
            out_ref[m, 0] = unit[m * size : (m + 1) * size]


def unit_rows(keep, received, owners):
    _, blocks, part, width = keep.shape
    size = part // owners
    direct = size % 16 == 0
    if direct:
        shape = (owners, blocks, size, width)
        out_spec = pl.BlockSpec((owners, 1, size, width), lambda b: (0, b, 0, 0))
    else:
        shape = (blocks, part, width)
        out_spec = pl.BlockSpec((1, part, width), lambda b: (b, 0, 0))
    out = pl.pallas_call(
        functools.partial(unit_kernel, len(received), owners if direct else None),
        out_shape=jax.ShapeDtypeStruct(shape, jnp.bfloat16),
        grid=(blocks,),
        in_specs=[pl.BlockSpec((1, 1, part, width), lambda b: (0, b, 0, 0))]
        + [pl.BlockSpec((1, part, width), lambda b: (b, 0, 0))] * len(received),
        out_specs=out_spec,
    )(keep, *received)
    if direct:
        return out
    return out.reshape(blocks, owners, size, width).transpose(1, 0, 2, 3)


def route_kernel(dests, slots, owners, asked_ref, pieces_ref, out_ref):
    def step(d, carry):
        side = d // owners
        requester = d - side * owners
        for k in range(slots):
            out_ref[d, k] = pieces_ref[asked_ref[requester, side * slots + k]]
        return carry

    lax.fori_loop(0, dests, step, 0)


def route(asked, pieces, owners, shares):
    slots = asked.shape[1] // shares
    dests = owners * shares
    return pl.pallas_call(
        functools.partial(route_kernel, dests, slots, owners),
        out_shape=jax.ShapeDtypeStruct((dests, slots) + pieces.shape[1:], jnp.bfloat16),
        in_specs=[pl.BlockSpec(memory_space=SMEM), pl.BlockSpec(memory_space=VMEM)],
        out_specs=pl.BlockSpec(memory_space=VMEM),
        compiler_params=vmem_params(48),
    )(asked, pieces)


def query_rows(parts, out_ref):
    _, _, core, side = place()
    size = out_ref.shape[1] // 32
    blocks = out_ref.shape[0]
    for rel, ref in enumerate(parts):
        base = (side ^ (rel // 2)) * (16 * size) + (core ^ (rel % 2)) * (2 * size)
        for z in range(4):
            for x in range(2):
                target = pl.multiple_of(base + z * 4 * size + x * size, 16)
                for b in range(blocks):
                    begin = ((z * 2 + x) * blocks + b) * size
                    out_ref[b, pl.ds(target, size)] = ref[begin : begin + size]


def score_kernel(length, parts, table_ref, *refs):
    if parts:
        cand_ref, out_ref, totals_ref, block_ref, query_ref = refs[parts:]
        query_rows(refs[:parts], query_ref)
    else:
        query_ref, cand_ref, out_ref, totals_ref = refs
    rows = query_ref.shape[1]
    slots = cand_ref.shape[-3]
    totals_ref[...] = jnp.ones_like(totals_ref)
    upper = lax.broadcasted_iota(jnp.int32, (length // 2, COLS), 0) + length // 2
    lane = lax.broadcasted_iota(jnp.int32, (16, length), 1)

    def slot_step(k, carry):
        if parts:
            pieces, _, size, _ = cand_ref.shape
            for piece in range(pieces):
                begin = (piece // 4 * 4 + piece % 2 * 2 + piece // 2 % 2) * size
                block_ref[begin : begin + size] = cand_ref[piece, k]
        for i in range(2):
            line = (2 * k + i) * LINE
            query = table_ref[line + 1]
            for start in range(0, rows, COLS):
                sim = lax.dot_general(
                    block_ref[...] if parts else cand_ref[k],
                    query_ref[query, start : start + COLS],
                    (((1,), (1,)), ((), ())),
                    preferred_element_type=jnp.float32,
                )
                for b in range(BLK):
                    live = table_ref[line + 3 + b]
                    low = jnp.exp2(sim[b * length : b * length + length // 2] * EXP2_SCALE)
                    high = jnp.exp2(sim[b * length + length // 2 : (b + 1) * length] * EXP2_SCALE)
                    both = low + jnp.where(upper < live, high, 0.0)
                    totals_ref[2 * k + i, b : b + 1, start : start + COLS] = jnp.sum(
                        both, axis=0, keepdims=True
                    )
        return carry

    lax.fori_loop(0, slots, slot_step, 0)
    for tile in range(out_ref.shape[0]):
        score = jnp.zeros((16, length), jnp.float32)
        for i in range(tile * PACK, min((tile + 1) * PACK, 2 * slots)):
            line = i * LINE
            keep = table_ref[line + 2].astype(jnp.float32) / (SHARPNESS * length)
            for a in range(BLK):
                live = table_ref[line + 3 + BLK + a]
                logs = jnp.log(totals_ref[i, :, a * length : (a + 1) * length])
                summed = jnp.sum(jnp.where(lane < live, logs, 0.0), axis=1, keepdims=True)
                score = jnp.where(lane == i % PACK * BLK + a, summed * keep, score)
        out_ref[tile] = score


def score(table, query, cand, blocks, length):
    slots, width = cand.shape[-3], cand.shape[-1]
    rows = BLK * length
    parts = len(query) if isinstance(query, list) else 0
    count = 2 * slots * rows * rows
    scratch = [VMEM((2 * slots, 16, rows), jnp.float32)]
    if parts:
        scratch += [VMEM((rows, width), jnp.bfloat16), VMEM((blocks, rows, width), jnp.bfloat16)]
    return pl.pallas_call(
        functools.partial(score_kernel, length, parts),
        out_shape=jax.ShapeDtypeStruct((-(-2 * slots // PACK), 16, length), jnp.float32),
        in_specs=[pl.BlockSpec(memory_space=SMEM)]
        + [pl.BlockSpec(memory_space=VMEM)] * (max(parts, 1) + 1),
        out_specs=pl.BlockSpec(memory_space=VMEM),
        scratch_shapes=scratch,
        compiler_params=vmem_params(28),
        cost_estimate=pl.CostEstimate(
            flops=2 * count * width, bytes_accessed=4 * rows * width, transcendentals=count
        ),
    )(table, *(query if parts else [query]), cand)


def place_kernel(shares, count, where_ref, pairs_ref, *refs):
    parts, out_ref = refs[:-1], refs[-1]
    for d, ref in enumerate(parts):
        side = lax.rem(where_ref[1] - d + shares, shares)
        for i in range(count):
            tile = ref[i // PACK]
            if i % PACK:
                tile = pltpu.roll(tile, tile.shape[1] - i % PACK * BLK, 1)
            out_ref[pairs_ref[side * count + i]] = tile[:BLK, :BLK]


def place_scores(where, pair_of, parts, pairs):
    shares = len(parts)
    return pl.pallas_call(
        functools.partial(place_kernel, shares, pairs // shares),
        out_shape=jax.ShapeDtypeStruct((pairs, BLK, BLK), jnp.float32),
        in_specs=[pl.BlockSpec(memory_space=SMEM)] * 2 + [pl.BlockSpec(memory_space=VMEM)] * shares,
        out_specs=pl.BlockSpec(memory_space=VMEM),
        compiler_params=vmem_params(4),
    )(where, pair_of, *parts)


def local_general(states, proj_weight, lengths, query_block, cand_block, pair_valid):
    shares = lax.axis_size("narrow")
    owners = lax.axis_size("wide")
    side = lax.axis_index("narrow").astype(jnp.int32)
    owner = lax.axis_index("wide").astype(jnp.int32)
    paras, length, width_part = states.shape
    width = proj_weight.shape[1]
    blocks = paras // BLK
    rows = BLK * length
    flat = states.reshape(blocks, rows, width_part)
    me = side.reshape(1)

    def shift(d):
        return [(i, (i + d) % shares) for i in range(shares)]

    slots = cand_block.shape[0] // 2 // shares
    places = jnp.stack([owner, side, jnp.int32(blocks)])
    sel, table, pair_of = plan(places, cand_block, query_block, pair_valid, lengths, slots)
    sent = project(me, flat, proj_weight, shares, 1, shares - 1, jnp.bfloat16)
    received = [lax.ppermute(sent[d - 1], "narrow", shift(d)) for d in range(1, shares)]
    asked = lax.all_to_all(
        jnp.broadcast_to(sel[None], (owners,) + sel.shape), "wide", 0, 0, tiled=True
    )
    kept = project(me, flat, proj_weight, shares, 0, 1, jnp.float32)
    mine = unit_rows(kept, received, owners)
    spread = lax.all_to_all(mine, "wide", 0, 0, tiled=True)
    size = mine.shape[2]
    by_side = [mine] + [lax.ppermute(mine, "narrow", shift(d)) for d in range(1, shares)]
    order = jnp.stack(by_side)
    query = jnp.stack(
        [lax.dynamic_index_in_dim(order, lax.rem(side - s + shares, shares), 0, False) for s in range(shares)]
    )
    query = query.transpose(2, 0, 1, 3, 4).reshape(blocks, rows, width)
    outgoing = route(asked, spread.reshape(owners * blocks, size, width), owners, shares)
    incoming = lax.all_to_all(outgoing, ("narrow", "wide"), 0, 0, tiled=True)
    cand = incoming.transpose(1, 0, 2, 3).reshape(-1, rows, width)
    part = score(table, query, cand, blocks, length)
    parts = [part] + [lax.ppermute(part, "narrow", shift(d)) for d in range(1, shares)]
    return place_scores(places, pair_of, parts, cand_block.shape[0])


def place():
    owner = lax.axis_index("wide")
    return owner // 4, owner // 2 % 2, owner % 2, lax.axis_index("narrow")


def split_kernel(first, over, states_ref, weight_ref, *refs):
    *outs, rows_ref, sems = refs
    _, _, core, side = place()
    blocks, part, _ = rows_ref.shape
    size = part // 16
    start = pl.multiple_of((side ^ over) * part, part)

    def load(b):
        return pltpu.make_async_copy(
            states_ref.at[first + b, pl.ds(start, part)], rows_ref.at[b], sems.at[b]
        )

    for b in range(blocks):
        load(b).start()
    for b in range(blocks):
        load(b).wait()
        for z in range(4):
            for flip in range(2):
                source = pl.multiple_of((core ^ flip) * (2 * size) + z * 4 * size, 16)
                both = jnp.dot(
                    rows_ref[b, pl.ds(source, 2 * size)],
                    weight_ref[...],
                    preferred_element_type=jnp.float32,
                ).astype(jnp.bfloat16)
                for x in range(2):
                    target = ((z * 2 + x) * blocks + b) * size
                    outs[flip][target : target + size] = both[x * size : (x + 1) * size]


def split(over, states, weight, first):
    _, rows, width = states.shape
    out_width = weight.shape[1]
    part = rows // 2
    out_rows = 8 * CHUNK * (part // 16)
    return pl.pallas_call(
        functools.partial(split_kernel, first, over),
        out_shape=(jax.ShapeDtypeStruct((out_rows, out_width), jnp.bfloat16),) * 2,
        in_specs=[pl.BlockSpec(memory_space=pltpu.HBM), pl.BlockSpec(memory_space=VMEM)],
        out_specs=[pl.BlockSpec(memory_space=VMEM)] * 2,
        scratch_shapes=[
            VMEM((CHUNK, part, width), jnp.bfloat16),
            pltpu.SemaphoreType.DMA((CHUNK,)),
        ],
        compiler_params=vmem_params(50),
        cost_estimate=pl.CostEstimate(
            flops=2 * CHUNK * part * width * out_width,
            bytes_accessed=2 * CHUNK * part * width,
            transcendentals=0,
        ),
    )(states, weight)


def gather_unit_kernel(size, sel_ref, sel_near_ref, y_ref, cy_ref, own_ref, c_ref, *outs):
    z, x, _, _ = place()
    sends, query = outs[:5], outs[5:]
    span = CHUNK * size
    shape = (16, own_ref.shape[1])
    row, lane = (lax.broadcasted_iota(jnp.int32, shape, axis) for axis in range(2))
    asked = jnp.zeros(shape, jnp.int32)
    for flip, ids_ref in enumerate((sel_ref, sel_near_ref)):
        for k in range(ids_ref.shape[0]):
            asked = jnp.where((row == flip) & (lane == k), ids_ref[k], asked)
    asked = asked.astype(jnp.float32).astype(jnp.bfloat16)
    near_ref, far_refs = sends[0], sends[1:]
    rows = 2 * span + 16
    here = z % 2 * 2 + x
    for rel in (*FAR, 0, 1, 2, 3):
        if rel < 4:
            send_ref, begin = near_ref, (here ^ rel) * rows
        else:
            send_ref, begin = far_refs[FAR.index(rel)], 0
        source = pl.multiple_of(((z ^ (rel // 2)) * 2 + (x ^ (rel % 2))) * span, 16)
        for flip, (one_ref, two_ref) in enumerate(((own_ref, y_ref), (c_ref, cy_ref))):
            total = one_ref[pl.ds(source, span)].astype(jnp.float32)
            total = total + two_ref[pl.ds(source, span)].astype(jnp.float32)
            norm = jnp.sum(total * total, axis=-1, keepdims=True)
            unit = (total * lax.rsqrt(norm + 1e-06)).astype(jnp.bfloat16)
            send_ref[pl.ds(pl.multiple_of(begin + flip * span, 16), span)] = unit
            query[flip][pl.ds(source, span)] = unit
        send_ref[pl.ds(pl.multiple_of(begin + 2 * span, 16), 16)] = asked


def gather_unit(sel, sel_near, y, cy, own, c, size):
    rows, width = own.shape
    piece = 2 * CHUNK * size + 16
    near, far = (jax.ShapeDtypeStruct((n * piece, width), jnp.bfloat16) for n in (4, 1))
    query = jax.ShapeDtypeStruct((rows, width), jnp.bfloat16)
    return pl.pallas_call(
        functools.partial(gather_unit_kernel, size),
        out_shape=(near,) + (far,) * 4 + (query,) * 2,
        in_specs=[pl.BlockSpec(memory_space=SMEM)] * 2 + [pl.BlockSpec(memory_space=VMEM)] * 4,
        out_specs=[pl.BlockSpec(memory_space=VMEM)] * 7,
        compiler_params=vmem_params(12),
    )(sel, sel_near, y, cy, own, c)


def cube_route_kernel(size, slots, near_ref, *refs):
    far, out_ref, pieces_ref, rows_ref, asked_ref, sem = refs[:4], *refs[4:]
    z, x, core, _ = place()
    blocks = pieces_ref.shape[0] // 16
    span = CHUNK * size
    rows = 2 * span + 16
    parts = [(near_ref, i * rows, z // 2 * 4 + i) for i in range(4)]
    parts += [(ref, 0, (z ^ (rel // 2)) * 2 + (x ^ (rel % 2))) for ref, rel in zip(far, FAR)]
    for ref, begin, chip in parts:
        ids = ref[begin + 2 * span : begin + rows].astype(jnp.float32)
        for flip in range(2):
            rows_ref[pl.ds(chip * 2 + (core ^ flip), 1)] = ids[flip : flip + 1].astype(jnp.int32)
    copy = pltpu.make_async_copy(rows_ref, asked_ref, sem)
    copy.start()
    for ref, begin, chip in parts:
        for flip in range(2):
            owner = chip * 2 + (core ^ flip)
            for b in range(blocks):
                row = begin + flip * span + b * size
                pieces_ref[owner * blocks + b] = ref[row : row + size]
    copy.wait()

    def step(d, carry):
        side = d // 16
        for k in range(slots):
            out_ref[d, k] = pieces_ref[asked_ref[d - side * 16, side * slots + k]]
        return carry

    lax.fori_loop(0, 32, step, 0, unroll=4)


def cube_route(spread, size, slots, blocks):
    width = spread[0].shape[1]
    return pl.pallas_call(
        functools.partial(cube_route_kernel, size, slots),
        out_shape=jax.ShapeDtypeStruct((32, slots, size, width), jnp.bfloat16),
        in_specs=[pl.BlockSpec(memory_space=VMEM)] * len(spread),
        out_specs=pl.BlockSpec(memory_space=VMEM),
        scratch_shapes=[
            VMEM((16 * blocks, size, width), jnp.bfloat16),
            VMEM((16, width), jnp.int32),
            SMEM((16, width), jnp.int32),
            pltpu.SemaphoreType.DMA,
        ],
        compiler_params=vmem_params(16),
    )(*spread)


def local_cube(states, proj_weight, lengths, query_block, cand_block, pair_valid):
    side = lax.axis_index("narrow").astype(jnp.int32)
    owner = lax.axis_index("wide").astype(jnp.int32)
    paras, length, width_part = states.shape
    width = proj_weight.shape[1]
    blocks = paras // BLK
    rows = BLK * length
    size = rows // 32
    slots = cand_block.shape[0] // 4
    flat = states.reshape(blocks, rows, width_part)

    def near(array, rel):
        flip = rel % 2 * 2 + rel // 2
        return lax.ppermute(array, ("wide", "narrow"), [(i, i ^ flip) for i in range(32)])

    def along(array, rel):
        flip = rel * 2
        return lax.ppermute(array, "wide", [(i, i ^ flip) for i in range(16)])

    places = jnp.stack([owner, side, jnp.int32(blocks)])
    sel, table, pair_of = plan(places, cand_block, query_block, pair_valid, lengths, slots)
    sel_near = near(sel, 1)
    far = split(1, flat, proj_weight, 0)
    weight, *far = lax.optimization_barrier((proj_weight, *far))
    y, cy = near(far[0], 2), near(far[1], 3)
    own, aside = split(0, flat, weight, 0)
    c = near(aside, 1)
    close, *sends, own, other = gather_unit(sel, sel_near, y, cy, own, c, size)
    own_y = near(own, 2)
    moved = [along(send, rel) for rel, send in zip(FAR, sends)]
    groups = [[z * 4 + x * 2 + core for z in (high, high + 1) for x in (0, 1)] for high in (0, 2) for core in (0, 1)]
    close = lax.all_to_all(close, "wide", 0, 0, tiled=True, axis_index_groups=groups)
    outgoing = cube_route([close, *moved], size, slots, blocks)
    outgoing, other, own_y = lax.optimization_barrier((outgoing, other, own_y))
    incoming = lax.all_to_all(outgoing, ("narrow", "wide"), 0, 0, tiled=True)
    other = near(other, 1)
    query = [own, other, own_y, near(other, 2)]
    part = score(table, query, incoming, blocks, length)
    parts = [part, lax.ppermute(part, "narrow", [(0, 1), (1, 0)])]
    return place_scores(places, pair_of, parts, cand_block.shape[0])


def solution(mesh):
    in_specs = (P("wide", None, "narrow"), P("narrow", None), P(), P("wide"), P("wide"), P("wide"))
    out_specs = P("wide", None, None)
    cube = mesh.shape["wide"] == 16 and mesh.shape["narrow"] == 2
    local = local_cube if cube else local_general
    return jax.shard_map(local, mesh=mesh, in_specs=in_specs, out_specs=out_specs, check_vma=False)
```

```python
import functools
import math

import jax
import jax.numpy as jnp
from jax import lax
from jax.experimental import pallas as pl
from jax.experimental.pallas import tpu as pltpu
from jax.sharding import PartitionSpec as P

BLK = 12
SHARPNESS = 20.0
EXP2_SCALE = SHARPNESS * math.log2(math.e)
COLS = 512
CHUNK = 4
LINE = 32
PACK = 6
SPREAD = (0, 1, 4, 6, 5, 7, 2, 3)
SMEM = pltpu.SMEM
VMEM = pltpu.VMEM


def vmem_params(mib):
    return pltpu.CompilerParams(vmem_limit_bytes=mib * 2**20)


def plan_kernel(pairs, slots, places_ref, cand_ref, query_block_ref, valid_ref, lengths_ref, sel_ref, table_ref, pairs_ref, *scratch):
    first_ref, second_ref, slot_ref = scratch
    owner, side, blocks = places_ref[0], places_ref[1], places_ref[2]

    def step(k, count):
        block = cand_ref[k]
        found = lax.fori_loop(
            0, k, lambda e, f: jnp.where(cand_ref[e] == block, slot_ref[e], f), jnp.int32(-1)
        )
        new = found < 0
        slot = jnp.minimum(jnp.where(new, count, found), pairs // 2 - 1)
        slot_ref[k] = slot

        @pl.when(new)
        def _():
            sel_ref[slot] = block
            first_ref[slot] = k

        second_ref[slot] = k
        return count + new.astype(jnp.int32)

    lax.fori_loop(0, pairs, step, jnp.int32(0))

    def line(i, carry):
        k = i // 2
        slot = side * slots + k
        pair = jnp.where(i - 2 * k == 0, first_ref[slot], second_ref[slot])
        query = query_block_ref[pair]
        table_ref[i * LINE + 1] = query
        table_ref[i * LINE + 2] = valid_ref[pair]
        for a in range(BLK):
            table_ref[i * LINE + 3 + a] = lengths_ref[sel_ref[slot] * BLK + a]
            table_ref[i * LINE + 3 + BLK + a] = lengths_ref[(owner * blocks + query) * BLK + a]
        return carry

    lax.fori_loop(0, 2 * slots, line, 0)

    def both(slot, carry):
        pairs_ref[2 * slot] = first_ref[slot]
        pairs_ref[2 * slot + 1] = second_ref[slot]
        return carry

    lax.fori_loop(0, pairs // 2, both, 0)


def plan(places, cand_block, query_block, valid, lengths, slots):
    pairs = cand_block.shape[0]
    shapes = (pairs // 2, 2 * slots * LINE, pairs)
    return pl.pallas_call(
        functools.partial(plan_kernel, pairs, slots),
        out_shape=[jax.ShapeDtypeStruct((n,), jnp.int32) for n in shapes],
        in_specs=[pl.BlockSpec(memory_space=SMEM)] * 5,
        out_specs=[pl.BlockSpec(memory_space=SMEM)] * 3,
        scratch_shapes=[SMEM((pairs,), jnp.int32)] * 3,
    )(places, cand_block, query_block, valid, lengths)


def project_kernel(me_ref, states_ref, weight_ref, out_ref):
    out_ref[0, 0] = jnp.dot(
        states_ref[0], weight_ref[...], preferred_element_type=jnp.float32
    ).astype(out_ref.dtype)


def project(me, states, weight, shares, offset, count, dtype):
    blocks, rows, width = states.shape
    out_width = weight.shape[1]
    part = rows // shares
    return pl.pallas_call(
        project_kernel,
        out_shape=jax.ShapeDtypeStruct((count, blocks, part, out_width), dtype),
        grid_spec=pltpu.PrefetchScalarGridSpec(
            num_scalar_prefetch=1,
            grid=(count, blocks),
            in_specs=[
                pl.BlockSpec(
                    (1, part, width), lambda d, b, m: (b, lax.rem(m[0] + offset + d, shares), 0)
                ),
                pl.BlockSpec((width, out_width), lambda d, b, m: (0, 0)),
            ],
            out_specs=pl.BlockSpec((1, 1, part, out_width), lambda d, b, m: (d, b, 0, 0)),
        ),
        cost_estimate=pl.CostEstimate(
            flops=2 * count * blocks * part * width * out_width,
            bytes_accessed=2 * count * blocks * part * width,
            transcendentals=0,
        ),
    )(me, states, weight)


def unit_kernel(others, pieces, keep_ref, *refs):
    out_ref = refs[-1]
    total = keep_ref[0, 0]
    for ref in refs[:others]:
        total = total + ref[0].astype(jnp.float32)
    norm = jnp.sum(total * total, axis=-1, keepdims=True)
    unit = (total * lax.rsqrt(norm + 1e-06)).astype(jnp.bfloat16)
    if pieces is None:
        out_ref[0] = unit
    else:
        size = unit.shape[0] // pieces
        for m in range(pieces):
            out_ref[m, 0] = unit[m * size : (m + 1) * size]


def unit_rows(keep, received, owners):
    _, blocks, part, width = keep.shape
    size = part // owners
    direct = size % 16 == 0
    if direct:
        shape = (owners, blocks, size, width)
        out_spec = pl.BlockSpec((owners, 1, size, width), lambda b: (0, b, 0, 0))
    else:
        shape = (blocks, part, width)
        out_spec = pl.BlockSpec((1, part, width), lambda b: (b, 0, 0))
    out = pl.pallas_call(
        functools.partial(unit_kernel, len(received), owners if direct else None),
        out_shape=jax.ShapeDtypeStruct(shape, jnp.bfloat16),
        grid=(blocks,),
        in_specs=[pl.BlockSpec((1, 1, part, width), lambda b: (0, b, 0, 0))]
        + [pl.BlockSpec((1, part, width), lambda b: (b, 0, 0))] * len(received),
        out_specs=out_spec,
    )(keep, *received)
    if direct:
        return out
    return out.reshape(blocks, owners, size, width).transpose(1, 0, 2, 3)


def route_kernel(dests, slots, owners, asked_ref, pieces_ref, out_ref):
    def step(d, carry):
        side = d // owners
        requester = d - side * owners
        for k in range(slots):
            out_ref[d, k] = pieces_ref[asked_ref[requester, side * slots + k]]
        return carry

    lax.fori_loop(0, dests, step, 0)


def route(asked, pieces, owners, shares):
    slots = asked.shape[1] // shares
    dests = owners * shares
    return pl.pallas_call(
        functools.partial(route_kernel, dests, slots, owners),
        out_shape=jax.ShapeDtypeStruct((dests, slots) + pieces.shape[1:], jnp.bfloat16),
        in_specs=[pl.BlockSpec(memory_space=SMEM), pl.BlockSpec(memory_space=VMEM)],
        out_specs=pl.BlockSpec(memory_space=VMEM),
        compiler_params=vmem_params(48),
    )(asked, pieces)


def query_rows(parts, out_ref):
    _, _, core, side = place()
    size = out_ref.shape[1] // 32
    blocks = out_ref.shape[0]
    for rel, ref in enumerate(parts):
        base = (side ^ (rel // 2)) * (16 * size) + (core ^ (rel % 2)) * (2 * size)
        for z in range(4):
            for x in range(2):
                target = pl.multiple_of(base + z * 4 * size + x * size, 16)
                for b in range(blocks):
                    begin = ((z * 2 + x) * blocks + b) * size
                    out_ref[b, pl.ds(target, size)] = ref[begin : begin + size]


def score_kernel(length, parts, table_ref, *refs):
    if parts:
        cand_ref, out_ref, totals_ref, block_ref, query_ref = refs[parts:]
        query_rows(refs[:parts], query_ref)
    else:
        query_ref, cand_ref, out_ref, totals_ref = refs
    rows = query_ref.shape[1]
    slots = cand_ref.shape[-3]
    totals_ref[...] = jnp.ones_like(totals_ref)
    upper = lax.broadcasted_iota(jnp.int32, (length // 2, COLS), 0) + length // 2
    lane = lax.broadcasted_iota(jnp.int32, (16, length), 1)

    def slot_step(k, carry):
        if parts:
            pieces, _, size, _ = cand_ref.shape
            for piece in range(pieces):
                begin = (piece // 4 * 4 + piece % 2 * 2 + piece // 2 % 2) * size
                block_ref[begin : begin + size] = cand_ref[piece, k]
        for i in range(2):
            line = (2 * k + i) * LINE
            query = table_ref[line + 1]
            for start in range(0, rows, COLS):
                sim = lax.dot_general(
                    block_ref[...] if parts else cand_ref[k],
                    query_ref[query, start : start + COLS],
                    (((1,), (1,)), ((), ())),
                    preferred_element_type=jnp.float32,
                )
                for b in range(BLK):
                    live = table_ref[line + 3 + b]
                    low = jnp.exp2(sim[b * length : b * length + length // 2] * EXP2_SCALE)
                    high = jnp.exp2(sim[b * length + length // 2 : (b + 1) * length] * EXP2_SCALE)
                    both = low + jnp.where(upper < live, high, 0.0)
                    totals_ref[2 * k + i, b : b + 1, start : start + COLS] = jnp.sum(
                        both, axis=0, keepdims=True
                    )
        return carry

    lax.fori_loop(0, slots, slot_step, 0)
    for tile in range(out_ref.shape[0]):
        score = jnp.zeros((16, length), jnp.float32)
        for i in range(tile * PACK, min((tile + 1) * PACK, 2 * slots)):
            line = i * LINE
            keep = table_ref[line + 2].astype(jnp.float32) / (SHARPNESS * length)
            for a in range(BLK):
                live = table_ref[line + 3 + BLK + a]
                logs = jnp.log(totals_ref[i, :, a * length : (a + 1) * length])
                summed = jnp.sum(jnp.where(lane < live, logs, 0.0), axis=1, keepdims=True)
                score = jnp.where(lane == i % PACK * BLK + a, summed * keep, score)
        out_ref[tile] = score


def score(table, query, cand, blocks, length):
    slots, width = cand.shape[-3], cand.shape[-1]
    rows = BLK * length
    parts = len(query) if isinstance(query, list) else 0
    count = 2 * slots * rows * rows
    scratch = [VMEM((2 * slots, 16, rows), jnp.float32)]
    if parts:
        scratch += [VMEM((rows, width), jnp.bfloat16), VMEM((blocks, rows, width), jnp.bfloat16)]
    return pl.pallas_call(
        functools.partial(score_kernel, length, parts),
        out_shape=jax.ShapeDtypeStruct((-(-2 * slots // PACK), 16, length), jnp.float32),
        in_specs=[pl.BlockSpec(memory_space=SMEM)]
        + [pl.BlockSpec(memory_space=VMEM)] * (max(parts, 1) + 1),
        out_specs=pl.BlockSpec(memory_space=VMEM),
        scratch_shapes=scratch,
        compiler_params=vmem_params(28),
        cost_estimate=pl.CostEstimate(
            flops=2 * count * width, bytes_accessed=4 * rows * width, transcendentals=count
        ),
    )(table, *(query if parts else [query]), cand)


def place_kernel(shares, count, where_ref, pairs_ref, *refs):
    parts, out_ref = refs[:-1], refs[-1]
    for d, ref in enumerate(parts):
        side = lax.rem(where_ref[1] - d + shares, shares)
        for i in range(count):
            tile = ref[i // PACK]
            if i % PACK:
                tile = pltpu.roll(tile, tile.shape[1] - i % PACK * BLK, 1)
            out_ref[pairs_ref[side * count + i]] = tile[:BLK, :BLK]


def place_scores(where, pair_of, parts, pairs):
    shares = len(parts)
    return pl.pallas_call(
        functools.partial(place_kernel, shares, pairs // shares),
        out_shape=jax.ShapeDtypeStruct((pairs, BLK, BLK), jnp.float32),
        in_specs=[pl.BlockSpec(memory_space=SMEM)] * 2 + [pl.BlockSpec(memory_space=VMEM)] * shares,
        out_specs=pl.BlockSpec(memory_space=VMEM),
        compiler_params=vmem_params(4),
    )(where, pair_of, *parts)


def local_general(states, proj_weight, lengths, query_block, cand_block, pair_valid):
    shares = lax.axis_size("narrow")
    owners = lax.axis_size("wide")
    side = lax.axis_index("narrow").astype(jnp.int32)
    owner = lax.axis_index("wide").astype(jnp.int32)
    paras, length, width_part = states.shape
    width = proj_weight.shape[1]
    blocks = paras // BLK
    rows = BLK * length
    flat = states.reshape(blocks, rows, width_part)
    me = side.reshape(1)

    def shift(d):
        return [(i, (i + d) % shares) for i in range(shares)]

    slots = cand_block.shape[0] // 2 // shares
    places = jnp.stack([owner, side, jnp.int32(blocks)])
    sel, table, pair_of = plan(places, cand_block, query_block, pair_valid, lengths, slots)
    sent = project(me, flat, proj_weight, shares, 1, shares - 1, jnp.bfloat16)
    received = [lax.ppermute(sent[d - 1], "narrow", shift(d)) for d in range(1, shares)]
    asked = lax.all_to_all(
        jnp.broadcast_to(sel[None], (owners,) + sel.shape), "wide", 0, 0, tiled=True
    )
    kept = project(me, flat, proj_weight, shares, 0, 1, jnp.float32)
    mine = unit_rows(kept, received, owners)
    spread = lax.all_to_all(mine, "wide", 0, 0, tiled=True)
    size = mine.shape[2]
    by_side = [mine] + [lax.ppermute(mine, "narrow", shift(d)) for d in range(1, shares)]
    order = jnp.stack(by_side)
    query = jnp.stack(
        [lax.dynamic_index_in_dim(order, lax.rem(side - s + shares, shares), 0, False) for s in range(shares)]
    )
    query = query.transpose(2, 0, 1, 3, 4).reshape(blocks, rows, width)
    outgoing = route(asked, spread.reshape(owners * blocks, size, width), owners, shares)
    incoming = lax.all_to_all(outgoing, ("narrow", "wide"), 0, 0, tiled=True)
    cand = incoming.transpose(1, 0, 2, 3).reshape(-1, rows, width)
    part = score(table, query, cand, blocks, length)
    parts = [part] + [lax.ppermute(part, "narrow", shift(d)) for d in range(1, shares)]
    return place_scores(places, pair_of, parts, cand_block.shape[0])


def place():
    owner = lax.axis_index("wide")
    return owner // 4, owner // 2 % 2, owner % 2, lax.axis_index("narrow")


def split_kernel(first, over, states_ref, weight_ref, *refs):
    *outs, rows_ref, sems = refs
    _, _, core, side = place()
    blocks, part, _ = rows_ref.shape
    size = part // 16
    start = pl.multiple_of((side ^ over) * part, part)

    def load(b):
        return pltpu.make_async_copy(
            states_ref.at[first + b, pl.ds(start, part)], rows_ref.at[b], sems.at[b]
        )

    for b in range(blocks):
        load(b).start()
    for b in range(blocks):
        load(b).wait()
        for z in range(4):
            for flip in range(2):
                source = pl.multiple_of((core ^ flip) * (2 * size) + z * 4 * size, 16)
                both = jnp.dot(
                    rows_ref[b, pl.ds(source, 2 * size)],
                    weight_ref[...],
                    preferred_element_type=jnp.float32,
                ).astype(jnp.bfloat16)
                for x in range(2):
                    target = ((z * 2 + x) * blocks + b) * size
                    outs[flip][target : target + size] = both[x * size : (x + 1) * size]


def split(over, states, weight, first):
    _, rows, width = states.shape
    out_width = weight.shape[1]
    part = rows // 2
    out_rows = 8 * CHUNK * (part // 16)
    return pl.pallas_call(
        functools.partial(split_kernel, first, over),
        out_shape=(jax.ShapeDtypeStruct((out_rows, out_width), jnp.bfloat16),) * 2,
        in_specs=[pl.BlockSpec(memory_space=pltpu.HBM), pl.BlockSpec(memory_space=VMEM)],
        out_specs=[pl.BlockSpec(memory_space=VMEM)] * 2,
        scratch_shapes=[
            VMEM((CHUNK, part, width), jnp.bfloat16),
            pltpu.SemaphoreType.DMA((CHUNK,)),
        ],
        compiler_params=vmem_params(50),
        cost_estimate=pl.CostEstimate(
            flops=2 * CHUNK * part * width * out_width,
            bytes_accessed=2 * CHUNK * part * width,
            transcendentals=0,
        ),
    )(states, weight)


def gather_unit_kernel(size, sel_ref, sel_near_ref, y_ref, cy_ref, own_ref, c_ref, *outs):
    z, x, _, _ = place()
    sends, query = outs[:8], outs[8:]
    span = CHUNK * size
    shape = (16, own_ref.shape[1])
    row, lane = (lax.broadcasted_iota(jnp.int32, shape, axis) for axis in range(2))
    asked = jnp.zeros(shape, jnp.int32)
    for flip, ids_ref in enumerate((sel_ref, sel_near_ref)):
        for k in range(ids_ref.shape[0]):
            asked = jnp.where((row == flip) & (lane == k), ids_ref[k], asked)
    asked = asked.astype(jnp.float32).astype(jnp.bfloat16)
    for rel, send_ref in zip(SPREAD, sends):
        source = pl.multiple_of(((z ^ (rel // 2)) * 2 + (x ^ (rel % 2))) * span, 16)
        for flip, (one_ref, two_ref) in enumerate(((own_ref, y_ref), (c_ref, cy_ref))):
            total = one_ref[pl.ds(source, span)].astype(jnp.float32)
            total = total + two_ref[pl.ds(source, span)].astype(jnp.float32)
            norm = jnp.sum(total * total, axis=-1, keepdims=True)
            unit = (total * lax.rsqrt(norm + 1e-06)).astype(jnp.bfloat16)
            send_ref[flip * span : (flip + 1) * span] = unit
            query[flip][pl.ds(source, span)] = unit
        send_ref[2 * span :] = asked


def gather_unit(sel, sel_near, y, cy, own, c, size):
    rows, width = own.shape
    send = jax.ShapeDtypeStruct((2 * CHUNK * size + 16, width), jnp.bfloat16)
    query = jax.ShapeDtypeStruct((rows, width), jnp.bfloat16)
    return pl.pallas_call(
        functools.partial(gather_unit_kernel, size),
        out_shape=(send,) * 8 + (query,) * 2,
        in_specs=[pl.BlockSpec(memory_space=SMEM)] * 2 + [pl.BlockSpec(memory_space=VMEM)] * 4,
        out_specs=[pl.BlockSpec(memory_space=VMEM)] * 10,
        compiler_params=vmem_params(12),
    )(sel, sel_near, y, cy, own, c)


def cube_route_kernel(size, slots, *refs):
    spread, out_ref, pieces_ref, rows_ref, asked_ref, sem = refs[:8], *refs[8:]
    z, x, core, _ = place()
    blocks = pieces_ref.shape[0] // 16
    span = CHUNK * size
    chips = [(z ^ (rel // 2)) * 2 + (x ^ (rel % 2)) for rel in SPREAD]
    for ref, chip in zip(spread, chips):
        ids = ref[2 * span :].astype(jnp.float32)
        for flip in range(2):
            rows_ref[pl.ds(chip * 2 + (core ^ flip), 1)] = ids[flip : flip + 1].astype(jnp.int32)
    copy = pltpu.make_async_copy(rows_ref, asked_ref, sem)
    copy.start()
    for ref, chip in zip(spread, chips):
        for flip in range(2):
            owner = chip * 2 + (core ^ flip)
            for b in range(blocks):
                row = flip * span + b * size
                pieces_ref[owner * blocks + b] = ref[row : row + size]
    copy.wait()

    def step(d, carry):
        side = d // 16
        for k in range(slots):
            out_ref[d, k] = pieces_ref[asked_ref[d - side * 16, side * slots + k]]
        return carry

    lax.fori_loop(0, 32, step, 0, unroll=4)


def cube_route(spread, size, slots, blocks):
    width = spread[0].shape[1]
    return pl.pallas_call(
        functools.partial(cube_route_kernel, size, slots),
        out_shape=jax.ShapeDtypeStruct((32, slots, size, width), jnp.bfloat16),
        in_specs=[pl.BlockSpec(memory_space=VMEM)] * len(spread),
        out_specs=pl.BlockSpec(memory_space=VMEM),
        scratch_shapes=[
            VMEM((16 * blocks, size, width), jnp.bfloat16),
            VMEM((16, width), jnp.int32),
            SMEM((16, width), jnp.int32),
            pltpu.SemaphoreType.DMA,
        ],
        compiler_params=vmem_params(16),
    )(*spread)


def local_cube(states, proj_weight, lengths, query_block, cand_block, pair_valid):
    side = lax.axis_index("narrow").astype(jnp.int32)
    owner = lax.axis_index("wide").astype(jnp.int32)
    paras, length, width_part = states.shape
    width = proj_weight.shape[1]
    blocks = paras // BLK
    rows = BLK * length
    size = rows // 32
    slots = cand_block.shape[0] // 4
    flat = states.reshape(blocks, rows, width_part)

    def near(array, rel):
        flip = rel % 2 * 2 + rel // 2
        return lax.ppermute(array, ("wide", "narrow"), [(i, i ^ flip) for i in range(32)])

    def along(array, rel):
        flip = rel * 2
        return lax.ppermute(array, "wide", [(i, i ^ flip) for i in range(16)])

    places = jnp.stack([owner, side, jnp.int32(blocks)])
    sel, table, pair_of = plan(places, cand_block, query_block, pair_valid, lengths, slots)
    sel_near = near(sel, 1)
    far = split(1, flat, proj_weight, 0)
    weight, *far = lax.optimization_barrier((proj_weight, *far))
    y, cy = near(far[0], 2), near(far[1], 3)
    own, aside = split(0, flat, weight, 0)
    c = near(aside, 1)
    *sends, own, other = gather_unit(sel, sel_near, y, cy, own, c, size)
    own_y = near(own, 2)
    spread = [along(send, rel) if rel else send for rel, send in zip(SPREAD, sends)]
    outgoing = cube_route(spread, size, slots, blocks)
    outgoing, other, own_y = lax.optimization_barrier((outgoing, other, own_y))
    incoming = lax.all_to_all(outgoing, ("narrow", "wide"), 0, 0, tiled=True)
    other = near(other, 1)
    query = [own, other, own_y, near(other, 2)]
    part = score(table, query, incoming, blocks, length)
    parts = [part, lax.ppermute(part, "narrow", [(0, 1), (1, 0)])]
    return place_scores(places, pair_of, parts, cand_block.shape[0])


def solution(mesh):
    in_specs = (P("wide", None, "narrow"), P("narrow", None), P(), P("wide"), P("wide"), P("wide"))
    out_specs = P("wide", None, None)
    cube = mesh.shape["wide"] == 16 and mesh.shape["narrow"] == 2
    local = local_cube if cube else local_general
    return jax.shard_map(local, mesh=mesh, in_specs=in_specs, out_specs=out_specs, check_vma=False)
```

```python
import functools
import math

import jax
import jax.numpy as jnp
from jax import lax
from jax.experimental import pallas as pl
from jax.experimental.pallas import tpu as pltpu
from jax.sharding import PartitionSpec as P

BLK = 12
SHARPNESS = 20.0
EXP2_SCALE = SHARPNESS * math.log2(math.e)
COLS = 512
CHUNK = 2
LINE = 32
PACK = 6
SPREAD = (0, 4, 6, 5, 7, 2, 3, 1)
SMEM = pltpu.SMEM
VMEM = pltpu.VMEM


def vmem_params(mib):
    return pltpu.CompilerParams(vmem_limit_bytes=mib * 2**20)


def plan_kernel(pairs, slots, places_ref, cand_ref, query_block_ref, valid_ref, lengths_ref, sel_ref, table_ref, pairs_ref, *scratch):
    first_ref, second_ref, slot_ref = scratch
    owner, side, blocks = places_ref[0], places_ref[1], places_ref[2]

    def step(k, count):
        block = cand_ref[k]
        found = lax.fori_loop(
            0, k, lambda e, f: jnp.where(cand_ref[e] == block, slot_ref[e], f), jnp.int32(-1)
        )
        new = found < 0
        slot = jnp.minimum(jnp.where(new, count, found), pairs // 2 - 1)
        slot_ref[k] = slot

        @pl.when(new)
        def _():
            sel_ref[slot] = block
            first_ref[slot] = k

        second_ref[slot] = k
        return count + new.astype(jnp.int32)

    lax.fori_loop(0, pairs, step, jnp.int32(0))

    def line(i, carry):
        k = i // 2
        slot = side * slots + k
        pair = jnp.where(i - 2 * k == 0, first_ref[slot], second_ref[slot])
        query = query_block_ref[pair]
        table_ref[i * LINE + 1] = query
        table_ref[i * LINE + 2] = valid_ref[pair]
        for a in range(BLK):
            table_ref[i * LINE + 3 + a] = lengths_ref[sel_ref[slot] * BLK + a]
            table_ref[i * LINE + 3 + BLK + a] = lengths_ref[(owner * blocks + query) * BLK + a]
        return carry

    lax.fori_loop(0, 2 * slots, line, 0)

    def both(slot, carry):
        pairs_ref[2 * slot] = first_ref[slot]
        pairs_ref[2 * slot + 1] = second_ref[slot]
        return carry

    lax.fori_loop(0, pairs // 2, both, 0)


def plan(places, cand_block, query_block, valid, lengths, slots):
    pairs = cand_block.shape[0]
    shapes = (pairs // 2, 2 * slots * LINE, pairs)
    return pl.pallas_call(
        functools.partial(plan_kernel, pairs, slots),
        out_shape=[jax.ShapeDtypeStruct((n,), jnp.int32) for n in shapes],
        in_specs=[pl.BlockSpec(memory_space=SMEM)] * 5,
        out_specs=[pl.BlockSpec(memory_space=SMEM)] * 3,
        scratch_shapes=[SMEM((pairs,), jnp.int32)] * 3,
    )(places, cand_block, query_block, valid, lengths)


def project_kernel(me_ref, states_ref, weight_ref, out_ref):
    out_ref[0, 0] = jnp.dot(
        states_ref[0], weight_ref[...], preferred_element_type=jnp.float32
    ).astype(out_ref.dtype)


def project(me, states, weight, shares, offset, count, dtype):
    blocks, rows, width = states.shape
    out_width = weight.shape[1]
    part = rows // shares
    return pl.pallas_call(
        project_kernel,
        out_shape=jax.ShapeDtypeStruct((count, blocks, part, out_width), dtype),
        grid_spec=pltpu.PrefetchScalarGridSpec(
            num_scalar_prefetch=1,
            grid=(count, blocks),
            in_specs=[
                pl.BlockSpec(
                    (1, part, width), lambda d, b, m: (b, lax.rem(m[0] + offset + d, shares), 0)
                ),
                pl.BlockSpec((width, out_width), lambda d, b, m: (0, 0)),
            ],
            out_specs=pl.BlockSpec((1, 1, part, out_width), lambda d, b, m: (d, b, 0, 0)),
        ),
        cost_estimate=pl.CostEstimate(
            flops=2 * count * blocks * part * width * out_width,
            bytes_accessed=2 * count * blocks * part * width,
            transcendentals=0,
        ),
    )(me, states, weight)


def unit_kernel(others, pieces, keep_ref, *refs):
    out_ref = refs[-1]
    total = keep_ref[0, 0]
    for ref in refs[:others]:
        total = total + ref[0].astype(jnp.float32)
    norm = jnp.sum(total * total, axis=-1, keepdims=True)
    unit = (total * lax.rsqrt(norm + 1e-06)).astype(jnp.bfloat16)
    if pieces is None:
        out_ref[0] = unit
    else:
        size = unit.shape[0] // pieces
        for m in range(pieces):
            out_ref[m, 0] = unit[m * size : (m + 1) * size]


def unit_rows(keep, received, owners):
    _, blocks, part, width = keep.shape
    size = part // owners
    direct = size % 16 == 0
    if direct:
        shape = (owners, blocks, size, width)
        out_spec = pl.BlockSpec((owners, 1, size, width), lambda b: (0, b, 0, 0))
    else:
        shape = (blocks, part, width)
        out_spec = pl.BlockSpec((1, part, width), lambda b: (b, 0, 0))
    out = pl.pallas_call(
        functools.partial(unit_kernel, len(received), owners if direct else None),
        out_shape=jax.ShapeDtypeStruct(shape, jnp.bfloat16),
        grid=(blocks,),
        in_specs=[pl.BlockSpec((1, 1, part, width), lambda b: (0, b, 0, 0))]
        + [pl.BlockSpec((1, part, width), lambda b: (b, 0, 0))] * len(received),
        out_specs=out_spec,
    )(keep, *received)
    if direct:
        return out
    return out.reshape(blocks, owners, size, width).transpose(1, 0, 2, 3)


def route_kernel(dests, slots, owners, asked_ref, pieces_ref, out_ref):
    def step(d, carry):
        side = d // owners
        requester = d - side * owners
        for k in range(slots):
            out_ref[d, k] = pieces_ref[asked_ref[requester, side * slots + k]]
        return carry

    lax.fori_loop(0, dests, step, 0)


def route(asked, pieces, owners, shares):
    slots = asked.shape[1] // shares
    dests = owners * shares
    return pl.pallas_call(
        functools.partial(route_kernel, dests, slots, owners),
        out_shape=jax.ShapeDtypeStruct((dests, slots) + pieces.shape[1:], jnp.bfloat16),
        in_specs=[pl.BlockSpec(memory_space=SMEM), pl.BlockSpec(memory_space=VMEM)],
        out_specs=pl.BlockSpec(memory_space=VMEM),
        compiler_params=vmem_params(48),
    )(asked, pieces)


def query_rows(parts, out_ref):
    _, _, core, side = place()
    size = out_ref.shape[1] // 32
    half = 8 * CHUNK * size
    early, early_far = parts[:2]
    pieces = [(ref, flip * half, far, flip, 0) for far, ref in ((0, early), (1, early_far)) for flip in range(2)]
    pieces += [(ref, 0, rel // 2, rel % 2, CHUNK) for rel, ref in enumerate(parts[2:])]
    for ref, begin, far, flip, first in pieces:
        base = (side ^ far) * (16 * size) + (core ^ flip) * (2 * size)
        for z in range(4):
            for x in range(2):
                target = pl.multiple_of(base + z * 4 * size + x * size, 16)
                for b in range(CHUNK):
                    row = begin + ((z * 2 + x) * CHUNK + b) * size
                    out_ref[first + b, pl.ds(target, size)] = ref[row : row + size]


def score_kernel(length, parts, table_ref, *refs):
    if parts:
        cand_ref, out_ref, totals_ref, block_ref, query_ref = refs[parts:]
        query_rows(refs[:parts], query_ref)
    else:
        query_ref, cand_ref, out_ref, totals_ref = refs
    rows = query_ref.shape[1]
    slots = cand_ref.shape[-3]
    totals_ref[...] = jnp.ones_like(totals_ref)
    upper = lax.broadcasted_iota(jnp.int32, (length // 2, COLS), 0) + length // 2
    lane = lax.broadcasted_iota(jnp.int32, (16, length), 1)

    def slot_step(k, carry):
        if parts:
            pieces, _, size, _ = cand_ref.shape
            for piece in range(pieces):
                begin = (piece // 4 * 4 + piece % 2 * 2 + piece // 2 % 2) * size
                block_ref[begin : begin + size] = cand_ref[piece, k]
        for i in range(2):
            line = (2 * k + i) * LINE
            query = table_ref[line + 1]
            for start in range(0, rows, COLS):
                sim = lax.dot_general(
                    block_ref[...] if parts else cand_ref[k],
                    query_ref[query, start : start + COLS],
                    (((1,), (1,)), ((), ())),
                    preferred_element_type=jnp.float32,
                )
                for b in range(BLK):
                    live = table_ref[line + 3 + b]
                    low = jnp.exp2(sim[b * length : b * length + length // 2] * EXP2_SCALE)
                    high = jnp.exp2(sim[b * length + length // 2 : (b + 1) * length] * EXP2_SCALE)
                    both = low + jnp.where(upper < live, high, 0.0)
                    totals_ref[2 * k + i, b : b + 1, start : start + COLS] = jnp.sum(
                        both, axis=0, keepdims=True
                    )
        return carry

    lax.fori_loop(0, slots, slot_step, 0)
    for tile in range(out_ref.shape[0]):
        score = jnp.zeros((16, length), jnp.float32)
        for i in range(tile * PACK, min((tile + 1) * PACK, 2 * slots)):
            line = i * LINE
            keep = table_ref[line + 2].astype(jnp.float32) / (SHARPNESS * length)
            for a in range(BLK):
                live = table_ref[line + 3 + BLK + a]
                logs = jnp.log(totals_ref[i, :, a * length : (a + 1) * length])
                summed = jnp.sum(jnp.where(lane < live, logs, 0.0), axis=1, keepdims=True)
                score = jnp.where(lane == i % PACK * BLK + a, summed * keep, score)
        out_ref[tile] = score


def score(table, query, cand, blocks, length):
    slots, width = cand.shape[-3], cand.shape[-1]
    rows = BLK * length
    parts = len(query) if isinstance(query, list) else 0
    count = 2 * slots * rows * rows
    scratch = [VMEM((2 * slots, 16, rows), jnp.float32)]
    if parts:
        scratch += [VMEM((rows, width), jnp.bfloat16), VMEM((blocks, rows, width), jnp.bfloat16)]
    return pl.pallas_call(
        functools.partial(score_kernel, length, parts),
        out_shape=jax.ShapeDtypeStruct((-(-2 * slots // PACK), 16, length), jnp.float32),
        in_specs=[pl.BlockSpec(memory_space=SMEM)]
        + [pl.BlockSpec(memory_space=VMEM)] * (max(parts, 1) + 1),
        out_specs=pl.BlockSpec(memory_space=VMEM),
        scratch_shapes=scratch,
        compiler_params=vmem_params(28),
        cost_estimate=pl.CostEstimate(
            flops=2 * count * width, bytes_accessed=4 * rows * width, transcendentals=count
        ),
    )(table, *(query if parts else [query]), cand)


def place_kernel(shares, count, where_ref, pairs_ref, *refs):
    parts, out_ref = refs[:-1], refs[-1]
    for d, ref in enumerate(parts):
        side = lax.rem(where_ref[1] - d + shares, shares)
        for i in range(count):
            tile = ref[i // PACK]
            if i % PACK:
                tile = pltpu.roll(tile, tile.shape[1] - i % PACK * BLK, 1)
            out_ref[pairs_ref[side * count + i]] = tile[:BLK, :BLK]


def place_scores(where, pair_of, parts, pairs):
    shares = len(parts)
    return pl.pallas_call(
        functools.partial(place_kernel, shares, pairs // shares),
        out_shape=jax.ShapeDtypeStruct((pairs, BLK, BLK), jnp.float32),
        in_specs=[pl.BlockSpec(memory_space=SMEM)] * 2 + [pl.BlockSpec(memory_space=VMEM)] * shares,
        out_specs=pl.BlockSpec(memory_space=VMEM),
        compiler_params=vmem_params(4),
    )(where, pair_of, *parts)


def local_general(states, proj_weight, lengths, query_block, cand_block, pair_valid):
    shares = lax.axis_size("narrow")
    owners = lax.axis_size("wide")
    side = lax.axis_index("narrow").astype(jnp.int32)
    owner = lax.axis_index("wide").astype(jnp.int32)
    paras, length, width_part = states.shape
    width = proj_weight.shape[1]
    blocks = paras // BLK
    rows = BLK * length
    flat = states.reshape(blocks, rows, width_part)
    me = side.reshape(1)

    def shift(d):
        return [(i, (i + d) % shares) for i in range(shares)]

    slots = cand_block.shape[0] // 2 // shares
    places = jnp.stack([owner, side, jnp.int32(blocks)])
    sel, table, pair_of = plan(places, cand_block, query_block, pair_valid, lengths, slots)
    sent = project(me, flat, proj_weight, shares, 1, shares - 1, jnp.bfloat16)
    received = [lax.ppermute(sent[d - 1], "narrow", shift(d)) for d in range(1, shares)]
    asked = lax.all_to_all(
        jnp.broadcast_to(sel[None], (owners,) + sel.shape), "wide", 0, 0, tiled=True
    )
    kept = project(me, flat, proj_weight, shares, 0, 1, jnp.float32)
    mine = unit_rows(kept, received, owners)
    spread = lax.all_to_all(mine, "wide", 0, 0, tiled=True)
    size = mine.shape[2]
    by_side = [mine] + [lax.ppermute(mine, "narrow", shift(d)) for d in range(1, shares)]
    order = jnp.stack(by_side)
    query = jnp.stack(
        [lax.dynamic_index_in_dim(order, lax.rem(side - s + shares, shares), 0, False) for s in range(shares)]
    )
    query = query.transpose(2, 0, 1, 3, 4).reshape(blocks, rows, width)
    outgoing = route(asked, spread.reshape(owners * blocks, size, width), owners, shares)
    incoming = lax.all_to_all(outgoing, ("narrow", "wide"), 0, 0, tiled=True)
    cand = incoming.transpose(1, 0, 2, 3).reshape(-1, rows, width)
    part = score(table, query, cand, blocks, length)
    parts = [part] + [lax.ppermute(part, "narrow", shift(d)) for d in range(1, shares)]
    return place_scores(places, pair_of, parts, cand_block.shape[0])


def place():
    owner = lax.axis_index("wide")
    return owner // 4, owner // 2 % 2, owner % 2, lax.axis_index("narrow")


def split_kernel(first, over, states_ref, weight_ref, *refs):
    *outs, rows_ref, sems = refs
    _, _, core, side = place()
    blocks, part, _ = rows_ref.shape
    size = part // 16
    start = pl.multiple_of((side ^ over) * part, part)

    def load(b):
        return pltpu.make_async_copy(
            states_ref.at[first + b, pl.ds(start, part)], rows_ref.at[b], sems.at[b]
        )

    for b in range(blocks):
        load(b).start()
    for b in range(blocks):
        load(b).wait()
        for z in range(4):
            for flip in range(2):
                source = pl.multiple_of((core ^ flip) * (2 * size) + z * 4 * size, 16)
                both = jnp.dot(
                    rows_ref[b, pl.ds(source, 2 * size)],
                    weight_ref[...],
                    preferred_element_type=jnp.float32,
                ).astype(jnp.bfloat16)
                for x in range(2):
                    target = ((z * 2 + x) * blocks + b) * size
                    outs[flip][target : target + size] = both[x * size : (x + 1) * size]


def split(over, states, weight, first):
    _, rows, width = states.shape
    out_width = weight.shape[1]
    part = rows // 2
    out_rows = 8 * CHUNK * (part // 16)
    return pl.pallas_call(
        functools.partial(split_kernel, first, over),
        out_shape=(jax.ShapeDtypeStruct((out_rows, out_width), jnp.bfloat16),) * 2,
        in_specs=[pl.BlockSpec(memory_space=pltpu.HBM), pl.BlockSpec(memory_space=VMEM)],
        out_specs=[pl.BlockSpec(memory_space=VMEM)] * 2,
        scratch_shapes=[
            VMEM((CHUNK, part, width), jnp.bfloat16),
            pltpu.SemaphoreType.DMA((CHUNK,)),
        ],
        compiler_params=vmem_params(50),
        cost_estimate=pl.CostEstimate(
            flops=2 * CHUNK * part * width * out_width,
            bytes_accessed=2 * CHUNK * part * width,
            transcendentals=0,
        ),
    )(states, weight)


def unit_sum(one, two):
    total = one.astype(jnp.float32) + two.astype(jnp.float32)
    norm = jnp.sum(total * total, axis=-1, keepdims=True)
    return (total * lax.rsqrt(norm + 1e-06)).astype(jnp.bfloat16)


def early_unit_kernel(size, sel_ref, y_ref, y_flip_ref, own_ref, own_flip_ref, send_ref, query_ref):
    _, _, core, _ = place()
    span = CHUNK * size
    rows = span + 16
    shape = (16, own_ref.shape[1])
    lane = lax.broadcasted_iota(jnp.int32, shape, 1)
    asked = jnp.zeros(shape, jnp.int32)
    for k in range(sel_ref.shape[0]):
        asked = jnp.where(lane == k, sel_ref[k], asked)
    asked = asked.astype(jnp.float32).astype(jnp.bfloat16)
    for flip, (one_ref, two_ref) in enumerate(((own_ref, y_ref), (own_flip_ref, y_flip_ref))):
        for chip in range(8):
            source = chip * span
            unit = unit_sum(one_ref[source : source + span], two_ref[source : source + span])
            begin = (chip * 2 + (core ^ flip)) * rows
            send_ref[pl.ds(pl.multiple_of(begin, 16), span)] = unit
            send_ref[pl.ds(pl.multiple_of(begin + span, 16), 16)] = asked
            query_ref[8 * span * flip + source : 8 * span * flip + source + span] = unit


def early_unit(sel, y, y_flip, own, own_flip, size):
    rows, width = own.shape
    return pl.pallas_call(
        functools.partial(early_unit_kernel, size),
        out_shape=(
            jax.ShapeDtypeStruct((16 * (CHUNK * size + 16), width), jnp.bfloat16),
            jax.ShapeDtypeStruct((2 * rows, width), jnp.bfloat16),
        ),
        in_specs=[pl.BlockSpec(memory_space=SMEM)] + [pl.BlockSpec(memory_space=VMEM)] * 4,
        out_specs=[pl.BlockSpec(memory_space=VMEM)] * 2,
        compiler_params=vmem_params(12),
    )(sel, y, y_flip, own, own_flip)


def late_unit_kernel(size, y_ref, cy_ref, own_ref, c_ref, *outs):
    z, x, _, _ = place()
    sends, query = outs[:8], outs[8:]
    span = CHUNK * size
    for rel, send_ref in zip(SPREAD, sends):
        source = pl.multiple_of(((z ^ (rel // 2)) * 2 + (x ^ (rel % 2))) * span, 16)
        for flip, (one_ref, two_ref) in enumerate(((own_ref, y_ref), (c_ref, cy_ref))):
            unit = unit_sum(one_ref[pl.ds(source, span)], two_ref[pl.ds(source, span)])
            send_ref[flip * span : (flip + 1) * span] = unit
            query[flip][pl.ds(source, span)] = unit


def late_unit(y, cy, own, c, size):
    rows, width = own.shape
    send = jax.ShapeDtypeStruct((2 * CHUNK * size, width), jnp.bfloat16)
    query = jax.ShapeDtypeStruct((rows, width), jnp.bfloat16)
    return pl.pallas_call(
        functools.partial(late_unit_kernel, size),
        out_shape=(send,) * 8 + (query,) * 2,
        in_specs=[pl.BlockSpec(memory_space=VMEM)] * 4,
        out_specs=[pl.BlockSpec(memory_space=VMEM)] * 10,
        compiler_params=vmem_params(12),
    )(y, cy, own, c)


def cube_route_kernel(size, slots, early_ref, *refs):
    late, out_ref, pieces_ref, rows_ref, asked_ref, sem = refs[:8], *refs[8:]
    z, x, core, _ = place()
    blocks = pieces_ref.shape[0] // 16
    span = CHUNK * size
    for owner in range(16):
        row = owner * (span + 16) + span
        rows_ref[owner : owner + 1] = early_ref[row : row + 16].astype(jnp.float32)[:1].astype(jnp.int32)
    copy = pltpu.make_async_copy(rows_ref, asked_ref, sem)
    copy.start()
    for owner in range(16):
        for b in range(CHUNK):
            row = owner * (span + 16) + b * size
            pieces_ref[owner * blocks + b] = early_ref[row : row + size]
    for rel, ref in zip(SPREAD, late):
        chip = (z ^ (rel // 2)) * 2 + (x ^ (rel % 2))
        for flip in range(2):
            owner = chip * 2 + (core ^ flip)
            for b in range(CHUNK):
                row = flip * span + b * size
                pieces_ref[owner * blocks + CHUNK + b] = ref[row : row + size]
    copy.wait()

    def step(d, carry):
        side = d // 16
        for k in range(slots):
            out_ref[d, k] = pieces_ref[asked_ref[d - side * 16, side * slots + k]]
        return carry

    lax.fori_loop(0, 32, step, 0, unroll=4)


def cube_route(spread, size, slots, blocks):
    width = spread[0].shape[1]
    return pl.pallas_call(
        functools.partial(cube_route_kernel, size, slots),
        out_shape=jax.ShapeDtypeStruct((32, slots, size, width), jnp.bfloat16),
        in_specs=[pl.BlockSpec(memory_space=VMEM)] * len(spread),
        out_specs=pl.BlockSpec(memory_space=VMEM),
        scratch_shapes=[
            VMEM((16 * blocks, size, width), jnp.bfloat16),
            VMEM((16, width), jnp.int32),
            SMEM((16, width), jnp.int32),
            pltpu.SemaphoreType.DMA,
        ],
        compiler_params=vmem_params(16),
    )(*spread)


def local_cube(states, proj_weight, lengths, query_block, cand_block, pair_valid):
    side = lax.axis_index("narrow").astype(jnp.int32)
    owner = lax.axis_index("wide").astype(jnp.int32)
    paras, length, width_part = states.shape
    width = proj_weight.shape[1]
    blocks = paras // BLK
    rows = BLK * length
    size = rows // 32
    slots = cand_block.shape[0] // 4
    flat = states.reshape(blocks, rows, width_part)

    def near(array, rel):
        flip = rel % 2 * 2 + rel // 2
        return lax.ppermute(array, ("wide", "narrow"), [(i, i ^ flip) for i in range(32)])

    def along(array, rel):
        flip = rel * 2
        return lax.ppermute(array, "wide", [(i, i ^ flip) for i in range(16)])

    places = jnp.stack([owner, side, jnp.int32(blocks)])
    sel, table, pair_of = plan(places, cand_block, query_block, pair_valid, lengths, slots)
    far = split(1, flat, proj_weight, 0)
    weight, *far = lax.optimization_barrier((proj_weight, *far))
    crossed = [near(part, 2) for part in far]
    far = split(1, flat, weight, CHUNK)
    weight, sel, *far = lax.optimization_barrier((weight, sel, *far))
    early = split(0, flat, weight, 0)
    own, aside = split(0, flat, weight, CHUNK)
    *early, own, aside = lax.optimization_barrier((*early, own, aside))
    send, early_query = early_unit(sel, *crossed, *early, size)
    y, cy, c = near(far[0], 2), near(far[1], 3), near(aside, 1)
    early_spread = lax.all_to_all(send, "wide", 0, 0, tiled=True)
    *sends, own, other = late_unit(y, cy, own, c, size)
    early_query, sends[0] = lax.optimization_barrier((early_query, sends[0]))
    early_far = near(early_query, 2)
    spread = [along(send, rel) if rel else send for rel, send in zip(SPREAD, sends)]
    outgoing = cube_route([early_spread, *spread], size, slots, blocks)
    outgoing, own, other, early_far = lax.optimization_barrier((outgoing, own, other, early_far))
    incoming = lax.all_to_all(outgoing, ("narrow", "wide"), 0, 0, tiled=True)
    other = near(other, 1)
    query = [early_query, early_far, own, other, near(own, 2), near(other, 2)]
    part = score(table, query, incoming, blocks, length)
    parts = [part, lax.ppermute(part, "narrow", [(0, 1), (1, 0)])]
    return place_scores(places, pair_of, parts, cand_block.shape[0])


def solution(mesh):
    in_specs = (P("wide", None, "narrow"), P("narrow", None), P(), P("wide"), P("wide"), P("wide"))
    out_specs = P("wide", None, None)
    cube = mesh.shape["wide"] == 16 and mesh.shape["narrow"] == 2
    local = local_cube if cube else local_general
    return jax.shard_map(local, mesh=mesh, in_specs=in_specs, out_specs=out_specs, check_vma=False)
```

```python
import functools
import math

import jax
import jax.numpy as jnp
from jax import lax
from jax.experimental import pallas as pl
from jax.experimental.pallas import tpu as pltpu
from jax.sharding import PartitionSpec as P

BLK = 12
SHARPNESS = 20.0
EXP2_SCALE = SHARPNESS * math.log2(math.e)
COLS = 512
CHUNK = 2
LINE = 32
PACK = 6
SPREAD = (0, 4, 6, 5, 7, 2, 3, 1)
SMEM = pltpu.SMEM
VMEM = pltpu.VMEM


def vmem_params(mib):
    return pltpu.CompilerParams(vmem_limit_bytes=mib * 2**20)


def plan_kernel(pairs, slots, places_ref, cand_ref, query_block_ref, valid_ref, lengths_ref, sel_ref, table_ref, pairs_ref, *scratch):
    first_ref, second_ref, slot_ref = scratch
    owner, side, blocks = places_ref[0], places_ref[1], places_ref[2]

    def step(k, count):
        block = cand_ref[k]
        found = lax.fori_loop(
            0, k, lambda e, f: jnp.where(cand_ref[e] == block, slot_ref[e], f), jnp.int32(-1)
        )
        new = found < 0
        slot = jnp.minimum(jnp.where(new, count, found), pairs // 2 - 1)
        slot_ref[k] = slot

        @pl.when(new)
        def _():
            sel_ref[slot] = block
            first_ref[slot] = k

        second_ref[slot] = k
        return count + new.astype(jnp.int32)

    lax.fori_loop(0, pairs, step, jnp.int32(0))

    def line(i, carry):
        k = i // 2
        slot = side * slots + k
        pair = jnp.where(i - 2 * k == 0, first_ref[slot], second_ref[slot])
        query = query_block_ref[pair]
        table_ref[i * LINE + 1] = query
        table_ref[i * LINE + 2] = valid_ref[pair]
        for a in range(BLK):
            table_ref[i * LINE + 3 + a] = lengths_ref[sel_ref[slot] * BLK + a]
            table_ref[i * LINE + 3 + BLK + a] = lengths_ref[(owner * blocks + query) * BLK + a]
        return carry

    lax.fori_loop(0, 2 * slots, line, 0)

    def both(slot, carry):
        pairs_ref[2 * slot] = first_ref[slot]
        pairs_ref[2 * slot + 1] = second_ref[slot]
        return carry

    lax.fori_loop(0, pairs // 2, both, 0)


def plan(places, cand_block, query_block, valid, lengths, slots):
    pairs = cand_block.shape[0]
    shapes = (pairs // 2, 2 * slots * LINE, pairs)
    return pl.pallas_call(
        functools.partial(plan_kernel, pairs, slots),
        out_shape=[jax.ShapeDtypeStruct((n,), jnp.int32) for n in shapes],
        in_specs=[pl.BlockSpec(memory_space=SMEM)] * 5,
        out_specs=[pl.BlockSpec(memory_space=SMEM)] * 3,
        scratch_shapes=[SMEM((pairs,), jnp.int32)] * 3,
    )(places, cand_block, query_block, valid, lengths)


def project_kernel(me_ref, states_ref, weight_ref, out_ref):
    out_ref[0, 0] = jnp.dot(
        states_ref[0], weight_ref[...], preferred_element_type=jnp.float32
    ).astype(out_ref.dtype)


def project(me, states, weight, shares, offset, count, dtype):
    blocks, rows, width = states.shape
    out_width = weight.shape[1]
    part = rows // shares
    return pl.pallas_call(
        project_kernel,
        out_shape=jax.ShapeDtypeStruct((count, blocks, part, out_width), dtype),
        grid_spec=pltpu.PrefetchScalarGridSpec(
            num_scalar_prefetch=1,
            grid=(count, blocks),
            in_specs=[
                pl.BlockSpec(
                    (1, part, width), lambda d, b, m: (b, lax.rem(m[0] + offset + d, shares), 0)
                ),
                pl.BlockSpec((width, out_width), lambda d, b, m: (0, 0)),
            ],
            out_specs=pl.BlockSpec((1, 1, part, out_width), lambda d, b, m: (d, b, 0, 0)),
        ),
        cost_estimate=pl.CostEstimate(
            flops=2 * count * blocks * part * width * out_width,
            bytes_accessed=2 * count * blocks * part * width,
            transcendentals=0,
        ),
    )(me, states, weight)


def unit_kernel(others, pieces, keep_ref, *refs):
    out_ref = refs[-1]
    total = keep_ref[0, 0]
    for ref in refs[:others]:
        total = total + ref[0].astype(jnp.float32)
    norm = jnp.sum(total * total, axis=-1, keepdims=True)
    unit = (total * lax.rsqrt(norm + 1e-06)).astype(jnp.bfloat16)
    if pieces is None:
        out_ref[0] = unit
    else:
        size = unit.shape[0] // pieces
        for m in range(pieces):
            out_ref[m, 0] = unit[m * size : (m + 1) * size]


def unit_rows(keep, received, owners):
    _, blocks, part, width = keep.shape
    size = part // owners
    direct = size % 16 == 0
    if direct:
        shape = (owners, blocks, size, width)
        out_spec = pl.BlockSpec((owners, 1, size, width), lambda b: (0, b, 0, 0))
    else:
        shape = (blocks, part, width)
        out_spec = pl.BlockSpec((1, part, width), lambda b: (b, 0, 0))
    out = pl.pallas_call(
        functools.partial(unit_kernel, len(received), owners if direct else None),
        out_shape=jax.ShapeDtypeStruct(shape, jnp.bfloat16),
        grid=(blocks,),
        in_specs=[pl.BlockSpec((1, 1, part, width), lambda b: (0, b, 0, 0))]
        + [pl.BlockSpec((1, part, width), lambda b: (b, 0, 0))] * len(received),
        out_specs=out_spec,
    )(keep, *received)
    if direct:
        return out
    return out.reshape(blocks, owners, size, width).transpose(1, 0, 2, 3)


def route_kernel(dests, slots, owners, asked_ref, pieces_ref, out_ref):
    def step(d, carry):
        side = d // owners
        requester = d - side * owners
        for k in range(slots):
            out_ref[d, k] = pieces_ref[asked_ref[requester, side * slots + k]]
        return carry

    lax.fori_loop(0, dests, step, 0)


def route(asked, pieces, owners, shares):
    slots = asked.shape[1] // shares
    dests = owners * shares
    return pl.pallas_call(
        functools.partial(route_kernel, dests, slots, owners),
        out_shape=jax.ShapeDtypeStruct((dests, slots) + pieces.shape[1:], jnp.bfloat16),
        in_specs=[pl.BlockSpec(memory_space=SMEM), pl.BlockSpec(memory_space=VMEM)],
        out_specs=pl.BlockSpec(memory_space=VMEM),
        compiler_params=vmem_params(48),
    )(asked, pieces)


def query_rows(parts, out_ref):
    _, _, core, side = place()
    size = out_ref.shape[1] // 32
    half = 8 * CHUNK * size
    early, early_far = parts[:2]
    pieces = [(ref, flip * half, far, flip, 0) for far, ref in ((0, early), (1, early_far)) for flip in range(2)]
    pieces += [(ref, 0, rel // 2, rel % 2, CHUNK) for rel, ref in enumerate(parts[2:])]
    for ref, begin, far, flip, first in pieces:
        base = (side ^ far) * (16 * size) + (core ^ flip) * (2 * size)
        for z in range(4):
            for x in range(2):
                target = pl.multiple_of(base + z * 4 * size + x * size, 16)
                for b in range(CHUNK):
                    row = begin + ((z * 2 + x) * CHUNK + b) * size
                    out_ref[first + b, pl.ds(target, size)] = ref[row : row + size]


def score_kernel(length, parts, table_ref, *refs):
    if parts:
        cand_ref, out_ref, totals_ref, block_ref, query_ref = refs[parts:]
        query_rows(refs[:parts], query_ref)
    else:
        query_ref, cand_ref, out_ref, totals_ref = refs
    rows = query_ref.shape[1]
    slots = cand_ref.shape[-3]
    totals_ref[...] = jnp.ones_like(totals_ref)
    upper = lax.broadcasted_iota(jnp.int32, (length // 2, COLS), 0) + length // 2
    lane = lax.broadcasted_iota(jnp.int32, (16, length), 1)

    def slot_step(k, carry):
        if parts:
            pieces, _, size, _ = cand_ref.shape
            for piece in range(pieces):
                begin = (piece // 4 * 4 + piece % 2 * 2 + piece // 2 % 2) * size
                block_ref[begin : begin + size] = cand_ref[piece, k]
        for i in range(2):
            line = (2 * k + i) * LINE
            query = table_ref[line + 1]
            for start in range(0, rows, COLS):
                sim = lax.dot_general(
                    block_ref[...] if parts else cand_ref[k],
                    query_ref[query, start : start + COLS],
                    (((1,), (1,)), ((), ())),
                    preferred_element_type=jnp.float32,
                )
                for b in range(BLK):
                    live = table_ref[line + 3 + b]
                    low = jnp.exp2(sim[b * length : b * length + length // 2] * EXP2_SCALE)
                    high = jnp.exp2(sim[b * length + length // 2 : (b + 1) * length] * EXP2_SCALE)
                    both = low + jnp.where(upper < live, high, 0.0)
                    totals_ref[2 * k + i, b : b + 1, start : start + COLS] = jnp.sum(
                        both, axis=0, keepdims=True
                    )
        return carry

    lax.fori_loop(0, slots, slot_step, 0)
    for tile in range(out_ref.shape[0]):
        score = jnp.zeros((16, length), jnp.float32)
        for i in range(tile * PACK, min((tile + 1) * PACK, 2 * slots)):
            line = i * LINE
            keep = table_ref[line + 2].astype(jnp.float32) / (SHARPNESS * length)
            for a in range(BLK):
                live = table_ref[line + 3 + BLK + a]
                logs = jnp.log(totals_ref[i, :, a * length : (a + 1) * length])
                summed = jnp.sum(jnp.where(lane < live, logs, 0.0), axis=1, keepdims=True)
                score = jnp.where(lane == i % PACK * BLK + a, summed * keep, score)
        out_ref[tile] = score


def score(table, query, cand, blocks, length):
    slots, width = cand.shape[-3], cand.shape[-1]
    rows = BLK * length
    parts = len(query) if isinstance(query, list) else 0
    count = 2 * slots * rows * rows
    scratch = [VMEM((2 * slots, 16, rows), jnp.float32)]
    if parts:
        scratch += [VMEM((rows, width), jnp.bfloat16), VMEM((blocks, rows, width), jnp.bfloat16)]
    return pl.pallas_call(
        functools.partial(score_kernel, length, parts),
        out_shape=jax.ShapeDtypeStruct((-(-2 * slots // PACK), 16, length), jnp.float32),
        in_specs=[pl.BlockSpec(memory_space=SMEM)]
        + [pl.BlockSpec(memory_space=VMEM)] * (max(parts, 1) + 1),
        out_specs=pl.BlockSpec(memory_space=VMEM),
        scratch_shapes=scratch,
        compiler_params=vmem_params(28),
        cost_estimate=pl.CostEstimate(
            flops=2 * count * width, bytes_accessed=4 * rows * width, transcendentals=count
        ),
    )(table, *(query if parts else [query]), cand)


def place_kernel(shares, count, where_ref, pairs_ref, *refs):
    parts, out_ref = refs[:-1], refs[-1]
    for d, ref in enumerate(parts):
        side = lax.rem(where_ref[1] - d + shares, shares)
        for i in range(count):
            tile = ref[i // PACK]
            if i % PACK:
                tile = pltpu.roll(tile, tile.shape[1] - i % PACK * BLK, 1)
            out_ref[pairs_ref[side * count + i]] = tile[:BLK, :BLK]


def place_scores(where, pair_of, parts, pairs):
    shares = len(parts)
    return pl.pallas_call(
        functools.partial(place_kernel, shares, pairs // shares),
        out_shape=jax.ShapeDtypeStruct((pairs, BLK, BLK), jnp.float32),
        in_specs=[pl.BlockSpec(memory_space=SMEM)] * 2 + [pl.BlockSpec(memory_space=VMEM)] * shares,
        out_specs=pl.BlockSpec(memory_space=VMEM),
        compiler_params=vmem_params(4),
    )(where, pair_of, *parts)


def local_general(states, proj_weight, lengths, query_block, cand_block, pair_valid):
    shares = lax.axis_size("narrow")
    owners = lax.axis_size("wide")
    side = lax.axis_index("narrow").astype(jnp.int32)
    owner = lax.axis_index("wide").astype(jnp.int32)
    paras, length, width_part = states.shape
    width = proj_weight.shape[1]
    blocks = paras // BLK
    rows = BLK * length
    flat = states.reshape(blocks, rows, width_part)
    me = side.reshape(1)

    def shift(d):
        return [(i, (i + d) % shares) for i in range(shares)]

    slots = cand_block.shape[0] // 2 // shares
    places = jnp.stack([owner, side, jnp.int32(blocks)])
    sel, table, pair_of = plan(places, cand_block, query_block, pair_valid, lengths, slots)
    sent = project(me, flat, proj_weight, shares, 1, shares - 1, jnp.bfloat16)
    received = [lax.ppermute(sent[d - 1], "narrow", shift(d)) for d in range(1, shares)]
    asked = lax.all_to_all(
        jnp.broadcast_to(sel[None], (owners,) + sel.shape), "wide", 0, 0, tiled=True
    )
    kept = project(me, flat, proj_weight, shares, 0, 1, jnp.float32)
    mine = unit_rows(kept, received, owners)
    spread = lax.all_to_all(mine, "wide", 0, 0, tiled=True)
    size = mine.shape[2]
    by_side = [mine] + [lax.ppermute(mine, "narrow", shift(d)) for d in range(1, shares)]
    order = jnp.stack(by_side)
    query = jnp.stack(
        [lax.dynamic_index_in_dim(order, lax.rem(side - s + shares, shares), 0, False) for s in range(shares)]
    )
    query = query.transpose(2, 0, 1, 3, 4).reshape(blocks, rows, width)
    outgoing = route(asked, spread.reshape(owners * blocks, size, width), owners, shares)
    incoming = lax.all_to_all(outgoing, ("narrow", "wide"), 0, 0, tiled=True)
    cand = incoming.transpose(1, 0, 2, 3).reshape(-1, rows, width)
    part = score(table, query, cand, blocks, length)
    parts = [part] + [lax.ppermute(part, "narrow", shift(d)) for d in range(1, shares)]
    return place_scores(places, pair_of, parts, cand_block.shape[0])


def place():
    owner = lax.axis_index("wide")
    return owner // 4, owner // 2 % 2, owner % 2, lax.axis_index("narrow")


def split_kernel(first, over, states_ref, weight_ref, *refs):
    *outs, rows_ref, sems = refs
    _, _, core, side = place()
    blocks, part, _ = rows_ref.shape
    size = part // 16
    start = pl.multiple_of((side ^ over) * part, part)

    def load(b):
        return pltpu.make_async_copy(
            states_ref.at[first + b, pl.ds(start, part)], rows_ref.at[b], sems.at[b]
        )

    for b in range(blocks):
        load(b).start()
    for b in range(blocks):
        load(b).wait()
        for z in range(4):
            for flip in range(2):
                source = pl.multiple_of((core ^ flip) * (2 * size) + z * 4 * size, 16)
                both = jnp.dot(
                    rows_ref[b, pl.ds(source, 2 * size)],
                    weight_ref[...],
                    preferred_element_type=jnp.float32,
                ).astype(jnp.bfloat16)
                for x in range(2):
                    target = ((z * 2 + x) * blocks + b) * size
                    outs[flip][target : target + size] = both[x * size : (x + 1) * size]


def split(over, states, weight, first):
    _, rows, width = states.shape
    out_width = weight.shape[1]
    part = rows // 2
    out_rows = 8 * CHUNK * (part // 16)
    return pl.pallas_call(
        functools.partial(split_kernel, first, over),
        out_shape=(jax.ShapeDtypeStruct((out_rows, out_width), jnp.bfloat16),) * 2,
        in_specs=[pl.BlockSpec(memory_space=pltpu.HBM), pl.BlockSpec(memory_space=VMEM)],
        out_specs=[pl.BlockSpec(memory_space=VMEM)] * 2,
        scratch_shapes=[
            VMEM((CHUNK, part, width), jnp.bfloat16),
            pltpu.SemaphoreType.DMA((CHUNK,)),
        ],
        compiler_params=vmem_params(50),
        cost_estimate=pl.CostEstimate(
            flops=2 * CHUNK * part * width * out_width,
            bytes_accessed=2 * CHUNK * part * width,
            transcendentals=0,
        ),
    )(states, weight)


def unit_sum(one, two):
    total = one.astype(jnp.float32) + two.astype(jnp.float32)
    norm = jnp.sum(total * total, axis=-1, keepdims=True)
    return (total * lax.rsqrt(norm + 1e-06)).astype(jnp.bfloat16)


def early_unit_kernel(size, sel_ref, y_ref, y_flip_ref, own_ref, own_flip_ref, send_ref, query_ref):
    _, _, core, _ = place()
    span = CHUNK * size
    rows = span + 16
    shape = (16, own_ref.shape[1])
    lane = lax.broadcasted_iota(jnp.int32, shape, 1)
    asked = jnp.zeros(shape, jnp.int32)
    for k in range(sel_ref.shape[0]):
        asked = jnp.where(lane == k, sel_ref[k], asked)
    asked = asked.astype(jnp.float32).astype(jnp.bfloat16)
    for flip, (one_ref, two_ref) in enumerate(((own_ref, y_ref), (own_flip_ref, y_flip_ref))):
        for chip in range(8):
            source = chip * span
            unit = unit_sum(one_ref[source : source + span], two_ref[source : source + span])
            begin = (chip * 2 + (core ^ flip)) * rows
            send_ref[pl.ds(pl.multiple_of(begin, 16), span)] = unit
            send_ref[pl.ds(pl.multiple_of(begin + span, 16), 16)] = asked
            query_ref[8 * span * flip + source : 8 * span * flip + source + span] = unit


def early_unit(sel, y, y_flip, own, own_flip, size):
    rows, width = own.shape
    return pl.pallas_call(
        functools.partial(early_unit_kernel, size),
        out_shape=(
            jax.ShapeDtypeStruct((16 * (CHUNK * size + 16), width), jnp.bfloat16),
            jax.ShapeDtypeStruct((2 * rows, width), jnp.bfloat16),
        ),
        in_specs=[pl.BlockSpec(memory_space=SMEM)] + [pl.BlockSpec(memory_space=VMEM)] * 4,
        out_specs=[pl.BlockSpec(memory_space=VMEM)] * 2,
        compiler_params=vmem_params(12),
    )(sel, y, y_flip, own, own_flip)


def late_unit_kernel(size, y_ref, cy_ref, own_ref, c_ref, *outs):
    z, x, _, _ = place()
    sends, query = outs[:8], outs[8:]
    span = CHUNK * size
    for rel, send_ref in zip(SPREAD, sends):
        source = pl.multiple_of(((z ^ (rel // 2)) * 2 + (x ^ (rel % 2))) * span, 16)
        for flip, (one_ref, two_ref) in enumerate(((own_ref, y_ref), (c_ref, cy_ref))):
            unit = unit_sum(one_ref[pl.ds(source, span)], two_ref[pl.ds(source, span)])
            send_ref[flip * span : (flip + 1) * span] = unit
            query[flip][pl.ds(source, span)] = unit


def late_unit(y, cy, own, c, size):
    rows, width = own.shape
    send = jax.ShapeDtypeStruct((2 * CHUNK * size, width), jnp.bfloat16)
    query = jax.ShapeDtypeStruct((rows, width), jnp.bfloat16)
    return pl.pallas_call(
        functools.partial(late_unit_kernel, size),
        out_shape=(send,) * 8 + (query,) * 2,
        in_specs=[pl.BlockSpec(memory_space=VMEM)] * 4,
        out_specs=[pl.BlockSpec(memory_space=VMEM)] * 10,
        compiler_params=vmem_params(12),
    )(y, cy, own, c)


def cube_route_kernel(size, slots, early_ref, *refs):
    late, out_ref, pieces_ref, rows_ref, asked_ref, sem = refs[:8], *refs[8:]
    z, x, core, _ = place()
    blocks = pieces_ref.shape[0] // 16
    span = CHUNK * size
    for owner in range(16):
        row = owner * (span + 16) + span
        rows_ref[owner : owner + 1] = early_ref[row : row + 16].astype(jnp.float32)[:1].astype(jnp.int32)
    copy = pltpu.make_async_copy(rows_ref, asked_ref, sem)
    copy.start()
    for owner in range(16):
        for b in range(CHUNK):
            row = owner * (span + 16) + b * size
            pieces_ref[owner * blocks + b] = early_ref[row : row + size]
    for rel, ref in zip(SPREAD, late):
        chip = (z ^ (rel // 2)) * 2 + (x ^ (rel % 2))
        for flip in range(2):
            owner = chip * 2 + (core ^ flip)
            for b in range(CHUNK):
                row = flip * span + b * size
                pieces_ref[owner * blocks + CHUNK + b] = ref[row : row + size]
    copy.wait()

    def step(d, carry):
        side = d // 16
        for k in range(slots):
            out_ref[d, k] = pieces_ref[asked_ref[d - side * 16, side * slots + k]]
        return carry

    lax.fori_loop(0, 32, step, 0, unroll=4)


def cube_route(spread, size, slots, blocks):
    width = spread[0].shape[1]
    return pl.pallas_call(
        functools.partial(cube_route_kernel, size, slots),
        out_shape=jax.ShapeDtypeStruct((32, slots, size, width), jnp.bfloat16),
        in_specs=[pl.BlockSpec(memory_space=VMEM)] * len(spread),
        out_specs=pl.BlockSpec(memory_space=VMEM),
        scratch_shapes=[
            VMEM((16 * blocks, size, width), jnp.bfloat16),
            VMEM((16, width), jnp.int32),
            SMEM((16, width), jnp.int32),
            pltpu.SemaphoreType.DMA,
        ],
        compiler_params=vmem_params(16),
    )(*spread)


def local_cube(states, proj_weight, lengths, query_block, cand_block, pair_valid):
    side = lax.axis_index("narrow").astype(jnp.int32)
    owner = lax.axis_index("wide").astype(jnp.int32)
    paras, length, width_part = states.shape
    width = proj_weight.shape[1]
    blocks = paras // BLK
    rows = BLK * length
    size = rows // 32
    slots = cand_block.shape[0] // 4
    flat = states.reshape(blocks, rows, width_part)

    def near(array, rel):
        flip = rel % 2 * 2 + rel // 2
        return lax.ppermute(array, ("wide", "narrow"), [(i, i ^ flip) for i in range(32)])

    def along(array, rel):
        flip = rel * 2
        return lax.ppermute(array, "wide", [(i, i ^ flip) for i in range(16)])

    places = jnp.stack([owner, side, jnp.int32(blocks)])
    sel, table, pair_of = plan(places, cand_block, query_block, pair_valid, lengths, slots)
    far = split(1, flat, proj_weight, 0)
    weight, *far = lax.optimization_barrier((proj_weight, *far))
    crossed = [near(part, 2) for part in far]
    far = split(1, flat, weight, CHUNK)
    weight, sel, *far = lax.optimization_barrier((weight, sel, *far))
    early = split(0, flat, weight, 0)
    own, aside = split(0, flat, weight, CHUNK)
    *early, own, aside = lax.optimization_barrier((*early, own, aside))
    y, cy, c = near(far[0], 2), near(far[1], 3), near(aside, 1)
    *crossed, y, cy, c = lax.optimization_barrier((*crossed, y, cy, c))
    send, early_query = early_unit(sel, *crossed, *early, size)
    early_spread = lax.all_to_all(send, "wide", 0, 0, tiled=True)
    *sends, own, other = late_unit(y, cy, own, c, size)
    early_query, sends[0] = lax.optimization_barrier((early_query, sends[0]))
    early_far = near(early_query, 2)
    spread = [along(send, rel) if rel else send for rel, send in zip(SPREAD, sends)]
    outgoing = cube_route([early_spread, *spread], size, slots, blocks)
    outgoing, own, other, early_far = lax.optimization_barrier((outgoing, own, other, early_far))
    incoming = lax.all_to_all(outgoing, ("narrow", "wide"), 0, 0, tiled=True)
    other = near(other, 1)
    query = [early_query, early_far, own, other, near(own, 2), near(other, 2)]
    part = score(table, query, incoming, blocks, length)
    parts = [part, lax.ppermute(part, "narrow", [(0, 1), (1, 0)])]
    return place_scores(places, pair_of, parts, cand_block.shape[0])


def solution(mesh):
    in_specs = (P("wide", None, "narrow"), P("narrow", None), P(), P("wide"), P("wide"), P("wide"))
    out_specs = P("wide", None, None)
    cube = mesh.shape["wide"] == 16 and mesh.shape["narrow"] == 2
    local = local_cube if cube else local_general
    return jax.shard_map(local, mesh=mesh, in_specs=in_specs, out_specs=out_specs, check_vma=False)
```

```python
import functools
import math

import jax
import jax.numpy as jnp
from jax import lax
from jax.experimental import pallas as pl
from jax.experimental.pallas import tpu as pltpu
from jax.sharding import PartitionSpec as P

BLK = 12
SHARPNESS = 20.0
EXP2_SCALE = SHARPNESS * math.log2(math.e)
COLS = 512
CHUNK = 4
LINE = 32
PACK = 6
SPREAD = (0, 1, 2, 4, 3, 6, 5, 7)
SMEM = pltpu.SMEM
VMEM = pltpu.VMEM


def vmem_params(mib):
    return pltpu.CompilerParams(vmem_limit_bytes=mib * 2**20)


def plan_kernel(pairs, slots, places_ref, cand_ref, query_block_ref, valid_ref, lengths_ref, sel_ref, table_ref, pairs_ref, *scratch):
    first_ref, second_ref, slot_ref = scratch
    owner, side, blocks = places_ref[0], places_ref[1], places_ref[2]

    def step(k, count):
        block = cand_ref[k]
        found = lax.fori_loop(
            0, k, lambda e, f: jnp.where(cand_ref[e] == block, slot_ref[e], f), jnp.int32(-1)
        )
        new = found < 0
        slot = jnp.minimum(jnp.where(new, count, found), pairs // 2 - 1)
        slot_ref[k] = slot

        @pl.when(new)
        def _():
            sel_ref[slot] = block
            first_ref[slot] = k

        second_ref[slot] = k
        return count + new.astype(jnp.int32)

    lax.fori_loop(0, pairs, step, jnp.int32(0))

    def line(i, carry):
        k = i // 2
        slot = side * slots + k
        pair = jnp.where(i - 2 * k == 0, first_ref[slot], second_ref[slot])
        query = query_block_ref[pair]
        table_ref[i * LINE + 1] = query
        table_ref[i * LINE + 2] = valid_ref[pair]
        for a in range(BLK):
            table_ref[i * LINE + 3 + a] = lengths_ref[sel_ref[slot] * BLK + a]
            table_ref[i * LINE + 3 + BLK + a] = lengths_ref[(owner * blocks + query) * BLK + a]
        return carry

    lax.fori_loop(0, 2 * slots, line, 0)

    def both(slot, carry):
        pairs_ref[2 * slot] = first_ref[slot]
        pairs_ref[2 * slot + 1] = second_ref[slot]
        return carry

    lax.fori_loop(0, pairs // 2, both, 0)


def plan(places, cand_block, query_block, valid, lengths, slots):
    pairs = cand_block.shape[0]
    shapes = (pairs // 2, 2 * slots * LINE, pairs)
    return pl.pallas_call(
        functools.partial(plan_kernel, pairs, slots),
        out_shape=[jax.ShapeDtypeStruct((n,), jnp.int32) for n in shapes],
        in_specs=[pl.BlockSpec(memory_space=SMEM)] * 5,
        out_specs=[pl.BlockSpec(memory_space=SMEM)] * 3,
        scratch_shapes=[SMEM((pairs,), jnp.int32)] * 3,
    )(places, cand_block, query_block, valid, lengths)


def project_kernel(me_ref, states_ref, weight_ref, out_ref):
    out_ref[0, 0] = jnp.dot(
        states_ref[0], weight_ref[...], preferred_element_type=jnp.float32
    ).astype(out_ref.dtype)


def project(me, states, weight, shares, offset, count, dtype):
    blocks, rows, width = states.shape
    out_width = weight.shape[1]
    part = rows // shares
    return pl.pallas_call(
        project_kernel,
        out_shape=jax.ShapeDtypeStruct((count, blocks, part, out_width), dtype),
        grid_spec=pltpu.PrefetchScalarGridSpec(
            num_scalar_prefetch=1,
            grid=(count, blocks),
            in_specs=[
                pl.BlockSpec(
                    (1, part, width), lambda d, b, m: (b, lax.rem(m[0] + offset + d, shares), 0)
                ),
                pl.BlockSpec((width, out_width), lambda d, b, m: (0, 0)),
            ],
            out_specs=pl.BlockSpec((1, 1, part, out_width), lambda d, b, m: (d, b, 0, 0)),
        ),
        cost_estimate=pl.CostEstimate(
            flops=2 * count * blocks * part * width * out_width,
            bytes_accessed=2 * count * blocks * part * width,
            transcendentals=0,
        ),
    )(me, states, weight)


def unit_kernel(others, pieces, keep_ref, *refs):
    out_ref = refs[-1]
    total = keep_ref[0, 0]
    for ref in refs[:others]:
        total = total + ref[0].astype(jnp.float32)
    norm = jnp.sum(total * total, axis=-1, keepdims=True)
    unit = (total * lax.rsqrt(norm + 1e-06)).astype(jnp.bfloat16)
    if pieces is None:
        out_ref[0] = unit
    else:
        size = unit.shape[0] // pieces
        for m in range(pieces):
            out_ref[m, 0] = unit[m * size : (m + 1) * size]


def unit_rows(keep, received, owners):
    _, blocks, part, width = keep.shape
    size = part // owners
    direct = size % 16 == 0
    if direct:
        shape = (owners, blocks, size, width)
        out_spec = pl.BlockSpec((owners, 1, size, width), lambda b: (0, b, 0, 0))
    else:
        shape = (blocks, part, width)
        out_spec = pl.BlockSpec((1, part, width), lambda b: (b, 0, 0))
    out = pl.pallas_call(
        functools.partial(unit_kernel, len(received), owners if direct else None),
        out_shape=jax.ShapeDtypeStruct(shape, jnp.bfloat16),
        grid=(blocks,),
        in_specs=[pl.BlockSpec((1, 1, part, width), lambda b: (0, b, 0, 0))]
        + [pl.BlockSpec((1, part, width), lambda b: (b, 0, 0))] * len(received),
        out_specs=out_spec,
    )(keep, *received)
    if direct:
        return out
    return out.reshape(blocks, owners, size, width).transpose(1, 0, 2, 3)


def route_kernel(dests, slots, owners, asked_ref, pieces_ref, out_ref):
    def step(d, carry):
        side = d // owners
        requester = d - side * owners
        for k in range(slots):
            out_ref[d, k] = pieces_ref[asked_ref[requester, side * slots + k]]
        return carry

    lax.fori_loop(0, dests, step, 0)


def route(asked, pieces, owners, shares):
    slots = asked.shape[1] // shares
    dests = owners * shares
    return pl.pallas_call(
        functools.partial(route_kernel, dests, slots, owners),
        out_shape=jax.ShapeDtypeStruct((dests, slots) + pieces.shape[1:], jnp.bfloat16),
        in_specs=[pl.BlockSpec(memory_space=SMEM), pl.BlockSpec(memory_space=VMEM)],
        out_specs=pl.BlockSpec(memory_space=VMEM),
        compiler_params=vmem_params(48),
    )(asked, pieces)


def query_rows(parts, out_ref):
    _, _, core, side = place()
    size = out_ref.shape[1] // 32
    blocks = out_ref.shape[0]
    for rel, ref in enumerate(parts):
        base = (side ^ (rel // 2)) * (16 * size) + (core ^ (rel % 2)) * (2 * size)
        for z in range(4):
            for x in range(2):
                target = pl.multiple_of(base + z * 4 * size + x * size, 16)
                for b in range(blocks):
                    begin = ((z * 2 + x) * blocks + b) * size
                    out_ref[b, pl.ds(target, size)] = ref[begin : begin + size]


def score_kernel(length, parts, table_ref, *refs):
    if parts:
        cand_ref, out_ref, totals_ref, block_ref, query_ref = refs[parts:]
        query_rows(refs[:parts], query_ref)
    else:
        query_ref, cand_ref, out_ref, totals_ref = refs
    rows = query_ref.shape[1]
    slots = cand_ref.shape[-3]
    totals_ref[...] = jnp.ones_like(totals_ref)
    upper = lax.broadcasted_iota(jnp.int32, (length // 2, COLS), 0) + length // 2
    lane = lax.broadcasted_iota(jnp.int32, (16, length), 1)

    def slot_step(k, carry):
        if parts:
            pieces, _, size, _ = cand_ref.shape
            for piece in range(pieces):
                begin = (piece // 4 * 4 + piece % 2 * 2 + piece // 2 % 2) * size
                block_ref[begin : begin + size] = cand_ref[piece, k]
        for i in range(2):
            line = (2 * k + i) * LINE
            query = table_ref[line + 1]
            for start in range(0, rows, COLS):
                sim = lax.dot_general(
                    block_ref[...] if parts else cand_ref[k],
                    query_ref[query, start : start + COLS],
                    (((1,), (1,)), ((), ())),
                    preferred_element_type=jnp.float32,
                )
                for b in range(BLK):
                    live = table_ref[line + 3 + b]
                    low = jnp.exp2(sim[b * length : b * length + length // 2] * EXP2_SCALE)
                    high = jnp.exp2(sim[b * length + length // 2 : (b + 1) * length] * EXP2_SCALE)
                    both = low + jnp.where(upper < live, high, 0.0)
                    totals_ref[2 * k + i, b : b + 1, start : start + COLS] = jnp.sum(
                        both, axis=0, keepdims=True
                    )
        return carry

    lax.fori_loop(0, slots, slot_step, 0)
    for tile in range(out_ref.shape[0]):
        score = jnp.zeros((16, length), jnp.float32)
        for i in range(tile * PACK, min((tile + 1) * PACK, 2 * slots)):
            line = i * LINE
            keep = table_ref[line + 2].astype(jnp.float32) / (SHARPNESS * length)
            for a in range(BLK):
                live = table_ref[line + 3 + BLK + a]
                logs = jnp.log(totals_ref[i, :, a * length : (a + 1) * length])
                summed = jnp.sum(jnp.where(lane < live, logs, 0.0), axis=1, keepdims=True)
                score = jnp.where(lane == i % PACK * BLK + a, summed * keep, score)
        out_ref[tile] = score


def score(table, query, cand, blocks, length):
    slots, width = cand.shape[-3], cand.shape[-1]
    rows = BLK * length
    parts = len(query) if isinstance(query, list) else 0
    count = 2 * slots * rows * rows
    scratch = [VMEM((2 * slots, 16, rows), jnp.float32)]
    if parts:
        scratch += [VMEM((rows, width), jnp.bfloat16), VMEM((blocks, rows, width), jnp.bfloat16)]
    return pl.pallas_call(
        functools.partial(score_kernel, length, parts),
        out_shape=jax.ShapeDtypeStruct((-(-2 * slots // PACK), 16, length), jnp.float32),
        in_specs=[pl.BlockSpec(memory_space=SMEM)]
        + [pl.BlockSpec(memory_space=VMEM)] * (max(parts, 1) + 1),
        out_specs=pl.BlockSpec(memory_space=VMEM),
        scratch_shapes=scratch,
        compiler_params=vmem_params(28),
        cost_estimate=pl.CostEstimate(
            flops=2 * count * width, bytes_accessed=4 * rows * width, transcendentals=count
        ),
    )(table, *(query if parts else [query]), cand)


def place_kernel(shares, count, where_ref, pairs_ref, *refs):
    parts, out_ref = refs[:-1], refs[-1]
    for d, ref in enumerate(parts):
        side = lax.rem(where_ref[1] - d + shares, shares)
        for i in range(count):
            tile = ref[i // PACK]
            if i % PACK:
                tile = pltpu.roll(tile, tile.shape[1] - i % PACK * BLK, 1)
            out_ref[pairs_ref[side * count + i]] = tile[:BLK, :BLK]


def place_scores(where, pair_of, parts, pairs):
    shares = len(parts)
    return pl.pallas_call(
        functools.partial(place_kernel, shares, pairs // shares),
        out_shape=jax.ShapeDtypeStruct((pairs, BLK, BLK), jnp.float32),
        in_specs=[pl.BlockSpec(memory_space=SMEM)] * 2 + [pl.BlockSpec(memory_space=VMEM)] * shares,
        out_specs=pl.BlockSpec(memory_space=VMEM),
        compiler_params=vmem_params(4),
    )(where, pair_of, *parts)


def local_general(states, proj_weight, lengths, query_block, cand_block, pair_valid):
    shares = lax.axis_size("narrow")
    owners = lax.axis_size("wide")
    side = lax.axis_index("narrow").astype(jnp.int32)
    owner = lax.axis_index("wide").astype(jnp.int32)
    paras, length, width_part = states.shape
    width = proj_weight.shape[1]
    blocks = paras // BLK
    rows = BLK * length
    flat = states.reshape(blocks, rows, width_part)
    me = side.reshape(1)

    def shift(d):
        return [(i, (i + d) % shares) for i in range(shares)]

    slots = cand_block.shape[0] // 2 // shares
    places = jnp.stack([owner, side, jnp.int32(blocks)])
    sel, table, pair_of = plan(places, cand_block, query_block, pair_valid, lengths, slots)
    sent = project(me, flat, proj_weight, shares, 1, shares - 1, jnp.bfloat16)
    received = [lax.ppermute(sent[d - 1], "narrow", shift(d)) for d in range(1, shares)]
    asked = lax.all_to_all(
        jnp.broadcast_to(sel[None], (owners,) + sel.shape), "wide", 0, 0, tiled=True
    )
    kept = project(me, flat, proj_weight, shares, 0, 1, jnp.float32)
    mine = unit_rows(kept, received, owners)
    spread = lax.all_to_all(mine, "wide", 0, 0, tiled=True)
    size = mine.shape[2]
    by_side = [mine] + [lax.ppermute(mine, "narrow", shift(d)) for d in range(1, shares)]
    order = jnp.stack(by_side)
    query = jnp.stack(
        [lax.dynamic_index_in_dim(order, lax.rem(side - s + shares, shares), 0, False) for s in range(shares)]
    )
    query = query.transpose(2, 0, 1, 3, 4).reshape(blocks, rows, width)
    outgoing = route(asked, spread.reshape(owners * blocks, size, width), owners, shares)
    incoming = lax.all_to_all(outgoing, ("narrow", "wide"), 0, 0, tiled=True)
    cand = incoming.transpose(1, 0, 2, 3).reshape(-1, rows, width)
    part = score(table, query, cand, blocks, length)
    parts = [part] + [lax.ppermute(part, "narrow", shift(d)) for d in range(1, shares)]
    return place_scores(places, pair_of, parts, cand_block.shape[0])


def place():
    owner = lax.axis_index("wide")
    return owner // 4, owner // 2 % 2, owner % 2, lax.axis_index("narrow")


def split_kernel(first, over, states_ref, weight_ref, *refs):
    *outs, rows_ref, sems = refs
    _, _, core, side = place()
    blocks, part, _ = rows_ref.shape
    size = part // 16
    start = pl.multiple_of((side ^ over) * part, part)

    def load(b):
        return pltpu.make_async_copy(
            states_ref.at[first + b, pl.ds(start, part)], rows_ref.at[b], sems.at[b]
        )

    for b in range(blocks):
        load(b).start()
    for b in range(blocks):
        load(b).wait()
        for z in range(4):
            for flip in range(2):
                source = pl.multiple_of((core ^ flip) * (2 * size) + z * 4 * size, 16)
                both = jnp.dot(
                    rows_ref[b, pl.ds(source, 2 * size)],
                    weight_ref[...],
                    preferred_element_type=jnp.float32,
                ).astype(jnp.bfloat16)
                for x in range(2):
                    target = ((z * 2 + x) * blocks + b) * size
                    outs[flip][target : target + size] = both[x * size : (x + 1) * size]


def split(over, states, weight, first):
    _, rows, width = states.shape
    out_width = weight.shape[1]
    part = rows // 2
    out_rows = 8 * CHUNK * (part // 16)
    return pl.pallas_call(
        functools.partial(split_kernel, first, over),
        out_shape=(jax.ShapeDtypeStruct((out_rows, out_width), jnp.bfloat16),) * 2,
        in_specs=[pl.BlockSpec(memory_space=pltpu.HBM), pl.BlockSpec(memory_space=VMEM)],
        out_specs=[pl.BlockSpec(memory_space=VMEM)] * 2,
        scratch_shapes=[
            VMEM((CHUNK, part, width), jnp.bfloat16),
            pltpu.SemaphoreType.DMA((CHUNK,)),
        ],
        compiler_params=vmem_params(50),
        cost_estimate=pl.CostEstimate(
            flops=2 * CHUNK * part * width * out_width,
            bytes_accessed=2 * CHUNK * part * width,
            transcendentals=0,
        ),
    )(states, weight)


def gather_unit_kernel(size, sel_ref, sel_near_ref, y_ref, cy_ref, own_ref, c_ref, *outs):
    z, x, _, _ = place()
    sends, query = outs[:8], outs[8:]
    span = CHUNK * size
    shape = (16, own_ref.shape[1])
    row, lane = (lax.broadcasted_iota(jnp.int32, shape, axis) for axis in range(2))
    asked = jnp.zeros(shape, jnp.int32)
    for flip, ids_ref in enumerate((sel_ref, sel_near_ref)):
        for k in range(ids_ref.shape[0]):
            asked = jnp.where((row == flip) & (lane == k), ids_ref[k], asked)
    asked = asked.astype(jnp.float32).astype(jnp.bfloat16)
    for rel, send_ref in zip(SPREAD, sends):
        source = pl.multiple_of(((z ^ (rel // 2)) * 2 + (x ^ (rel % 2))) * span, 16)
        for flip, (one_ref, two_ref) in enumerate(((own_ref, y_ref), (c_ref, cy_ref))):
            total = one_ref[pl.ds(source, span)].astype(jnp.float32)
            total = total + two_ref[pl.ds(source, span)].astype(jnp.float32)
            norm = jnp.sum(total * total, axis=-1, keepdims=True)
            unit = (total * lax.rsqrt(norm + 1e-06)).astype(jnp.bfloat16)
            send_ref[flip * span : (flip + 1) * span] = unit
            query[flip][pl.ds(source, span)] = unit
        send_ref[2 * span :] = asked


def gather_unit(sel, sel_near, y, cy, own, c, size):
    rows, width = own.shape
    send = jax.ShapeDtypeStruct((2 * CHUNK * size + 16, width), jnp.bfloat16)
    query = jax.ShapeDtypeStruct((rows, width), jnp.bfloat16)
    return pl.pallas_call(
        functools.partial(gather_unit_kernel, size),
        out_shape=(send,) * 8 + (query,) * 2,
        in_specs=[pl.BlockSpec(memory_space=SMEM)] * 2 + [pl.BlockSpec(memory_space=VMEM)] * 4,
        out_specs=[pl.BlockSpec(memory_space=VMEM)] * 10,
        compiler_params=vmem_params(12),
    )(sel, sel_near, y, cy, own, c)


def cube_route_kernel(size, slots, *refs):
    spread, out_ref, pieces_ref, rows_ref, asked_ref, sem = refs[:8], *refs[8:]
    z, x, core, _ = place()
    blocks = pieces_ref.shape[0] // 16
    span = CHUNK * size
    chips = [(z ^ (rel // 2)) * 2 + (x ^ (rel % 2)) for rel in SPREAD]
    for ref, chip in zip(spread, chips):
        ids = ref[2 * span :].astype(jnp.float32)
        for flip in range(2):
            rows_ref[pl.ds(chip * 2 + (core ^ flip), 1)] = ids[flip : flip + 1].astype(jnp.int32)
    copy = pltpu.make_async_copy(rows_ref, asked_ref, sem)
    copy.start()
    for ref, chip in zip(spread, chips):
        for flip in range(2):
            owner = chip * 2 + (core ^ flip)
            for b in range(blocks):
                row = flip * span + b * size
                pieces_ref[owner * blocks + b] = ref[row : row + size]
    copy.wait()

    def step(d, carry):
        side = d // 16
        for k in range(slots):
            out_ref[d, k] = pieces_ref[asked_ref[d - side * 16, side * slots + k]]
        return carry

    lax.fori_loop(0, 32, step, 0, unroll=4)


def cube_route(spread, size, slots, blocks):
    width = spread[0].shape[1]
    return pl.pallas_call(
        functools.partial(cube_route_kernel, size, slots),
        out_shape=jax.ShapeDtypeStruct((32, slots, size, width), jnp.bfloat16),
        in_specs=[pl.BlockSpec(memory_space=VMEM)] * len(spread),
        out_specs=pl.BlockSpec(memory_space=VMEM),
        scratch_shapes=[
            VMEM((16 * blocks, size, width), jnp.bfloat16),
            VMEM((16, width), jnp.int32),
            SMEM((16, width), jnp.int32),
            pltpu.SemaphoreType.DMA,
        ],
        compiler_params=vmem_params(16),
    )(*spread)


def local_cube(states, proj_weight, lengths, query_block, cand_block, pair_valid):
    side = lax.axis_index("narrow").astype(jnp.int32)
    owner = lax.axis_index("wide").astype(jnp.int32)
    paras, length, width_part = states.shape
    width = proj_weight.shape[1]
    blocks = paras // BLK
    rows = BLK * length
    size = rows // 32
    slots = cand_block.shape[0] // 4
    flat = states.reshape(blocks, rows, width_part)

    def near(array, rel):
        flip = rel % 2 * 2 + rel // 2
        return lax.ppermute(array, ("wide", "narrow"), [(i, i ^ flip) for i in range(32)])

    def along(array, rel):
        flip = rel * 2
        return lax.ppermute(array, "wide", [(i, i ^ flip) for i in range(16)])

    places = jnp.stack([owner, side, jnp.int32(blocks)])
    sel, table, pair_of = plan(places, cand_block, query_block, pair_valid, lengths, slots)
    sel_near = near(sel, 1)
    far = split(1, flat, proj_weight, 0)
    weight, *far = lax.optimization_barrier((proj_weight, *far))
    y, cy = near(far[0], 2), near(far[1], 3)
    own, aside = split(0, flat, weight, 0)
    c = near(aside, 1)
    *sends, own, other = gather_unit(sel, sel_near, y, cy, own, c, size)
    other = near(other, 1)
    sends[4], other = lax.optimization_barrier((sends[4], other))
    spread = [along(send, rel) if rel else send for rel, send in zip(SPREAD, sends)]
    own_y = near(own, 2)
    outgoing = cube_route(spread, size, slots, blocks)
    outgoing, own_y, other = lax.optimization_barrier((outgoing, own_y, other))
    incoming = lax.all_to_all(outgoing, ("narrow", "wide"), 0, 0, tiled=True)
    query = [own, other, own_y, near(other, 2)]
    part = score(table, query, incoming, blocks, length)
    parts = [part, lax.ppermute(part, "narrow", [(0, 1), (1, 0)])]
    return place_scores(places, pair_of, parts, cand_block.shape[0])


def solution(mesh):
    in_specs = (P("wide", None, "narrow"), P("narrow", None), P(), P("wide"), P("wide"), P("wide"))
    out_specs = P("wide", None, None)
    cube = mesh.shape["wide"] == 16 and mesh.shape["narrow"] == 2
    local = local_cube if cube else local_general
    return jax.shard_map(local, mesh=mesh, in_specs=in_specs, out_specs=out_specs, check_vma=False)
```

```python
import functools
import math

import jax
import jax.numpy as jnp
from jax import lax
from jax.experimental import pallas as pl
from jax.experimental.pallas import tpu as pltpu
from jax.sharding import PartitionSpec as P

BLK = 12
SHARPNESS = 20.0
EXP2_SCALE = SHARPNESS * math.log2(math.e)
COLS = 512
CHUNK = 4
LINE = 32
PACK = 6
SPREAD = (0, 1, 2, 4, 3, 6, 5, 7)
SMEM = pltpu.SMEM
VMEM = pltpu.VMEM


def vmem_params(mib):
    return pltpu.CompilerParams(vmem_limit_bytes=mib * 2**20)


def plan_kernel(pairs, slots, places_ref, cand_ref, query_block_ref, valid_ref, lengths_ref, sel_ref, table_ref, pairs_ref, *scratch):
    first_ref, second_ref, slot_ref = scratch
    owner, side, blocks = places_ref[0], places_ref[1], places_ref[2]

    def step(k, count):
        block = cand_ref[k]
        found = lax.fori_loop(
            0, k, lambda e, f: jnp.where(cand_ref[e] == block, slot_ref[e], f), jnp.int32(-1)
        )
        new = found < 0
        slot = jnp.minimum(jnp.where(new, count, found), pairs // 2 - 1)
        slot_ref[k] = slot

        @pl.when(new)
        def _():
            sel_ref[slot] = block
            first_ref[slot] = k

        second_ref[slot] = k
        return count + new.astype(jnp.int32)

    lax.fori_loop(0, pairs, step, jnp.int32(0))

    def line(i, carry):
        k = i // 2
        slot = side * slots + k
        pair = jnp.where(i - 2 * k == 0, first_ref[slot], second_ref[slot])
        query = query_block_ref[pair]
        table_ref[i * LINE + 1] = query
        table_ref[i * LINE + 2] = valid_ref[pair]
        for a in range(BLK):
            table_ref[i * LINE + 3 + a] = lengths_ref[sel_ref[slot] * BLK + a]
            table_ref[i * LINE + 3 + BLK + a] = lengths_ref[(owner * blocks + query) * BLK + a]
        return carry

    lax.fori_loop(0, 2 * slots, line, 0)

    def both(slot, carry):
        pairs_ref[2 * slot] = first_ref[slot]
        pairs_ref[2 * slot + 1] = second_ref[slot]
        return carry

    lax.fori_loop(0, pairs // 2, both, 0)


def plan(places, cand_block, query_block, valid, lengths, slots):
    pairs = cand_block.shape[0]
    shapes = (pairs // 2, 2 * slots * LINE, pairs)
    return pl.pallas_call(
        functools.partial(plan_kernel, pairs, slots),
        out_shape=[jax.ShapeDtypeStruct((n,), jnp.int32) for n in shapes],
        in_specs=[pl.BlockSpec(memory_space=SMEM)] * 5,
        out_specs=[pl.BlockSpec(memory_space=SMEM)] * 3,
        scratch_shapes=[SMEM((pairs,), jnp.int32)] * 3,
        compiler_params=vmem_params(4),
    )(places, cand_block, query_block, valid, lengths)


def project_kernel(me_ref, states_ref, weight_ref, out_ref):
    out_ref[0, 0] = jnp.dot(
        states_ref[0], weight_ref[...], preferred_element_type=jnp.float32
    ).astype(out_ref.dtype)


def project(me, states, weight, shares, offset, count, dtype):
    blocks, rows, width = states.shape
    out_width = weight.shape[1]
    part = rows // shares
    return pl.pallas_call(
        project_kernel,
        out_shape=jax.ShapeDtypeStruct((count, blocks, part, out_width), dtype),
        grid_spec=pltpu.PrefetchScalarGridSpec(
            num_scalar_prefetch=1,
            grid=(count, blocks),
            in_specs=[
                pl.BlockSpec(
                    (1, part, width), lambda d, b, m: (b, lax.rem(m[0] + offset + d, shares), 0)
                ),
                pl.BlockSpec((width, out_width), lambda d, b, m: (0, 0)),
            ],
            out_specs=pl.BlockSpec((1, 1, part, out_width), lambda d, b, m: (d, b, 0, 0)),
        ),
        cost_estimate=pl.CostEstimate(
            flops=2 * count * blocks * part * width * out_width,
            bytes_accessed=2 * count * blocks * part * width,
            transcendentals=0,
        ),
    )(me, states, weight)


def unit_kernel(others, pieces, keep_ref, *refs):
    out_ref = refs[-1]
    total = keep_ref[0, 0]
    for ref in refs[:others]:
        total = total + ref[0].astype(jnp.float32)
    norm = jnp.sum(total * total, axis=-1, keepdims=True)
    unit = (total * lax.rsqrt(norm + 1e-06)).astype(jnp.bfloat16)
    if pieces is None:
        out_ref[0] = unit
    else:
        size = unit.shape[0] // pieces
        for m in range(pieces):
            out_ref[m, 0] = unit[m * size : (m + 1) * size]


def unit_rows(keep, received, owners):
    _, blocks, part, width = keep.shape
    size = part // owners
    direct = size % 16 == 0
    if direct:
        shape = (owners, blocks, size, width)
        out_spec = pl.BlockSpec((owners, 1, size, width), lambda b: (0, b, 0, 0))
    else:
        shape = (blocks, part, width)
        out_spec = pl.BlockSpec((1, part, width), lambda b: (b, 0, 0))
    out = pl.pallas_call(
        functools.partial(unit_kernel, len(received), owners if direct else None),
        out_shape=jax.ShapeDtypeStruct(shape, jnp.bfloat16),
        grid=(blocks,),
        in_specs=[pl.BlockSpec((1, 1, part, width), lambda b: (0, b, 0, 0))]
        + [pl.BlockSpec((1, part, width), lambda b: (b, 0, 0))] * len(received),
        out_specs=out_spec,
    )(keep, *received)
    if direct:
        return out
    return out.reshape(blocks, owners, size, width).transpose(1, 0, 2, 3)


def route_kernel(dests, slots, owners, asked_ref, pieces_ref, out_ref):
    def step(d, carry):
        side = d // owners
        requester = d - side * owners
        for k in range(slots):
            out_ref[d, k] = pieces_ref[asked_ref[requester, side * slots + k]]
        return carry

    lax.fori_loop(0, dests, step, 0)


def route(asked, pieces, owners, shares):
    slots = asked.shape[1] // shares
    dests = owners * shares
    return pl.pallas_call(
        functools.partial(route_kernel, dests, slots, owners),
        out_shape=jax.ShapeDtypeStruct((dests, slots) + pieces.shape[1:], jnp.bfloat16),
        in_specs=[pl.BlockSpec(memory_space=SMEM), pl.BlockSpec(memory_space=VMEM)],
        out_specs=pl.BlockSpec(memory_space=VMEM),
        compiler_params=vmem_params(48),
    )(asked, pieces)


def query_rows(parts, out_ref):
    _, _, core, side = place()
    size = out_ref.shape[1] // 32
    blocks = out_ref.shape[0]
    for rel, ref in enumerate(parts):
        base = (side ^ (rel // 2)) * (16 * size) + (core ^ (rel % 2)) * (2 * size)
        for z in range(4):
            for x in range(2):
                target = pl.multiple_of(base + z * 4 * size + x * size, 16)
                for b in range(blocks):
                    begin = ((z * 2 + x) * blocks + b) * size
                    out_ref[b, pl.ds(target, size)] = ref[begin : begin + size]


def score_kernel(length, parts, table_ref, *refs):
    if parts:
        cand_ref, out_ref, totals_ref, block_ref, query_ref = refs[parts:]
        query_rows(refs[:parts], query_ref)
    else:
        query_ref, cand_ref, out_ref, totals_ref = refs
    rows = query_ref.shape[1]
    slots = cand_ref.shape[-3]
    totals_ref[...] = jnp.ones_like(totals_ref)
    upper = lax.broadcasted_iota(jnp.int32, (length // 2, COLS), 0) + length // 2
    lane = lax.broadcasted_iota(jnp.int32, (16, length), 1)

    def slot_step(k, carry):
        if parts:
            pieces, _, size, _ = cand_ref.shape
            for piece in range(pieces):
                begin = (piece // 4 * 4 + piece % 2 * 2 + piece // 2 % 2) * size
                block_ref[begin : begin + size] = cand_ref[piece, k]
        for i in range(2):
            line = (2 * k + i) * LINE
            query = table_ref[line + 1]
            for start in range(0, rows, COLS):
                sim = lax.dot_general(
                    block_ref[...] if parts else cand_ref[k],
                    query_ref[query, start : start + COLS],
                    (((1,), (1,)), ((), ())),
                    preferred_element_type=jnp.float32,
                )
                for b in range(BLK):
                    live = table_ref[line + 3 + b]
                    low = jnp.exp2(sim[b * length : b * length + length // 2] * EXP2_SCALE)
                    high = jnp.exp2(sim[b * length + length // 2 : (b + 1) * length] * EXP2_SCALE)
                    both = low + jnp.where(upper < live, high, 0.0)
                    totals_ref[2 * k + i, b : b + 1, start : start + COLS] = jnp.sum(
                        both, axis=0, keepdims=True
                    )
        return carry

    lax.fori_loop(0, slots, slot_step, 0)
    for tile in range(out_ref.shape[0]):
        score = jnp.zeros((16, length), jnp.float32)
        for i in range(tile * PACK, min((tile + 1) * PACK, 2 * slots)):
            line = i * LINE
            keep = table_ref[line + 2].astype(jnp.float32) / (SHARPNESS * length)
            for a in range(BLK):
                live = table_ref[line + 3 + BLK + a]
                logs = jnp.log(totals_ref[i, :, a * length : (a + 1) * length])
                summed = jnp.sum(jnp.where(lane < live, logs, 0.0), axis=1, keepdims=True)
                score = jnp.where(lane == i % PACK * BLK + a, summed * keep, score)
        out_ref[tile] = score


def score(table, query, cand, blocks, length):
    slots, width = cand.shape[-3], cand.shape[-1]
    rows = BLK * length
    parts = len(query) if isinstance(query, list) else 0
    count = 2 * slots * rows * rows
    scratch = [VMEM((2 * slots, 16, rows), jnp.float32)]
    if parts:
        scratch += [VMEM((rows, width), jnp.bfloat16), VMEM((blocks, rows, width), jnp.bfloat16)]
    return pl.pallas_call(
        functools.partial(score_kernel, length, parts),
        out_shape=jax.ShapeDtypeStruct((-(-2 * slots // PACK), 16, length), jnp.float32),
        in_specs=[pl.BlockSpec(memory_space=SMEM)]
        + [pl.BlockSpec(memory_space=VMEM)] * (max(parts, 1) + 1),
        out_specs=pl.BlockSpec(memory_space=VMEM),
        scratch_shapes=scratch,
        compiler_params=vmem_params(28),
        cost_estimate=pl.CostEstimate(
            flops=2 * count * width, bytes_accessed=4 * rows * width, transcendentals=count
        ),
    )(table, *(query if parts else [query]), cand)


def place_kernel(shares, count, where_ref, pairs_ref, *refs):
    parts, out_ref = refs[:-1], refs[-1]
    for d, ref in enumerate(parts):
        side = lax.rem(where_ref[1] - d + shares, shares)
        for i in range(count):
            tile = ref[i // PACK]
            if i % PACK:
                tile = pltpu.roll(tile, tile.shape[1] - i % PACK * BLK, 1)
            out_ref[pairs_ref[side * count + i]] = tile[:BLK, :BLK]


def place_scores(where, pair_of, parts, pairs):
    shares = len(parts)
    return pl.pallas_call(
        functools.partial(place_kernel, shares, pairs // shares),
        out_shape=jax.ShapeDtypeStruct((pairs, BLK, BLK), jnp.float32),
        in_specs=[pl.BlockSpec(memory_space=SMEM)] * 2 + [pl.BlockSpec(memory_space=VMEM)] * shares,
        out_specs=pl.BlockSpec(memory_space=VMEM),
        compiler_params=vmem_params(4),
    )(where, pair_of, *parts)


def local_general(states, proj_weight, lengths, query_block, cand_block, pair_valid):
    shares = lax.axis_size("narrow")
    owners = lax.axis_size("wide")
    side = lax.axis_index("narrow").astype(jnp.int32)
    owner = lax.axis_index("wide").astype(jnp.int32)
    paras, length, width_part = states.shape
    width = proj_weight.shape[1]
    blocks = paras // BLK
    rows = BLK * length
    flat = states.reshape(blocks, rows, width_part)
    me = side.reshape(1)

    def shift(d):
        return [(i, (i + d) % shares) for i in range(shares)]

    slots = cand_block.shape[0] // 2 // shares
    places = jnp.stack([owner, side, jnp.int32(blocks)])
    sel, table, pair_of = plan(places, cand_block, query_block, pair_valid, lengths, slots)
    sent = project(me, flat, proj_weight, shares, 1, shares - 1, jnp.bfloat16)
    received = [lax.ppermute(sent[d - 1], "narrow", shift(d)) for d in range(1, shares)]
    asked = lax.all_to_all(
        jnp.broadcast_to(sel[None], (owners,) + sel.shape), "wide", 0, 0, tiled=True
    )
    kept = project(me, flat, proj_weight, shares, 0, 1, jnp.float32)
    mine = unit_rows(kept, received, owners)
    spread = lax.all_to_all(mine, "wide", 0, 0, tiled=True)
    size = mine.shape[2]
    by_side = [mine] + [lax.ppermute(mine, "narrow", shift(d)) for d in range(1, shares)]
    order = jnp.stack(by_side)
    query = jnp.stack(
        [lax.dynamic_index_in_dim(order, lax.rem(side - s + shares, shares), 0, False) for s in range(shares)]
    )
    query = query.transpose(2, 0, 1, 3, 4).reshape(blocks, rows, width)
    outgoing = route(asked, spread.reshape(owners * blocks, size, width), owners, shares)
    incoming = lax.all_to_all(outgoing, ("narrow", "wide"), 0, 0, tiled=True)
    cand = incoming.transpose(1, 0, 2, 3).reshape(-1, rows, width)
    part = score(table, query, cand, blocks, length)
    parts = [part] + [lax.ppermute(part, "narrow", shift(d)) for d in range(1, shares)]
    return place_scores(places, pair_of, parts, cand_block.shape[0])


def place():
    owner = lax.axis_index("wide")
    return owner // 4, owner // 2 % 2, owner % 2, lax.axis_index("narrow")


def split_kernel(first, over, states_ref, weight_ref, *refs):
    *outs, rows_ref, sems = refs
    _, _, core, side = place()
    blocks, part, _ = rows_ref.shape
    size = part // 16
    start = pl.multiple_of((side ^ over) * part, part)

    def load(b):
        return pltpu.make_async_copy(
            states_ref.at[first + b, pl.ds(start, part)], rows_ref.at[b], sems.at[b]
        )

    for b in range(blocks):
        load(b).start()
    for b in range(blocks):
        load(b).wait()
        for z in range(4):
            for flip in range(2):
                source = pl.multiple_of((core ^ flip) * (2 * size) + z * 4 * size, 16)
                both = jnp.dot(
                    rows_ref[b, pl.ds(source, 2 * size)],
                    weight_ref[...],
                    preferred_element_type=jnp.float32,
                ).astype(jnp.bfloat16)
                for x in range(2):
                    target = ((z * 2 + x) * blocks + b) * size
                    outs[flip][target : target + size] = both[x * size : (x + 1) * size]


def split(over, states, weight, first):
    _, rows, width = states.shape
    out_width = weight.shape[1]
    part = rows // 2
    out_rows = 8 * CHUNK * (part // 16)
    return pl.pallas_call(
        functools.partial(split_kernel, first, over),
        out_shape=(jax.ShapeDtypeStruct((out_rows, out_width), jnp.bfloat16),) * 2,
        in_specs=[pl.BlockSpec(memory_space=pltpu.HBM), pl.BlockSpec(memory_space=VMEM)],
        out_specs=[pl.BlockSpec(memory_space=VMEM)] * 2,
        scratch_shapes=[
            VMEM((CHUNK, part, width), jnp.bfloat16),
            pltpu.SemaphoreType.DMA((CHUNK,)),
        ],
        compiler_params=vmem_params(50),
        cost_estimate=pl.CostEstimate(
            flops=2 * CHUNK * part * width * out_width,
            bytes_accessed=2 * CHUNK * part * width,
            transcendentals=0,
        ),
    )(states, weight)


def gather_unit_kernel(size, sel_ref, sel_near_ref, y_ref, cy_ref, own_ref, c_ref, *outs):
    z, x, _, _ = place()
    sends, query = outs[:8], outs[8:]
    span = CHUNK * size
    shape = (16, own_ref.shape[1])
    row, lane = (lax.broadcasted_iota(jnp.int32, shape, axis) for axis in range(2))
    asked = jnp.zeros(shape, jnp.int32)
    for flip, ids_ref in enumerate((sel_ref, sel_near_ref)):
        for k in range(ids_ref.shape[0]):
            asked = jnp.where((row == flip) & (lane == k), ids_ref[k], asked)
    asked = asked.astype(jnp.float32).astype(jnp.bfloat16)
    for rel, send_ref in zip(SPREAD, sends):
        source = pl.multiple_of(((z ^ (rel // 2)) * 2 + (x ^ (rel % 2))) * span, 16)
        for flip, (one_ref, two_ref) in enumerate(((own_ref, y_ref), (c_ref, cy_ref))):
            total = one_ref[pl.ds(source, span)].astype(jnp.float32)
            total = total + two_ref[pl.ds(source, span)].astype(jnp.float32)
            norm = jnp.sum(total * total, axis=-1, keepdims=True)
            unit = (total * lax.rsqrt(norm + 1e-06)).astype(jnp.bfloat16)
            send_ref[flip * span : (flip + 1) * span] = unit
            query[flip][pl.ds(source, span)] = unit
        send_ref[2 * span :] = asked


def gather_unit(sel, sel_near, y, cy, own, c, size):
    rows, width = own.shape
    send = jax.ShapeDtypeStruct((2 * CHUNK * size + 16, width), jnp.bfloat16)
    query = jax.ShapeDtypeStruct((rows, width), jnp.bfloat16)
    return pl.pallas_call(
        functools.partial(gather_unit_kernel, size),
        out_shape=(send,) * 8 + (query,) * 2,
        in_specs=[pl.BlockSpec(memory_space=SMEM)] * 2 + [pl.BlockSpec(memory_space=VMEM)] * 4,
        out_specs=[pl.BlockSpec(memory_space=VMEM)] * 10,
        compiler_params=vmem_params(12),
    )(sel, sel_near, y, cy, own, c)


def cube_route_kernel(size, slots, *refs):
    spread, out_ref, pieces_ref, rows_ref, asked_ref, sem = refs[:8], *refs[8:]
    z, x, core, _ = place()
    blocks = pieces_ref.shape[0] // 16
    span = CHUNK * size
    chips = [(z ^ (rel // 2)) * 2 + (x ^ (rel % 2)) for rel in SPREAD]
    for ref, chip in zip(spread, chips):
        ids = ref[2 * span :].astype(jnp.float32)
        for flip in range(2):
            rows_ref[pl.ds(chip * 2 + (core ^ flip), 1)] = ids[flip : flip + 1].astype(jnp.int32)
    copy = pltpu.make_async_copy(rows_ref, asked_ref, sem)
    copy.start()
    for ref, chip in zip(spread, chips):
        for flip in range(2):
            owner = chip * 2 + (core ^ flip)
            for b in range(blocks):
                row = flip * span + b * size
                pieces_ref[owner * blocks + b] = ref[row : row + size]
    copy.wait()

    def step(d, carry):
        side = d // 16
        for k in range(slots):
            out_ref[d, k] = pieces_ref[asked_ref[d - side * 16, side * slots + k]]
        return carry

    lax.fori_loop(0, 32, step, 0, unroll=4)


def cube_route(spread, size, slots, blocks):
    width = spread[0].shape[1]
    return pl.pallas_call(
        functools.partial(cube_route_kernel, size, slots),
        out_shape=jax.ShapeDtypeStruct((32, slots, size, width), jnp.bfloat16),
        in_specs=[pl.BlockSpec(memory_space=VMEM)] * len(spread),
        out_specs=pl.BlockSpec(memory_space=VMEM),
        scratch_shapes=[
            VMEM((16 * blocks, size, width), jnp.bfloat16),
            VMEM((16, width), jnp.int32),
            SMEM((16, width), jnp.int32),
            pltpu.SemaphoreType.DMA,
        ],
        compiler_params=vmem_params(16),
    )(*spread)


def local_cube(states, proj_weight, lengths, query_block, cand_block, pair_valid):
    side = lax.axis_index("narrow").astype(jnp.int32)
    owner = lax.axis_index("wide").astype(jnp.int32)
    paras, length, width_part = states.shape
    width = proj_weight.shape[1]
    blocks = paras // BLK
    rows = BLK * length
    size = rows // 32
    slots = cand_block.shape[0] // 4
    flat = states.reshape(blocks, rows, width_part)

    def near(array, rel):
        flip = rel % 2 * 2 + rel // 2
        return lax.ppermute(array, ("wide", "narrow"), [(i, i ^ flip) for i in range(32)])

    def along(array, rel):
        flip = rel * 2
        return lax.ppermute(array, "wide", [(i, i ^ flip) for i in range(16)])

    places = jnp.stack([owner, side, jnp.int32(blocks)])
    sel, table, pair_of = plan(places, cand_block, query_block, pair_valid, lengths, slots)
    sel_near = near(sel, 1)
    far = split(1, flat, proj_weight, 0)
    weight, *far = lax.optimization_barrier((proj_weight, *far))
    y, cy = near(far[0], 2), near(far[1], 3)
    own, aside = split(0, flat, weight, 0)
    c = near(aside, 1)
    *sends, own, other = gather_unit(sel, sel_near, y, cy, own, c, size)
    other = near(other, 1)
    sends[4], other = lax.optimization_barrier((sends[4], other))
    spread = [along(send, rel) if rel else send for rel, send in zip(SPREAD, sends)]
    own_y = near(own, 2)
    outgoing = cube_route(spread, size, slots, blocks)
    outgoing, own_y, other = lax.optimization_barrier((outgoing, own_y, other))
    incoming = lax.all_to_all(outgoing, ("narrow", "wide"), 0, 0, tiled=True)
    query = [own, other, own_y, near(other, 2)]
    part = score(table, query, incoming, blocks, length)
    parts = [part, lax.ppermute(part, "narrow", [(0, 1), (1, 0)])]
    return place_scores(places, pair_of, parts, cand_block.shape[0])


def solution(mesh):
    in_specs = (P("wide", None, "narrow"), P("narrow", None), P(), P("wide"), P("wide"), P("wide"))
    out_specs = P("wide", None, None)
    cube = mesh.shape["wide"] == 16 and mesh.shape["narrow"] == 2
    local = local_cube if cube else local_general
    return jax.shard_map(local, mesh=mesh, in_specs=in_specs, out_specs=out_specs, check_vma=False)
```

```python
import functools
import math

import jax
import jax.numpy as jnp
from jax import lax
from jax.experimental import pallas as pl
from jax.experimental.pallas import tpu as pltpu
from jax.sharding import PartitionSpec as P

BLK = 12
SHARPNESS = 20.0
EXP2_SCALE = SHARPNESS * math.log2(math.e)
COLS = 512
CHUNK = 4
LINE = 32
PACK = 6
SPREAD = (0, 1, 2, 5, 3, 7, 4, 6)
SMEM = pltpu.SMEM
VMEM = pltpu.VMEM


def vmem_params(mib):
    return pltpu.CompilerParams(vmem_limit_bytes=mib * 2**20)


def plan_kernel(pairs, slots, places_ref, cand_ref, query_block_ref, valid_ref, lengths_ref, sel_ref, table_ref, pairs_ref, *scratch):
    first_ref, second_ref, slot_ref = scratch
    owner, side, blocks = places_ref[0], places_ref[1], places_ref[2]

    def step(k, count):
        block = cand_ref[k]
        found = lax.fori_loop(
            0, k, lambda e, f: jnp.where(cand_ref[e] == block, slot_ref[e], f), jnp.int32(-1)
        )
        new = found < 0
        slot = jnp.minimum(jnp.where(new, count, found), pairs // 2 - 1)
        slot_ref[k] = slot

        @pl.when(new)
        def _():
            sel_ref[slot] = block
            first_ref[slot] = k

        second_ref[slot] = k
        return count + new.astype(jnp.int32)

    lax.fori_loop(0, pairs, step, jnp.int32(0))

    def line(i, carry):
        k = i // 2
        slot = side * slots + k
        pair = jnp.where(i - 2 * k == 0, first_ref[slot], second_ref[slot])
        query = query_block_ref[pair]
        table_ref[i * LINE + 1] = query
        table_ref[i * LINE + 2] = valid_ref[pair]
        for a in range(BLK):
            table_ref[i * LINE + 3 + a] = lengths_ref[sel_ref[slot] * BLK + a]
            table_ref[i * LINE + 3 + BLK + a] = lengths_ref[(owner * blocks + query) * BLK + a]
        return carry

    lax.fori_loop(0, 2 * slots, line, 0)

    def both(slot, carry):
        pairs_ref[2 * slot] = first_ref[slot]
        pairs_ref[2 * slot + 1] = second_ref[slot]
        return carry

    lax.fori_loop(0, pairs // 2, both, 0)


def plan(places, cand_block, query_block, valid, lengths, slots):
    pairs = cand_block.shape[0]
    shapes = (pairs // 2, 2 * slots * LINE, pairs)
    return pl.pallas_call(
        functools.partial(plan_kernel, pairs, slots),
        out_shape=[jax.ShapeDtypeStruct((n,), jnp.int32) for n in shapes],
        in_specs=[pl.BlockSpec(memory_space=SMEM)] * 5,
        out_specs=[pl.BlockSpec(memory_space=SMEM)] * 3,
        scratch_shapes=[SMEM((pairs,), jnp.int32)] * 3,
        compiler_params=vmem_params(4),
    )(places, cand_block, query_block, valid, lengths)


def project_kernel(me_ref, states_ref, weight_ref, out_ref):
    out_ref[0, 0] = jnp.dot(
        states_ref[0], weight_ref[...], preferred_element_type=jnp.float32
    ).astype(out_ref.dtype)


def project(me, states, weight, shares, offset, count, dtype):
    blocks, rows, width = states.shape
    out_width = weight.shape[1]
    part = rows // shares
    return pl.pallas_call(
        project_kernel,
        out_shape=jax.ShapeDtypeStruct((count, blocks, part, out_width), dtype),
        grid_spec=pltpu.PrefetchScalarGridSpec(
            num_scalar_prefetch=1,
            grid=(count, blocks),
            in_specs=[
                pl.BlockSpec(
                    (1, part, width), lambda d, b, m: (b, lax.rem(m[0] + offset + d, shares), 0)
                ),
                pl.BlockSpec((width, out_width), lambda d, b, m: (0, 0)),
            ],
            out_specs=pl.BlockSpec((1, 1, part, out_width), lambda d, b, m: (d, b, 0, 0)),
        ),
        cost_estimate=pl.CostEstimate(
            flops=2 * count * blocks * part * width * out_width,
            bytes_accessed=2 * count * blocks * part * width,
            transcendentals=0,
        ),
    )(me, states, weight)


def unit_kernel(others, pieces, keep_ref, *refs):
    out_ref = refs[-1]
    total = keep_ref[0, 0]
    for ref in refs[:others]:
        total = total + ref[0].astype(jnp.float32)
    norm = jnp.sum(total * total, axis=-1, keepdims=True)
    unit = (total * lax.rsqrt(norm + 1e-06)).astype(jnp.bfloat16)
    if pieces is None:
        out_ref[0] = unit
    else:
        size = unit.shape[0] // pieces
        for m in range(pieces):
            out_ref[m, 0] = unit[m * size : (m + 1) * size]


def unit_rows(keep, received, owners):
    _, blocks, part, width = keep.shape
    size = part // owners
    direct = size % 16 == 0
    if direct:
        shape = (owners, blocks, size, width)
        out_spec = pl.BlockSpec((owners, 1, size, width), lambda b: (0, b, 0, 0))
    else:
        shape = (blocks, part, width)
        out_spec = pl.BlockSpec((1, part, width), lambda b: (b, 0, 0))
    out = pl.pallas_call(
        functools.partial(unit_kernel, len(received), owners if direct else None),
        out_shape=jax.ShapeDtypeStruct(shape, jnp.bfloat16),
        grid=(blocks,),
        in_specs=[pl.BlockSpec((1, 1, part, width), lambda b: (0, b, 0, 0))]
        + [pl.BlockSpec((1, part, width), lambda b: (b, 0, 0))] * len(received),
        out_specs=out_spec,
    )(keep, *received)
    if direct:
        return out
    return out.reshape(blocks, owners, size, width).transpose(1, 0, 2, 3)


def route_kernel(dests, slots, owners, asked_ref, pieces_ref, out_ref):
    def step(d, carry):
        side = d // owners
        requester = d - side * owners
        for k in range(slots):
            out_ref[d, k] = pieces_ref[asked_ref[requester, side * slots + k]]
        return carry

    lax.fori_loop(0, dests, step, 0)


def route(asked, pieces, owners, shares):
    slots = asked.shape[1] // shares
    dests = owners * shares
    return pl.pallas_call(
        functools.partial(route_kernel, dests, slots, owners),
        out_shape=jax.ShapeDtypeStruct((dests, slots) + pieces.shape[1:], jnp.bfloat16),
        in_specs=[pl.BlockSpec(memory_space=SMEM), pl.BlockSpec(memory_space=VMEM)],
        out_specs=pl.BlockSpec(memory_space=VMEM),
        compiler_params=vmem_params(48),
    )(asked, pieces)


def query_rows(parts, out_ref):
    _, _, core, side = place()
    size = out_ref.shape[1] // 32
    blocks = out_ref.shape[0]
    for rel, ref in enumerate(parts):
        base = (side ^ (rel // 2)) * (16 * size) + (core ^ (rel % 2)) * (2 * size)
        for z in range(4):
            for x in range(2):
                target = pl.multiple_of(base + z * 4 * size + x * size, 16)
                for b in range(blocks):
                    begin = ((z * 2 + x) * blocks + b) * size
                    out_ref[b, pl.ds(target, size)] = ref[begin : begin + size]


def score_kernel(length, parts, table_ref, *refs):
    if parts:
        cand_ref, out_ref, totals_ref, block_ref, query_ref = refs[parts:]
        query_rows(refs[:parts], query_ref)
    else:
        query_ref, cand_ref, out_ref, totals_ref = refs
    rows = query_ref.shape[1]
    slots = cand_ref.shape[-3]
    totals_ref[...] = jnp.ones_like(totals_ref)
    upper = lax.broadcasted_iota(jnp.int32, (length // 2, COLS), 0) + length // 2
    lane = lax.broadcasted_iota(jnp.int32, (16, length), 1)

    def slot_step(k, carry):
        if parts:
            pieces, _, size, _ = cand_ref.shape
            for piece in range(pieces):
                begin = (piece // 4 * 4 + piece % 2 * 2 + piece // 2 % 2) * size
                block_ref[begin : begin + size] = cand_ref[piece, k]
        for i in range(2):
            line = (2 * k + i) * LINE
            query = table_ref[line + 1]
            for start in range(0, rows, COLS):
                sim = lax.dot_general(
                    block_ref[...] if parts else cand_ref[k],
                    query_ref[query, start : start + COLS],
                    (((1,), (1,)), ((), ())),
                    preferred_element_type=jnp.float32,
                )
                for b in range(BLK):
                    live = table_ref[line + 3 + b]
                    low = jnp.exp2(sim[b * length : b * length + length // 2] * EXP2_SCALE)
                    high = jnp.exp2(sim[b * length + length // 2 : (b + 1) * length] * EXP2_SCALE)
                    both = low + jnp.where(upper < live, high, 0.0)
                    totals_ref[2 * k + i, b : b + 1, start : start + COLS] = jnp.sum(
                        both, axis=0, keepdims=True
                    )
        return carry

    lax.fori_loop(0, slots, slot_step, 0)
    for tile in range(out_ref.shape[0]):
        score = jnp.zeros((16, length), jnp.float32)
        for i in range(tile * PACK, min((tile + 1) * PACK, 2 * slots)):
            line = i * LINE
            keep = table_ref[line + 2].astype(jnp.float32) / (SHARPNESS * length)
            for a in range(BLK):
                live = table_ref[line + 3 + BLK + a]
                logs = jnp.log(totals_ref[i, :, a * length : (a + 1) * length])
                summed = jnp.sum(jnp.where(lane < live, logs, 0.0), axis=1, keepdims=True)
                score = jnp.where(lane == i % PACK * BLK + a, summed * keep, score)
        out_ref[tile] = score


def score(table, query, cand, blocks, length):
    slots, width = cand.shape[-3], cand.shape[-1]
    rows = BLK * length
    parts = len(query) if isinstance(query, list) else 0
    count = 2 * slots * rows * rows
    scratch = [VMEM((2 * slots, 16, rows), jnp.float32)]
    if parts:
        scratch += [VMEM((rows, width), jnp.bfloat16), VMEM((blocks, rows, width), jnp.bfloat16)]
    return pl.pallas_call(
        functools.partial(score_kernel, length, parts),
        out_shape=jax.ShapeDtypeStruct((-(-2 * slots // PACK), 16, length), jnp.float32),
        in_specs=[pl.BlockSpec(memory_space=SMEM)]
        + [pl.BlockSpec(memory_space=VMEM)] * (max(parts, 1) + 1),
        out_specs=pl.BlockSpec(memory_space=VMEM),
        scratch_shapes=scratch,
        compiler_params=vmem_params(28),
        cost_estimate=pl.CostEstimate(
            flops=2 * count * width, bytes_accessed=4 * rows * width, transcendentals=count
        ),
    )(table, *(query if parts else [query]), cand)


def place_kernel(shares, count, where_ref, pairs_ref, *refs):
    parts, out_ref = refs[:-1], refs[-1]
    for d, ref in enumerate(parts):
        side = lax.rem(where_ref[1] - d + shares, shares)
        for i in range(count):
            tile = ref[i // PACK]
            if i % PACK:
                tile = pltpu.roll(tile, tile.shape[1] - i % PACK * BLK, 1)
            out_ref[pairs_ref[side * count + i]] = tile[:BLK, :BLK]


def place_scores(where, pair_of, parts, pairs):
    shares = len(parts)
    return pl.pallas_call(
        functools.partial(place_kernel, shares, pairs // shares),
        out_shape=jax.ShapeDtypeStruct((pairs, BLK, BLK), jnp.float32),
        in_specs=[pl.BlockSpec(memory_space=SMEM)] * 2 + [pl.BlockSpec(memory_space=VMEM)] * shares,
        out_specs=pl.BlockSpec(memory_space=VMEM),
        compiler_params=vmem_params(4),
    )(where, pair_of, *parts)


def local_general(states, proj_weight, lengths, query_block, cand_block, pair_valid):
    shares = lax.axis_size("narrow")
    owners = lax.axis_size("wide")
    side = lax.axis_index("narrow").astype(jnp.int32)
    owner = lax.axis_index("wide").astype(jnp.int32)
    paras, length, width_part = states.shape
    width = proj_weight.shape[1]
    blocks = paras // BLK
    rows = BLK * length
    flat = states.reshape(blocks, rows, width_part)
    me = side.reshape(1)

    def shift(d):
        return [(i, (i + d) % shares) for i in range(shares)]

    slots = cand_block.shape[0] // 2 // shares
    places = jnp.stack([owner, side, jnp.int32(blocks)])
    sel, table, pair_of = plan(places, cand_block, query_block, pair_valid, lengths, slots)
    sent = project(me, flat, proj_weight, shares, 1, shares - 1, jnp.bfloat16)
    received = [lax.ppermute(sent[d - 1], "narrow", shift(d)) for d in range(1, shares)]
    asked = lax.all_to_all(
        jnp.broadcast_to(sel[None], (owners,) + sel.shape), "wide", 0, 0, tiled=True
    )
    kept = project(me, flat, proj_weight, shares, 0, 1, jnp.float32)
    mine = unit_rows(kept, received, owners)
    spread = lax.all_to_all(mine, "wide", 0, 0, tiled=True)
    size = mine.shape[2]
    by_side = [mine] + [lax.ppermute(mine, "narrow", shift(d)) for d in range(1, shares)]
    order = jnp.stack(by_side)
    query = jnp.stack(
        [lax.dynamic_index_in_dim(order, lax.rem(side - s + shares, shares), 0, False) for s in range(shares)]
    )
    query = query.transpose(2, 0, 1, 3, 4).reshape(blocks, rows, width)
    outgoing = route(asked, spread.reshape(owners * blocks, size, width), owners, shares)
    incoming = lax.all_to_all(outgoing, ("narrow", "wide"), 0, 0, tiled=True)
    cand = incoming.transpose(1, 0, 2, 3).reshape(-1, rows, width)
    part = score(table, query, cand, blocks, length)
    parts = [part] + [lax.ppermute(part, "narrow", shift(d)) for d in range(1, shares)]
    return place_scores(places, pair_of, parts, cand_block.shape[0])


def place():
    owner = lax.axis_index("wide")
    return owner // 4, owner // 2 % 2, owner % 2, lax.axis_index("narrow")


def split_kernel(first, over, states_ref, weight_ref, *refs):
    *outs, rows_ref, sems = refs
    _, _, core, side = place()
    blocks, part, _ = rows_ref.shape
    size = part // 16
    start = pl.multiple_of((side ^ over) * part, part)

    def load(b):
        return pltpu.make_async_copy(
            states_ref.at[first + b, pl.ds(start, part)], rows_ref.at[b], sems.at[b]
        )

    for b in range(blocks):
        load(b).start()
    for b in range(blocks):
        load(b).wait()
        for z in range(4):
            for flip in range(2):
                source = pl.multiple_of((core ^ flip) * (2 * size) + z * 4 * size, 16)
                both = jnp.dot(
                    rows_ref[b, pl.ds(source, 2 * size)],
                    weight_ref[...],
                    preferred_element_type=jnp.float32,
                ).astype(jnp.bfloat16)
                for x in range(2):
                    target = ((z * 2 + x) * blocks + b) * size
                    outs[flip][target : target + size] = both[x * size : (x + 1) * size]


def split(over, states, weight, first):
    _, rows, width = states.shape
    out_width = weight.shape[1]
    part = rows // 2
    out_rows = 8 * CHUNK * (part // 16)
    return pl.pallas_call(
        functools.partial(split_kernel, first, over),
        out_shape=(jax.ShapeDtypeStruct((out_rows, out_width), jnp.bfloat16),) * 2,
        in_specs=[pl.BlockSpec(memory_space=pltpu.HBM), pl.BlockSpec(memory_space=VMEM)],
        out_specs=[pl.BlockSpec(memory_space=VMEM)] * 2,
        scratch_shapes=[
            VMEM((CHUNK, part, width), jnp.bfloat16),
            pltpu.SemaphoreType.DMA((CHUNK,)),
        ],
        compiler_params=vmem_params(50),
        cost_estimate=pl.CostEstimate(
            flops=2 * CHUNK * part * width * out_width,
            bytes_accessed=2 * CHUNK * part * width,
            transcendentals=0,
        ),
    )(states, weight)


def gather_unit_kernel(size, sel_ref, sel_near_ref, y_ref, cy_ref, own_ref, c_ref, *outs):
    z, x, _, _ = place()
    sends, query = outs[:8], outs[8:]
    span = CHUNK * size
    shape = (16, own_ref.shape[1])
    row, lane = (lax.broadcasted_iota(jnp.int32, shape, axis) for axis in range(2))
    asked = jnp.zeros(shape, jnp.int32)
    for flip, ids_ref in enumerate((sel_ref, sel_near_ref)):
        for k in range(ids_ref.shape[0]):
            asked = jnp.where((row == flip) & (lane == k), ids_ref[k], asked)
    asked = asked.astype(jnp.float32).astype(jnp.bfloat16)
    for rel, send_ref in zip(SPREAD, sends):
        source = pl.multiple_of(((z ^ (rel // 2)) * 2 + (x ^ (rel % 2))) * span, 16)
        for flip, (one_ref, two_ref) in enumerate(((own_ref, y_ref), (c_ref, cy_ref))):
            total = one_ref[pl.ds(source, span)].astype(jnp.float32)
            total = total + two_ref[pl.ds(source, span)].astype(jnp.float32)
            norm = jnp.sum(total * total, axis=-1, keepdims=True)
            unit = (total * lax.rsqrt(norm + 1e-06)).astype(jnp.bfloat16)
            send_ref[flip * span : (flip + 1) * span] = unit
            query[flip][pl.ds(source, span)] = unit
        send_ref[2 * span :] = asked


def gather_unit(sel, sel_near, y, cy, own, c, size):
    rows, width = own.shape
    send = jax.ShapeDtypeStruct((2 * CHUNK * size + 16, width), jnp.bfloat16)
    query = jax.ShapeDtypeStruct((rows, width), jnp.bfloat16)
    return pl.pallas_call(
        functools.partial(gather_unit_kernel, size),
        out_shape=(send,) * 8 + (query,) * 2,
        in_specs=[pl.BlockSpec(memory_space=SMEM)] * 2 + [pl.BlockSpec(memory_space=VMEM)] * 4,
        out_specs=[pl.BlockSpec(memory_space=VMEM)] * 10,
        compiler_params=vmem_params(12),
    )(sel, sel_near, y, cy, own, c)


def cube_route_kernel(size, slots, *refs):
    spread, out_ref, pieces_ref, rows_ref, asked_ref, sem = refs[:8], *refs[8:]
    z, x, core, _ = place()
    blocks = pieces_ref.shape[0] // 16
    span = CHUNK * size
    chips = [(z ^ (rel // 2)) * 2 + (x ^ (rel % 2)) for rel in SPREAD]
    for ref, chip in zip(spread, chips):
        ids = ref[2 * span :].astype(jnp.float32)
        for flip in range(2):
            rows_ref[pl.ds(chip * 2 + (core ^ flip), 1)] = ids[flip : flip + 1].astype(jnp.int32)
    copy = pltpu.make_async_copy(rows_ref, asked_ref, sem)
    copy.start()
    for ref, chip in zip(spread, chips):
        for flip in range(2):
            owner = chip * 2 + (core ^ flip)
            for b in range(blocks):
                row = flip * span + b * size
                pieces_ref[owner * blocks + b] = ref[row : row + size]
    copy.wait()

    def step(d, carry):
        side = d // 16
        for k in range(slots):
            out_ref[d, k] = pieces_ref[asked_ref[d - side * 16, side * slots + k]]
        return carry

    lax.fori_loop(0, 32, step, 0, unroll=4)


def cube_route(spread, size, slots, blocks):
    width = spread[0].shape[1]
    return pl.pallas_call(
        functools.partial(cube_route_kernel, size, slots),
        out_shape=jax.ShapeDtypeStruct((32, slots, size, width), jnp.bfloat16),
        in_specs=[pl.BlockSpec(memory_space=VMEM)] * len(spread),
        out_specs=pl.BlockSpec(memory_space=VMEM),
        scratch_shapes=[
            VMEM((16 * blocks, size, width), jnp.bfloat16),
            VMEM((16, width), jnp.int32),
            SMEM((16, width), jnp.int32),
            pltpu.SemaphoreType.DMA,
        ],
        compiler_params=vmem_params(16),
    )(*spread)


def local_cube(states, proj_weight, lengths, query_block, cand_block, pair_valid):
    side = lax.axis_index("narrow").astype(jnp.int32)
    owner = lax.axis_index("wide").astype(jnp.int32)
    paras, length, width_part = states.shape
    width = proj_weight.shape[1]
    blocks = paras // BLK
    rows = BLK * length
    size = rows // 32
    slots = cand_block.shape[0] // 4
    flat = states.reshape(blocks, rows, width_part)

    def near(array, rel):
        flip = rel % 2 * 2 + rel // 2
        return lax.ppermute(array, ("wide", "narrow"), [(i, i ^ flip) for i in range(32)])

    def along(array, rel):
        flip = rel * 2
        return lax.ppermute(array, "wide", [(i, i ^ flip) for i in range(16)])

    places = jnp.stack([owner, side, jnp.int32(blocks)])
    sel, table, pair_of = plan(places, cand_block, query_block, pair_valid, lengths, slots)
    sel_near = near(sel, 1)
    far = split(1, flat, proj_weight, 0)
    weight, *far = lax.optimization_barrier((proj_weight, *far))
    y, cy = near(far[0], 2), near(far[1], 3)
    own, aside = split(0, flat, weight, 0)
    c = near(aside, 1)
    *sends, own, other = gather_unit(sel, sel_near, y, cy, own, c, size)
    other = near(other, 1)
    sends[4], other = lax.optimization_barrier((sends[4], other))
    spread = [along(send, rel) if rel else send for rel, send in zip(SPREAD, sends)]
    own_y = near(own, 2)
    outgoing = cube_route(spread, size, slots, blocks)
    outgoing, own_y, other = lax.optimization_barrier((outgoing, own_y, other))
    incoming = lax.all_to_all(outgoing, ("narrow", "wide"), 0, 0, tiled=True)
    query = [own, other, own_y, near(other, 2)]
    part = score(table, query, incoming, blocks, length)
    parts = [part, lax.ppermute(part, "narrow", [(0, 1), (1, 0)])]
    return place_scores(places, pair_of, parts, cand_block.shape[0])


def solution(mesh):
    in_specs = (P("wide", None, "narrow"), P("narrow", None), P(), P("wide"), P("wide"), P("wide"))
    out_specs = P("wide", None, None)
    cube = mesh.shape["wide"] == 16 and mesh.shape["narrow"] == 2
    local = local_cube if cube else local_general
    return jax.shard_map(local, mesh=mesh, in_specs=in_specs, out_specs=out_specs, check_vma=False)
```
